32 devices in a mesh: section: 2 (over x), copy: 2 (over y), dp: 8 (over z, core).
Axes of the slice: x: 2, y: 2, z: 4, core: 2. Of those that a mesh axis runs over, the one named last changes fastest.
Arguments:
- boundary: bfloat16 [2, 2, 8, 1024, 512], P('section', None, 'dp', 'copy'), may hold values from -6 to 6
- sentence_ids: int32 [2, 8, 1024], P(None, 'dp'), may hold values from 0 to 31, never falling along the last dimension, each value on 1 to 64 neighbouring positions
- qkv_weight: bfloat16 [2, 512, 1536], P('section'), may hold values from -0.25 to 0.25
- out_weight: bfloat16 [2, 512, 512], P('section'), may hold values from -0.75 to 0.75
- inner_weight: bfloat16 [2, 512, 2048], P('section'), may hold values from -0.25 to 0.25
- outer_weight: bfloat16 [2, 2048, 512], P('section'), may hold values from -0.1875 to 0.1875
- norm_gain: float32 [2, 2, 512], P('section'), may hold values from 0.5 to 1.5
- norm_bias: float32 [2, 2, 512], P('section'), may hold values from -1.8 to 1.8
Outputs:
- result: bfloat16 [2, 2, 8, 1024, 512], P('section', None, 'dp', 'copy')
- grad_qkv: float32 [2, 512, 1536], P('section')
- grad_out: float32 [2, 512, 512], P('section')
- grad_inner: float32 [2, 512, 2048], P('section')
- grad_outer: float32 [2, 2048, 512], P('section')
- grad_gain: float32 [2, 2, 512], P('section')
- grad_bias: float32 [2, 2, 512], P('section')
The draws below stay inside these ranges and needn't reach their ends.
Inputs may be any that keep to these rules, and one draw needn't show every extreme that they name: `sentence_ids`: along each row the ids never fall; each sentence spans 1 to 64 tokens, and in every draw some sentence spans exactly 64.
All inputs are finite; a program needn't handle non-finite values.
Results may differ from the reference program's by a relative error of at most 0.017.
Values may be sent and summed in bfloat16 or wider, within the bound.
A program may use at most 256 MiB of HBM per device.

```python
import math
import jax
import jax.numpy as jnp
import numpy as np
from jax import lax

D = 512
HEADS = 8
FF = 2048
SEQ = 1024
MICRO = 2
ROWS = 8


def block_scale(stream_key, shape, cuts, least, largest):
    factor_of, own = 1.0, jax.random.fold_in(stream_key, 6)
    for axis_at, shards_of in cuts:
        steps = jnp.exp(jax.random.uniform(jax.random.fold_in(own, axis_at), (shards_of,), jnp.float32, least / len(cuts), largest / len(cuts)))
        factor_of = factor_of * jnp.repeat(steps, shape[axis_at] // shards_of).reshape([-1 if axis == axis_at else 1 for axis in range(len(shape))])
    return factor_of


def length_profile(number_of, total, most, skew):
    loads = [(1 << 20) // math.isqrt(grade ** skew) + 1 for grade in range(2, number_of + 1)]
    surplus, holding = total - most - (number_of - 1), [1] * (number_of - 1)
    while surplus > 0:
        free = [i for i in range(number_of - 1) if holding[i] < most]
        whole, left = sum([loads[i] for i in free]), surplus
        for i in free:
            addition = min(most - holding[i], max(1, left * loads[i] // whole), surplus)
            holding[i] = holding[i] + addition
            surplus = surplus - addition
    return np.array([most] + holding)


def ragged(stream_key, count, total, limit, lean):
    if count == 2:
        one = jax.random.randint(stream_key, (), max(1, total - limit), min(limit, total - 1) + 1)
        return jnp.stack([one, total - one])
    tallies = jnp.asarray(length_profile(count, total, limit, lean), jnp.int32)
    pairs = (count - 1) // 2
    donor, sink = tallies[1:1 + 2 * pairs:2], tallies[2:2 + 2 * pairs:2]
    room = jnp.minimum(donor - 1, limit - sink)
    moved = jax.random.randint(jax.random.fold_in(stream_key, 1), (pairs,), 0, 1 << 20) % (room + 1)
    tallies = tallies.at[1:1 + 2 * pairs:2].set(donor - moved).at[2:2 + 2 * pairs:2].set(sink + moved)
    return tallies[jax.random.permutation(jax.random.fold_in(stream_key, 2), count)]


def scatter_about(key, extent, deviation, limit, cuts=(), held_as=jnp.bfloat16):
    values = jax.random.normal(key, extent, jnp.float32) * deviation
    if len(cuts) > 0:
        values = block_scale(key, extent, cuts, -0.22, 0.18) * values
    return jnp.clip(values, min=-limit, max=limit).astype(held_as)


def setup_inputs(seed: int = 0) -> dict:
    streams_of = jax.random.split(jax.random.key(seed), 9)
    boundary = scatter_about(streams_of[0], (2, MICRO, ROWS, SEQ, D), 1.0, 6.0, ((0, 2), (2, 8), (3, 2)))
    sentence_ids = jax.vmap(lambda own: jnp.searchsorted(jnp.cumsum(ragged(own, max(SEQ // 32, 8), SEQ, max(SEQ // 16, 4), 0)), jnp.arange(SEQ), side="right"))(jax.random.split(streams_of[1], MICRO * ROWS)).reshape((MICRO, ROWS, SEQ)).astype(jnp.int32)
    qkv_weight = scatter_about(streams_of[2], (2, D, 3 * D), D ** -0.5, 0.25, ((0, 2),))
    out_weight = scatter_about(streams_of[3], (2, D, D), (D // 8) ** -0.5, 0.75, ((0, 2),))
    inner_weight = scatter_about(streams_of[4], (2, D, FF), D ** -0.5, 0.25, ((0, 2),))
    outer_weight = scatter_about(streams_of[5], (2, FF, D), (FF // 2) ** -0.5, 0.1875, ((0, 2),))
    norm_gain = jnp.clip(1.0 + 0.1 * jax.random.normal(streams_of[6], (2, 2, D), jnp.float32), 0.5, 1.5)
    norm_bias = scatter_about(streams_of[7], (2, 2, D), 0.3, 1.8, ((0, 2),), jnp.float32)
    return {"boundary": boundary, "sentence_ids": sentence_ids, "qkv_weight": qkv_weight, "out_weight": out_weight, "inner_weight": inner_weight, "outer_weight": outer_weight, "norm_gain": norm_gain, "norm_bias": norm_bias}


NEG = -1e+30
EPS = 1e-05
HIGH = lax.Precision.HIGHEST

@jax.custom_vjp
def low(v):
    return lax.optimization_barrier(v.astype(jnp.bfloat16)).astype(jnp.float32)

@jax.custom_vjp
def low_back(v):
    return v

def low_keep(v):
    return (low(v), None)

def low_pass(kept, grad):
    return (grad,)

def back_keep(v):
    return (v, None)

def back_low(kept, grad):
    return (low(grad),)
low.defvjp(low_keep, low_pass)
low_back.defvjp(back_keep, back_low)

def normalize(resid, gain, shift):
    center = resid - lax.optimization_barrier(jnp.mean(resid, axis=-1, keepdims=True))
    spread = lax.optimization_barrier(jnp.mean(center * center, axis=-1, keepdims=True))
    return center * lax.rsqrt(spread + EPS) * gain + shift

def layer(params, hidden, sentence):
    qkv_weight, out_weight, inner_weight, outer_weight, gains, shifts = params
    count, length, width = hidden.shape
    head_dim = width // HEADS
    scale = head_dim ** (-0.5)
    mixed = jnp.einsum('gsd,de->gse', hidden, qkv_weight, precision=HIGH)
    mixed = low_back(low(mixed)).reshape(count, length, 3, HEADS, head_dim)
    query, key, value = (mixed[:, :, 0], mixed[:, :, 1], mixed[:, :, 2])
    scores = low_back(jnp.einsum('gqhd,gkhd->ghqk', query, key, precision=HIGH) * scale)
    allowed = (sentence[:, :, None] == sentence[:, None, :])[:, None]
    scores = jnp.where(allowed, scores, NEG)
    peak = lax.optimization_barrier(jnp.max(scores, axis=-1, keepdims=True))
    weights = jnp.exp(scores - peak)
    probs = weights / lax.optimization_barrier(jnp.sum(weights, axis=-1, keepdims=True))
    attended = jnp.einsum('ghqk,gkhd->gqhd', low(probs), value, precision=HIGH)
    attended = low_back(low(attended)).reshape(count, length, width)
    resid = hidden + low_back(jnp.einsum('gsd,de->gse', attended, out_weight, precision=HIGH))
    normed = normalize(resid, gains[0], shifts[0])
    inner = low_back(jnp.einsum('gsd,df->gsf', low(normed), inner_weight, precision=HIGH))
    active = low(jax.nn.gelu(inner, approximate=False))
    outer = low_back(jnp.einsum('gsf,fd->gsd', active, outer_weight, precision=HIGH))
    return normalize(normed + outer, gains[1], shifts[1])

def reference(boundary, sentence_ids, qkv_weight, out_weight, inner_weight, outer_weight, norm_gain, norm_bias):
    micro_count, batch_rows, length, width = boundary.shape[1:]
    count = micro_count * batch_rows
    group = math.gcd(count, max(1, 4096 // length))

    def section_params(index):
        return (qkv_weight[index].astype(jnp.float32), out_weight[index].astype(jnp.float32), inner_weight[index].astype(jnp.float32), outer_weight[index].astype(jnp.float32), norm_gain[index].astype(jnp.float32), norm_bias[index].astype(jnp.float32))
    first = section_params(0)
    second = section_params(1)
    inputs = boundary[0].astype(jnp.float32).reshape(count // group, group, length, width)
    cotangents = boundary[1].astype(jnp.float32).reshape(count // group, group, length, width)
    sentences = sentence_ids.reshape(count // group, group, length)

    def one_group(totals, pieces):
        group_in, group_cot, group_ids = pieces

        def whole(params_one, params_two, start):
            middle = layer(params_one, start, group_ids)
            return layer(params_two, low_back(low(middle)), group_ids)
        output, pull = jax.vjp(whole, first, second, group_in)
        grads_one, grads_two, grad_start = pull(group_cot)
        totals = jax.tree.map(lambda total, one, two: total + jnp.stack([one, two]), totals, grads_one, grads_two)
        return (totals, (grad_start, output))
    zeros = jax.tree.map(lambda item: jnp.zeros((2,) + item.shape, item.dtype), first)
    totals, (grad_starts, outputs) = lax.scan(one_group, zeros, (inputs, cotangents, sentences))
    result = jnp.stack([grad_starts.reshape(micro_count, batch_rows, length, width), outputs.reshape(micro_count, batch_rows, length, width)]).astype(jnp.bfloat16)
    return (result, totals[0], totals[1], totals[2], totals[3], totals[4], totals[5])
```

```python
import functools

import jax
import jax.numpy as jnp
from jax import lax
from jax.experimental import pallas as pl
from jax.experimental.pallas import tpu as pltpu
from jax.sharding import PartitionSpec as P

HEADS = 8
REACH = 32
SPAN = 64
WINDOW = 256
NEG = -1e30
EPS = 1e-05
PIECES = 2
GROUPS = 3
BLOCKS = {1: ((0, 192, 0), (192, 80, 112), (272, 80, 192), (352, 192, 288)), 2: ((0, 160, 0), (160, 144, 48))}
MESH = pl.DeviceIdType.MESH
F32 = jnp.float32
BF16 = jnp.bfloat16


def mul(left, right):
    return jnp.dot(left, right, preferred_element_type=F32)


def against(left, right):
    return lax.dot_general(left, right, (((1,), (1,)), ((), ())), preferred_element_type=F32)


def contract(left, right):
    return lax.dot_general(left, right, (((0,), (0,)), ((), ())), preferred_element_type=F32)


def gelu(x):
    phi = 0.5 + 0.5 * lax.erf(x * 0.7071067811865476)
    bell = jnp.exp(x * x * -0.5) * 0.3989422804014327
    return (x * phi).astype(BF16), (phi + x * bell).astype(BF16)


def normalize(resid):
    center = resid - jnp.mean(resid, axis=-1, keepdims=True)
    spread = jnp.mean(center * center, axis=-1, keepdims=True)
    inverse = lax.rsqrt(spread + EPS)
    return center * inverse, inverse


def normalize_back(upstream, scaled, inverse, gain):
    tilted = upstream * gain
    first = jnp.mean(tilted, axis=-1, keepdims=True)
    second = jnp.mean(tilted * scaled, axis=-1, keepdims=True)
    return inverse * (tilted - first - scaled * second)


def halves(pair):
    lane = lax.broadcasted_iota(jnp.int32, pair.shape, 1)
    zero = jnp.zeros_like(pair)
    return jnp.where(lane < 64, pair, zero), jnp.where(lane < 64, zero, pair)


def kernel(
    units, rows, chips, width, inner_width,
    given, id_col, id_row, valid, w_qkv, w_out, w_in, w_outer, gains, shifts,
    result, summed, vectors,
    xb, ob, mixed, att, nlow, act, dg, one, two, inv_one, inv_two, goi, gai, gmix, probs,
    bias, gatt, hold, dkv, mine, sib, rsb, vec, slots,
    in_sem, out_sem, x_send, x_recv, sib_send, sib_recv, rs_send, rs_recv, ag_send, ag_recv,
    slot_send, slot_recv, pass_send, pass_recv, own_sem,
):
    blocks = BLOCKS[PIECES]
    section, copy, dp = lax.axis_index("section"), lax.axis_index("copy"), lax.axis_index("dp")
    core, layer = lax.rem(dp, 2), lax.div(dp, 2)
    line = chips // 2
    place = jnp.where(copy == 0, layer, chips - 1 - layer)

    def at(position):
        far = position >= line
        return (section, jnp.where(far, 1, 0), 2 * jnp.where(far, chips - 1 - position, position) + core)

    def around(position):
        return lax.rem(position + 2 * chips, chips)

    across = (1 - section, copy, dp)
    sibling = (section, copy, dp + 1 - 2 * core)
    ahead, behind = at(around(place + 1)), at(around(place - 1))

    vec[...] = jnp.zeros_like(vec)
    barrier = pltpu.get_barrier_semaphore()
    for other in (across, sibling, ahead, behind):
        pl.semaphore_signal(barrier, inc=1, device_id=other, device_id_type=MESH)
    load = pltpu.make_async_copy(given, xb.at[0], in_sem)
    load.start()
    load.wait()
    pl.semaphore_wait(barrier, 4)

    def unit_rows(unit):
        return pl.ds(pl.multiple_of(unit * rows, 16), rows)

    def x_copy(unit):
        span = unit_rows(unit)
        return pltpu.make_async_remote_copy(
            src_ref=ob.at[0, span], dst_ref=xb.at[1, span], send_sem=x_send.at[unit],
            recv_sem=x_recv.at[unit], device_id=across, device_id_type=MESH,
        )

    def forward(unit):
        span = unit_rows(unit)
        start = pl.multiple_of(unit * rows, 16)
        hidden = xb[section, span]
        scaled_qkv = mul(hidden, w_qkv[...])
        lane = lax.broadcasted_iota(jnp.int32, scaled_qkv.shape, 1)
        mixed[span] = jnp.where(lane < width, scaled_qkv * 0.125, scaled_qkv).astype(BF16)
        for index, (first, size, begin) in enumerate(blocks):
            allowed = id_col[unit, first : first + size] == id_row[unit, index : index + 1]
            bias[first : first + size] = jnp.where(allowed, 0.0, NEG)

        def pair_step(pair, _):
            lanes = pl.multiple_of(pair * 128, 128)
            for first, size, begin in blocks:
                near = pl.ds(pl.multiple_of(start + begin, 16), WINDOW)
                own = pl.ds(pl.multiple_of(start + first, 16), size)
                query = mixed[own, pl.ds(lanes, 128)]
                keys = halves(mixed[near, pl.ds(pl.multiple_of(width + pair * 128, 128), 128)])
                values = halves(mixed[near, pl.ds(pl.multiple_of(2 * width + pair * 128, 128), 128)])
                shares = []
                for head in range(2):
                    scores = against(query, keys[head]) + bias[first : first + size]
                    weights = jnp.exp(scores - jnp.max(scores, axis=-1, keepdims=True))
                    share = (weights * (1.0 / jnp.sum(weights, axis=-1, keepdims=True))).astype(BF16)
                    probs[own, pl.ds(pl.multiple_of(pair * 512 + head * 256, 256), 256)] = share
                    shares.append(share)
                attended = mul(jnp.concatenate(shares, axis=1), jnp.concatenate(values, axis=0))
                att[own, pl.ds(lanes, 128)] = attended.astype(BF16)
            return 0

        lax.fori_loop(0, width // 128, pair_step, 0)
        scaled, inverse = normalize(xb[section, span].astype(F32) + mul(att[span], w_out[...]))
        one[span] = scaled
        inv_one[span] = inverse
        normed = scaled * gains[0:1] + shifts[0:1]
        hold[...] = normed
        low = normed.astype(BF16)
        nlow[span] = low
        tile = 512
        count = inner_width // tile
        inner = mul(nlow[span], w_in[:, 0:tile])
        outer = hold[...]
        for step in range(count):
            ahead_inner = None
            if step + 1 < count:
                ahead_inner = mul(nlow[span], w_in[:, (step + 1) * tile : (step + 2) * tile])
            cols = pl.ds(step * tile, tile)
            active, slope = gelu(inner)
            act[span, cols] = active
            dg[span, cols] = slope
            outer = outer + mul(active, w_outer[cols])
            inner = ahead_inner
        scaled, inverse = normalize(outer)
        two[span] = scaled
        inv_two[span] = inverse
        ob[section, span] = (scaled * gains[1:2] + shifts[1:2]).astype(BF16)

    def backward(unit):
        span = unit_rows(unit)
        start = pl.multiple_of(unit * rows, 16)
        upstream = xb[1 - section, span].astype(F32) * valid[unit]
        scaled = two[span]
        vec[1:2] += jnp.sum(upstream * scaled, axis=0, keepdims=True)
        vec[3:4] += jnp.sum(upstream, axis=0, keepdims=True)
        grad_two = normalize_back(upstream, scaled, inv_two[span], gains[1:2])
        hold[...] = grad_two
        goi[span] = grad_two.astype(BF16)
        tile = 512
        count = inner_width // tile
        grad_active = against(goi[span], w_outer[0:tile])
        total = hold[...]
        for step in range(count):
            next_active = None
            if step + 1 < count:
                next_active = against(goi[span], w_outer[(step + 1) * tile : (step + 2) * tile])
            cols = pl.ds(step * tile, tile)
            grad_inner = (grad_active * dg[span, cols].astype(F32)).astype(BF16)
            dg[span, cols] = grad_inner
            total = total + against(grad_inner, w_in[:, step * tile : (step + 1) * tile])
            grad_active = next_active
        scaled = one[span]
        vec[0:1] += jnp.sum(total * scaled, axis=0, keepdims=True)
        vec[2:3] += jnp.sum(total, axis=0, keepdims=True)
        grad_one = normalize_back(total, scaled, inv_one[span], gains[0:1])
        hold[...] = grad_one
        low = grad_one.astype(BF16)
        gai[span] = low
        gatt[...] = against(low, w_out[...]).astype(BF16)

        def pair_step(pair, _):
            lanes = pl.multiple_of(pair * 128, 128)
            key_lanes = pl.ds(pl.multiple_of(width + pair * 128, 128), 128)
            value_lanes = pl.ds(pl.multiple_of(2 * width + pair * 128, 128), 128)
            dkv[...] = jnp.zeros_like(dkv)
            for first, size, begin in blocks:
                near = pl.ds(pl.multiple_of(start + begin, 16), WINDOW)
                own = pl.ds(pl.multiple_of(start + first, 16), size)
                queries = halves(mixed[own, pl.ds(lanes, 128)])
                keys = halves(mixed[near, key_lanes])
                values = halves(mixed[near, value_lanes])
                grad_pair = gatt[first : first + size, pl.ds(lanes, 128)]
                shares, grads = [], []
                for head in range(2):
                    share = probs[own, pl.ds(pl.multiple_of(pair * 512 + head * 256, 256), 256)]
                    wide = share.astype(F32)
                    grad_probs = against(grad_pair, values[head])
                    rowwise = jnp.sum(wide * grad_probs, axis=-1, keepdims=True)
                    grads.append((wide * (grad_probs - rowwise)).astype(BF16))
                    shares.append(share)
                grad_query = mul(jnp.concatenate(grads, axis=1), jnp.concatenate(keys, axis=0))
                gmix[own, pl.ds(lanes, 128)] = (grad_query * 0.125).astype(BF16)
                dkv[0, begin : begin + WINDOW] += contract(
                    jnp.concatenate(grads, axis=0), jnp.concatenate(queries, axis=0)
                )
                dkv[1, begin : begin + WINDOW] += contract(
                    jnp.concatenate(shares, axis=0), jnp.concatenate(halves(grad_pair), axis=0)
                )
            gmix[span, key_lanes] = dkv[0].astype(BF16)
            gmix[span, value_lanes] = dkv[1].astype(BF16)
            return 0

        lax.fori_loop(0, width // 128, pair_step, 0)
        ob[1 - section, span] = (hold[...] + against(gmix[span], w_qkv[...])).astype(BF16)

    def slot_step(slot, _):
        is_forward = jnp.where(section == 0, slot < units, lax.rem(slot, 2) == 0)
        unit = jnp.where(section == 0, lax.rem(slot, units), lax.div(slot, 2))

        @pl.when(is_forward)
        def _():
            @pl.when(section == 1)
            def _():
                x_copy(unit).wait_recv()

            forward(unit)

            @pl.when(section == 0)
            def _():
                x_copy(unit).start()

        @pl.when(jnp.logical_not(is_forward))
        def _():
            @pl.when(section == 0)
            def _():
                x_copy(unit).wait_recv()

            backward(unit)

            @pl.when(section == 1)
            def _():
                x_copy(unit).start()

        return 0

    lax.fori_loop(0, 2 * units, slot_step, 0)
    write = pltpu.make_async_copy(ob.at[1], result, out_sem)
    write.start()

    half = 1024
    seg = half // chips

    def sib_copy(group):
        return [
            pltpu.make_async_remote_copy(
                src_ref=probs.at[pl.ds(0, half), pl.ds(pl.multiple_of((group * 2 + way) * 256, 256), 256)],
                dst_ref=sib.at[group, way], send_sem=sib_send.at[group, way],
                recv_sem=sib_recv.at[group, way], device_id=sibling, device_id_type=MESH,
            )
            for way in range(2)
        ]

    def keep(group, block, value):
        value = value.astype(BF16)
        spot = pl.ds(pl.multiple_of(lax.rem(block, 2) * 512, 512), 512)
        here = lax.div(block, 2) == core

        @pl.when(here)
        def _():
            for way in range(2):
                mine[group, way, spot] = value[:, way * 256 : (way + 1) * 256]

        @pl.when(jnp.logical_not(here))
        def _():
            for way in range(2):
                cols = pl.ds((group * 2 + way) * 256, 256)
                probs[spot, cols] = value[:, way * 256 : (way + 1) * 256]

    def outer_block(block, _):
        cols = pl.ds(pl.multiple_of(block * 512, 512), 512)
        keep(0, block, contract(act[:, cols], goi[...]))
        return 0

    def inner_block(block, _):
        cols = pl.ds(pl.multiple_of(block * 512, 512), 512)
        keep(1, block, contract(nlow[...], dg[:, cols]))
        return 0

    def mixed_block(block, _):
        cols = pl.ds(pl.multiple_of((block - 1) * 512, 512), 512)
        keep(2, block, contract(xb[section], gmix[:, cols]))
        return 0

    def joined(group):
        for way, copy_of in enumerate(sib_copy(group)):
            copy_of.wait_recv()
            mine[group, way] = (mine[group, way].astype(F32) + sib[group, way].astype(F32)).astype(BF16)

    def segment(position):
        return pl.ds(pl.multiple_of(around(position) * seg, 16), seg)

    def target(way):
        return tuple(jnp.where(way == 0, a, b) for a, b in zip(ahead, behind))

    def rs_copy(group, way, step, source):
        return pltpu.make_async_remote_copy(
            src_ref=source, dst_ref=rsb.at[group, way, step], send_sem=rs_send.at[group, way, step],
            recv_sem=rs_recv.at[group, way, step], device_id=target(way), device_id_type=MESH,
        )

    def final_rows(position):
        return pl.ds(pl.multiple_of(core * half + around(position) * seg, 16), seg)

    def ag_copy(group, way, step, source, position):
        return pltpu.make_async_remote_copy(
            src_ref=source, dst_ref=summed.at[group, way, final_rows(position)],
            send_sem=ag_send.at[group, way, step], recv_sem=ag_recv.at[group, way, step],
            device_id=target(way), device_id_type=MESH,
        )

    def pass_copy(group, way, source, position):
        return pltpu.make_async_remote_copy(
            src_ref=source, dst_ref=summed.at[group, way, final_rows(position)],
            send_sem=pass_send.at[group, way], recv_sem=pass_recv.at[group, way],
            device_id=sibling, device_id_type=MESH,
        )

    def own_copy(group, way):
        sign = 1 - 2 * way
        return pltpu.make_async_copy(
            rsb.at[group, way, chips - 2], summed.at[group, way, final_rows(place + sign)],
            own_sem.at[group, way],
        )

    def ring(group, way, step):
        sign = 1 - 2 * way

        @pl.when(step == 0)
        def _():
            rs_copy(group, way, 0, mine.at[group, way, segment(place)]).start()

        @pl.when(jnp.logical_and(step >= 1, step < chips))
        def _():
            last = step - 1
            slot = rsb.at[group, way, last]
            rs_copy(group, way, last, slot).wait_recv()
            part = mine[group, way, segment(place - sign * step)]
            rsb[group, way, last] = (rsb[group, way, last].astype(F32) + part.astype(F32)).astype(BF16)

            @pl.when(step < chips - 1)
            def _():
                rs_copy(group, way, step, slot).start()

            @pl.when(step == chips - 1)
            def _():
                ag_copy(group, way, 0, slot, place + sign).start()
                pass_copy(group, way, slot, place + sign).start()
                own_copy(group, way).start()

        @pl.when(jnp.logical_and(step >= chips, step < 2 * chips - 1))
        def _():
            last = step - chips
            position = place - sign * last
            arrived = summed.at[group, way, final_rows(position)]
            ag_copy(group, way, last, arrived, position).wait_recv()

            @pl.when(last + 1 < chips - 1)
            def _():
                ag_copy(group, way, last + 1, arrived, position).start()

            pass_copy(group, way, arrived, position).start()

    def slot_copy(step):
        return pltpu.make_async_remote_copy(
            src_ref=slots.at[step], dst_ref=slots.at[step + 1], send_sem=slot_send.at[step],
            recv_sem=slot_recv.at[step], device_id=ahead, device_id_type=MESH,
        )

    vec_copy = pltpu.make_async_remote_copy(
        src_ref=vec.at[pl.ds(0, 8)], dst_ref=vec.at[pl.ds(8, 8)], send_sem=slot_send.at[chips],
        recv_sem=slot_recv.at[chips], device_id=sibling, device_id_type=MESH,
    )
    vec_copy.start()
    lax.fori_loop(0, 4, outer_block, 0)
    for copy_of in sib_copy(0):
        copy_of.start()
    lax.fori_loop(0, 4, inner_block, 0)
    for copy_of in sib_copy(1):
        copy_of.start()
    joined(0)
    for way in range(2):
        ring(0, way, 0)
    keep(2, 0, contract(att[...], gai[...]))
    lax.fori_loop(1, 4, mixed_block, 0)
    for copy_of in sib_copy(2):
        copy_of.start()
    joined(1)
    joined(2)
    vec_copy.wait()
    slots[0] = vec[0:8] + vec[8:16]

    def round_step(index, _):
        def each(flat, _):
            group, way = lax.div(flat, 2), lax.rem(flat, 2)
            step = jnp.where(group == 0, index, index - 1)

            @pl.when(step >= 0)
            def _():
                ring(group, way, step)

            return 0

        lax.fori_loop(0, 2 * GROUPS, each, 0)

        @pl.when(index < chips)
        def _():
            @pl.when(index > 1)
            def _():
                slot_copy(index - 2).wait_recv()

            slot_copy(index - 1).start()

        return 0

    lax.fori_loop(1, 2 * chips, round_step, 0)
    slot_copy(chips - 2).wait_recv()
    total = jnp.zeros((8, width), F32)
    for position in range(chips):
        total = total + slots[around(place - position)]
    vectors[...] = total

    def drain(flat, _):
        group, way = lax.div(flat, 2), lax.rem(flat, 2)
        own_copy(group, way).wait()

        def each(step, _):
            rs_copy(group, way, step, rsb.at[group, way, 0]).wait_send()
            ag_copy(group, way, step, rsb.at[group, way, 0], place).wait_send()
            return 0

        lax.fori_loop(0, chips - 1, each, 0)
        whole = pltpu.make_async_remote_copy(
            src_ref=summed.at[group, way, pl.ds(0, half)], dst_ref=summed.at[group, way, pl.ds(0, half)],
            send_sem=pass_send.at[group, way], recv_sem=pass_recv.at[group, way],
            device_id=sibling, device_id_type=MESH,
        )
        whole.wait_send()
        whole.wait_recv()
        return 0

    lax.fori_loop(0, 2 * GROUPS, drain, 0)
    for group in range(GROUPS):
        for copy_of in sib_copy(group):
            copy_of.wait_send()

    def drain_slots(step, _):
        slot_copy(step).wait_send()
        return 0

    lax.fori_loop(0, chips - 1, drain_slots, 0)

    def drain_units(unit, _):
        x_copy(unit).wait_send()
        return 0

    lax.fori_loop(0, units, drain_units, 0)
    write.wait()


def per_device(mesh, boundary, sentence_ids, qkv_weight, out_weight, inner_weight, outer_weight, norm_gain, norm_bias):
    micro, local, width = boundary.shape[1], boundary.shape[3], boundary.shape[4]
    inner_width = inner_weight.shape[2]
    length = sentence_ids.shape[2]
    chips = mesh.shape["copy"] * mesh.shape["dp"] // 2
    copy = lax.axis_index("copy")
    reach = local + REACH
    pieces = PIECES
    rows = reach if pieces == 1 else reach // 2 + REACH
    begins = (0,) if pieces == 1 else (0, reach - rows)
    units = micro * pieces
    tokens = units * rows
    own = boundary[0, :, 0]
    ids = sentence_ids[:, 0]

    def swap(strip):
        return lax.ppermute(strip, "copy", [(0, 1), (1, 0)])

    def split(whole):
        return jnp.stack([whole[m, b : b + rows] for m in range(micro) for b in begins])

    strip = lax.dynamic_slice_in_dim(own, (1 - copy) * (local - REACH), REACH, 1)
    strip = swap(strip)
    reaching = jnp.where(
        copy == 0, jnp.concatenate([own, strip], axis=1), jnp.concatenate([strip, own], axis=1)
    )
    given = split(reaching).reshape(tokens, width)
    start = copy * (local - REACH)
    near_ids = lax.dynamic_slice_in_dim(ids, start, reach, 1)
    unit_ids = split(near_ids)
    cuts = (local,) if pieces == 1 else (reach // 2, local, length - reach // 2)
    spot = jnp.arange(length)
    owner = sum((spot >= cut).astype(jnp.int32) for cut in cuts)[None]
    for index, cut in enumerate(cuts):
        crossing = ids == ids[:, cut - 1 : cut]
        left = jnp.sum(crossing & (spot < cut), axis=1, keepdims=True)
        right = jnp.sum(crossing & (spot >= cut), axis=1, keepdims=True)
        owner = jnp.where(crossing, jnp.where(left >= right, index, index + 1), owner)
    near_owner = lax.dynamic_slice_in_dim(owner, start, reach, 1) - copy * pieces
    valid = jnp.stack(
        [near_owner[m, b : b + rows] == j for m in range(micro) for j, b in enumerate(begins)]
    )
    id_row = jnp.stack([unit_ids[:, b : b + WINDOW] for _, _, b in BLOCKS[pieces]], axis=1)

    any_space = pl.BlockSpec(memory_space=pl.ANY)
    vmem = pl.BlockSpec(memory_space=pltpu.VMEM)
    dma = pltpu.SemaphoreType.DMA
    hops = chips - 1
    result, summed, vectors = pl.pallas_call(
        functools.partial(kernel, units, rows, chips, width, inner_width),
        out_shape=(
            jax.ShapeDtypeStruct((tokens, width), BF16),
            jax.ShapeDtypeStruct((GROUPS, 2, 2048, 256), BF16),
            jax.ShapeDtypeStruct((8, width), F32),
        ),
        in_specs=[any_space] + [vmem] * 9,
        out_specs=(any_space, any_space, vmem),
        scratch_shapes=[
            pltpu.VMEM((2, tokens, width), BF16),
            pltpu.VMEM((2, tokens, width), BF16),
            pltpu.VMEM((tokens, 3 * width), BF16),
            pltpu.VMEM((tokens, width), BF16),
            pltpu.VMEM((tokens, width), BF16),
            pltpu.VMEM((tokens, inner_width), BF16),
            pltpu.VMEM((tokens, inner_width), BF16),
            pltpu.VMEM((tokens, width), F32),
            pltpu.VMEM((tokens, width), F32),
            pltpu.VMEM((tokens, 1), F32),
            pltpu.VMEM((tokens, 1), F32),
            pltpu.VMEM((tokens, width), BF16),
            pltpu.VMEM((tokens, width), BF16),
            pltpu.VMEM((tokens, 3 * width), BF16),
            pltpu.VMEM((tokens, HEADS * WINDOW), BF16),
            pltpu.VMEM((rows, WINDOW), F32),
            pltpu.VMEM((rows, width), BF16),
            pltpu.VMEM((rows, width), F32),
            pltpu.VMEM((2, rows, 128), F32),
            pltpu.VMEM((GROUPS, 2, 1024, 256), BF16),
            pltpu.VMEM((GROUPS, 2, 1024, 256), BF16),
            pltpu.VMEM((GROUPS, 2, hops, 1024 // chips, 256), BF16),
            pltpu.VMEM((16, width), F32),
            pltpu.VMEM((chips, 8, width), F32),
            dma, dma, dma((units,)), dma((units,)), dma((GROUPS, 2)), dma((GROUPS, 2)),
            dma((GROUPS, 2, hops)), dma((GROUPS, 2, hops)), dma((GROUPS, 2, hops)), dma((GROUPS, 2, hops)),
            dma((chips + 1,)), dma((chips + 1,)), dma((GROUPS, 2)), dma((GROUPS, 2)), dma((GROUPS, 2)),
        ],
        compiler_params=pltpu.CompilerParams(
            collective_id=0, has_side_effects=True, vmem_limit_bytes=63 * 1024 * 1024
        ),
    )(
        given, unit_ids[:, :, None], id_row, valid[:, :, None].astype(F32),
        qkv_weight[0], out_weight[0], inner_weight[0], outer_weight[0], norm_gain[0], norm_bias[0],
    )

    parts = result.reshape(micro, pieces, rows, width)
    valid = valid.reshape(micro, pieces, rows, 1)
    merged, merged_valid = parts[:, 0], valid[:, 0]
    if pieces == 2:
        cut = begins[1]
        over = rows - cut
        blend = jnp.where(valid[:, 0, cut:], parts[:, 0, cut:], parts[:, 1, :over])
        merged = jnp.concatenate([parts[:, 0, :cut], blend, parts[:, 1, over:]], axis=1)
        merged_valid = jnp.concatenate(
            [valid[:, 0, :cut], valid[:, 0, cut:] | valid[:, 1, :over], valid[:, 1, over:]], axis=1
        )
    strip = swap(lax.dynamic_slice_in_dim(merged, (1 - copy) * local, REACH, 1))
    final = lax.dynamic_slice_in_dim(merged, copy * REACH, local, 1)
    final_valid = lax.dynamic_slice_in_dim(merged_valid, copy * REACH, local, 1)
    edge = (1 - copy) * (local - REACH)
    kept = jnp.where(
        lax.dynamic_slice_in_dim(final_valid, edge, REACH, 1),
        lax.dynamic_slice_in_dim(final, edge, REACH, 1), strip,
    )
    final = lax.dynamic_update_slice_in_dim(final, kept, edge, 1)

    wide = summed.astype(F32)
    joined = jnp.concatenate([wide[:, 0], wide[:, 1]], axis=-1)
    grad_inner = joined[1].reshape(4, 512, 512).transpose(1, 0, 2).reshape(width, inner_width)
    grad_qkv = joined[2, 512:].reshape(3, 512, 512).transpose(1, 0, 2).reshape(width, 3 * width)
    return (
        final[None, :, None], grad_qkv[None], joined[2, :512][None], grad_inner[None], joined[0][None],
        vectors[None, 0:2], vectors[None, 2:4],
    )


def solution(mesh):
    weight = P("section", None, None)
    edge = P("section", None, "dp", "copy", None)
    return jax.shard_map(
        functools.partial(per_device, mesh),
        mesh=mesh,
        in_specs=(edge, P(None, "dp", None)) + (weight,) * 6,
        out_specs=(edge,) + (weight,) * 6,
        check_vma=False,
    )
```

```python
import functools

import jax
import jax.numpy as jnp
from jax import lax
from jax.experimental import pallas as pl
from jax.experimental.pallas import tpu as pltpu
from jax.sharding import PartitionSpec as P

HEADS = 8
REACH = 32
WINDOW = 256
NEG = -1e30
EPS = 1e-05
GROUPS = 3
BLOCKS = ((0, 160, 0), (160, 144, 48))
MESH = pl.DeviceIdType.MESH
F32 = jnp.float32
BF16 = jnp.bfloat16


def mul(left, right):
    return jnp.dot(left, right, preferred_element_type=F32)


def against(left, right):
    return lax.dot_general(left, right, (((1,), (1,)), ((), ())), preferred_element_type=F32)


def contract(left, right):
    return lax.dot_general(left, right, (((0,), (0,)), ((), ())), preferred_element_type=F32)


def gelu(x):
    phi = 0.5 + 0.5 * lax.erf(x * 0.7071067811865476)
    bell = jnp.exp(x * x * -0.5) * 0.3989422804014327
    return (x * phi).astype(BF16), (phi + x * bell).astype(BF16)


def normalize(resid):
    center = resid - jnp.mean(resid, axis=-1, keepdims=True)
    spread = jnp.mean(center * center, axis=-1, keepdims=True)
    inverse = lax.rsqrt(spread + EPS)
    return center * inverse, inverse


def normalize_back(upstream, scaled, inverse, gain):
    tilted = upstream * gain
    first = jnp.mean(tilted, axis=-1, keepdims=True)
    second = jnp.mean(tilted * scaled, axis=-1, keepdims=True)
    return inverse * (tilted - first - scaled * second)


def halves(pair):
    lane = lax.broadcasted_iota(jnp.int32, pair.shape, 1)
    zero = jnp.zeros_like(pair)
    return jnp.where(lane < 64, pair, zero), jnp.where(lane < 64, zero, pair)


def kernel(
    units, rows, chips, width, inner_width,
    boundary, ids, qkv_weight, out_weight, inner_weight, outer_weight, gain_rows, shift_rows,
    result, summed, vectors,
    w_qkv, w_out, w_in, w_outer, info, column,
    xb, ob, mixed, att, nlow, act, dg, one, two, inv_one, inv_two, goi, gai, gmix, probs, scale,
    bias, gatt, hold, dkv, strip, mine, sib, rsb, vec, slots,
    weight_sem, in_sem, out_sem, x_send, x_recv, y_send, y_recv, sib_send, sib_recv, rs_send, rs_recv,
    ag_send, ag_recv, slot_send, slot_recv, pass_send, pass_recv, own_sem,
):
    blocks = BLOCKS
    micro, local = boundary.shape[1], boundary.shape[3]
    length = ids.shape[2]
    reach = local + REACH
    shift = reach - rows
    section, copy, dp = lax.axis_index("section"), lax.axis_index("copy"), lax.axis_index("dp")
    core, layer = lax.rem(dp, 2), lax.div(dp, 2)
    line = chips // 2
    place = jnp.where(copy == 0, layer, chips - 1 - layer)
    gains, shifts = gain_rows.at[0], shift_rows.at[0]

    def either(first, second):
        return jnp.where(copy == 0, first, second)

    def at(position):
        far = position >= line
        return (section, jnp.where(far, 1, 0), 2 * jnp.where(far, chips - 1 - position, position) + core)

    def around(position):
        return lax.rem(position + 2 * chips, chips)

    across = (1 - section, copy, dp)
    beside = (section, 1 - copy, dp)
    sibling = (section, copy, dp + 1 - 2 * core)
    ahead, behind = at(around(place + 1)), at(around(place - 1))

    def load(unit):
        group, odd = unit // 2, unit % 2
        if odd:
            source, target, size = either(shift, 0), either(0, REACH), rows - REACH
        else:
            source, target, size = either(0, local - rows), 0, rows
        return pltpu.make_async_copy(
            boundary.at[0, group, 0, pl.ds(pl.multiple_of(source, 16), size)],
            xb.at[0, pl.ds(pl.multiple_of(unit * rows + target, 16), size)], in_sem.at[unit],
        )

    def halo(group):
        source, target = either(local - REACH, 0), (2 * group + 1) * rows + either(0, rows - REACH)
        return pltpu.make_async_remote_copy(
            src_ref=boundary.at[0, group, 0, pl.ds(pl.multiple_of(source, 16), REACH)],
            dst_ref=xb.at[0, pl.ds(pl.multiple_of(target, 16), REACH)],
            send_sem=y_send.at[group], recv_sem=y_recv.at[group],
            device_id=beside, device_id_type=MESH,
        )

    weights = [
        pltpu.make_async_copy(source.at[0], target, weight_sem.at[index])
        for index, (source, target) in enumerate(
            ((qkv_weight, w_qkv), (out_weight, w_out), (inner_weight, w_in), (outer_weight, w_outer))
        )
    ]
    vec[...] = jnp.zeros_like(vec)
    barrier = pltpu.get_barrier_semaphore()
    for other in (across, beside, sibling, ahead, behind):
        pl.semaphore_signal(barrier, inc=1, device_id=other, device_id_type=MESH)
    load(0).start()
    weights[0].start()
    for unit in range(1, units):
        load(unit).start()
    for weight in weights[1:]:
        weight.start()

    spot = lax.broadcasted_iota(jnp.int32, (micro, length), 1)
    sentence = ids[:, 0, :]
    cuts = (reach // 2, local, length - reach // 2)
    owner = jnp.zeros((micro, length), jnp.int32)
    for cut in cuts:
        owner = owner + jnp.where(spot >= cut, 1, 0)
    for index, cut in enumerate(cuts):
        crossing = sentence == sentence[:, cut - 1 : cut]
        left = jnp.sum(jnp.where(crossing & (spot < cut), 1.0, 0.0), axis=1, keepdims=True)
        right = jnp.sum(jnp.where(crossing & (spot >= cut), 1.0, 0.0), axis=1, keepdims=True)
        side = jnp.where(left >= right, index, index + 1)
        owner = jnp.where(crossing, side, owner)
    info[...] = jnp.zeros_like(info)
    info[0:micro] = sentence.astype(F32)
    info[micro : 2 * micro] = owner.astype(F32)
    column[...] = info[...].T

    def piece_of(unit):
        odd = lax.rem(unit, 2)
        return either(odd, 1 - odd)

    def begin_of(unit):
        return copy * (local - REACH) + piece_of(unit) * shift

    def pick(unit, first, size, kind):
        spots = pl.ds(pl.multiple_of(begin_of(unit) + first, 16), size)
        both = column[spots, kind * micro : (kind + 1) * micro]
        return jnp.where(unit < 2, both[:, 0:1], both[:, 1:2])

    def owned(unit, first, size):
        return pick(unit, first, size, 1) == (2 * copy + piece_of(unit)).astype(F32)

    load(0).wait()
    weights[0].wait()

    def unit_rows(unit):
        return pl.ds(pl.multiple_of(unit * rows, 16), rows)

    def x_copy(unit):
        span = unit_rows(unit)
        return pltpu.make_async_remote_copy(
            src_ref=ob.at[0, span], dst_ref=xb.at[1, span], send_sem=x_send.at[unit],
            recv_sem=x_recv.at[unit], device_id=across, device_id_type=MESH,
        )

    def forward(unit, slot):
        span = unit_rows(unit)
        start = pl.multiple_of(unit * rows, 16)
        hidden = xb[section, span]
        scaled_qkv = mul(hidden, w_qkv[...])
        lane = lax.broadcasted_iota(jnp.int32, scaled_qkv.shape, 1)
        mixed[span] = jnp.where(lane < width, scaled_qkv * 0.125, scaled_qkv).astype(BF16)
        for index, (first, size, begin) in enumerate(blocks):
            turned = pltpu.roll(info[0:8], length - begin_of(unit) - begin, 1)[0:micro, 0:WINDOW]
            near_ids = jnp.where(unit < 2, turned[0:1], turned[1:2])
            allowed = pick(unit, first, size, 0) == near_ids
            bias[first : first + size] = jnp.where(allowed, 0.0, NEG)

        def pair_step(pair, _):
            lanes = pl.multiple_of(pair * 128, 128)
            for first, size, begin in blocks:
                near = pl.ds(pl.multiple_of(start + begin, 16), WINDOW)
                own = pl.ds(pl.multiple_of(start + first, 16), size)
                query = mixed[own, pl.ds(lanes, 128)]
                keys = halves(mixed[near, pl.ds(pl.multiple_of(width + pair * 128, 128), 128)])
                values = halves(mixed[near, pl.ds(pl.multiple_of(2 * width + pair * 128, 128), 128)])
                ones = halves(jnp.ones((WINDOW, 128), BF16))
                shares = []
                for head in range(2):
                    scores = against(query, keys[head]) + bias[first : first + size]
                    share = jnp.exp(scores - jnp.max(scores, axis=-1, keepdims=True)).astype(BF16)
                    probs[own, pl.ds(pl.multiple_of(pair * 512 + head * 256, 256), 256)] = share
                    shares.append(share)
                sides = [jnp.concatenate([values[head], ones[head]], axis=1) for head in range(2)]
                sums = mul(jnp.concatenate(shares, axis=1), jnp.concatenate(sides, axis=0))
                inverse = 1.0 / sums[:, 128:]
                att[own, pl.ds(lanes, 128)] = (sums[:, :128] * inverse).astype(BF16)
                scale[own, pl.ds(lanes, 128)] = inverse
            return 0

        lax.fori_loop(0, width // 128, pair_step, 0, unroll=True)
        @pl.when(slot == 0)
        def _():
            for weight in weights[1:]:
                weight.wait()
            for odd in range(1, units):
                load(odd).wait()
            pl.semaphore_wait(barrier, 5)
            for group in range(micro):
                halo(group).start()

        scaled, inverse = normalize(xb[section, span].astype(F32) + mul(att[span], w_out[...]))
        one[span] = scaled
        inv_one[span] = inverse
        normed = scaled * gains[0:1] + shifts[0:1]
        hold[...] = normed
        low = normed.astype(BF16)
        nlow[span] = low
        tile = 512
        count = inner_width // tile
        inner = mul(nlow[span], w_in[:, 0:tile])
        outer = hold[...]
        for step in range(count):
            ahead_inner = None
            if step + 1 < count:
                ahead_inner = mul(nlow[span], w_in[:, (step + 1) * tile : (step + 2) * tile])
            cols = pl.ds(step * tile, tile)
            active, slope = gelu(inner)
            act[span, cols] = active
            dg[span, cols] = slope
            outer = outer + mul(active, w_outer[cols])
            inner = ahead_inner
        scaled, inverse = normalize(outer)
        two[span] = scaled
        inv_two[span] = inverse
        ob[section, span] = (scaled * gains[1:2] + shifts[1:2]).astype(BF16)

    def backward(unit):
        span = unit_rows(unit)
        start = pl.multiple_of(unit * rows, 16)
        upstream = jnp.where(owned(unit, 0, rows), xb[1 - section, span].astype(F32), 0.0)
        scaled = two[span]
        vec[1:2] += jnp.sum(upstream * scaled, axis=0, keepdims=True)
        vec[3:4] += jnp.sum(upstream, axis=0, keepdims=True)
        grad_two = normalize_back(upstream, scaled, inv_two[span], gains[1:2])
        hold[...] = grad_two
        goi[span] = grad_two.astype(BF16)
        tile = 512
        count = inner_width // tile
        grad_active = against(goi[span], w_outer[0:tile])
        total = hold[...]
        for step in range(count):
            next_active = None
            if step + 1 < count:
                next_active = against(goi[span], w_outer[(step + 1) * tile : (step + 2) * tile])
            cols = pl.ds(step * tile, tile)
            grad_inner = (grad_active * dg[span, cols].astype(F32)).astype(BF16)
            dg[span, cols] = grad_inner
            total = total + against(grad_inner, w_in[:, step * tile : (step + 1) * tile])
            grad_active = next_active
        scaled = one[span]
        vec[0:1] += jnp.sum(total * scaled, axis=0, keepdims=True)
        vec[2:3] += jnp.sum(total, axis=0, keepdims=True)
        grad_one = normalize_back(total, scaled, inv_one[span], gains[0:1])
        hold[...] = grad_one
        low = grad_one.astype(BF16)
        gai[span] = low
        gatt[...] = (against(low, w_out[...]) * scale[span]).astype(BF16)

        def pair_step(pair, _):
            lanes = pl.multiple_of(pair * 128, 128)
            key_lanes = pl.ds(pl.multiple_of(width + pair * 128, 128), 128)
            value_lanes = pl.ds(pl.multiple_of(2 * width + pair * 128, 128), 128)
            dkv[...] = jnp.zeros_like(dkv)
            for first, size, begin in blocks:
                near = pl.ds(pl.multiple_of(start + begin, 16), WINDOW)
                own = pl.ds(pl.multiple_of(start + first, 16), size)
                queries = halves(mixed[own, pl.ds(lanes, 128)])
                keys = halves(mixed[near, key_lanes])
                values = halves(mixed[near, value_lanes])
                minus = halves(jnp.full((WINDOW, 128), -1.0, BF16))
                grad_pair = gatt[first : first + size, pl.ds(lanes, 128)]
                paired = (grad_pair.astype(F32) * att[own, pl.ds(lanes, 128)].astype(F32)).astype(BF16)
                left = jnp.concatenate([grad_pair, paired], axis=1)
                shares, grads = [], []
                for head in range(2):
                    share = probs[own, pl.ds(pl.multiple_of(pair * 512 + head * 256, 256), 256)]
                    tilt = against(left, jnp.concatenate([values[head], minus[head]], axis=1))
                    grads.append((share.astype(F32) * tilt).astype(BF16))
                    shares.append(share)
                grad_query = mul(jnp.concatenate(grads, axis=1), jnp.concatenate(keys, axis=0))
                gmix[own, pl.ds(lanes, 128)] = (grad_query * 0.125).astype(BF16)
                grad_key = contract(jnp.concatenate(queries, axis=0), jnp.concatenate(grads, axis=0))
                grad_value = contract(
                    jnp.concatenate(halves(grad_pair), axis=0), jnp.concatenate(shares, axis=0)
                )
                dkv[0, begin : begin + WINDOW] += grad_key.T
                dkv[1, begin : begin + WINDOW] += grad_value.T
            gmix[span, key_lanes] = dkv[0].astype(BF16)
            gmix[span, value_lanes] = dkv[1].astype(BF16)
            return 0

        lax.fori_loop(0, width // 128, pair_step, 0, unroll=True)
        ob[1 - section, span] = (hold[...] + against(gmix[span], w_qkv[...])).astype(BF16)

    def slot_step(slot, _):
        is_forward = jnp.where(section == 0, slot < units, lax.rem(slot, 2) == 0)
        unit = jnp.where(section == 0, lax.rem(slot, units), lax.div(slot, 2))

        first_use = jnp.where(section == 0, is_forward, jnp.logical_not(is_forward))

        @pl.when(jnp.logical_and(first_use, lax.rem(unit, 2) == 1))
        def _():
            halo(lax.div(unit, 2)).wait_recv()

        @pl.when(is_forward)
        def _():
            @pl.when(section == 1)
            def _():
                x_copy(unit).wait_recv()

            forward(unit, slot)

            @pl.when(section == 0)
            def _():
                x_copy(unit).start()

        @pl.when(jnp.logical_not(is_forward))
        def _():
            @pl.when(section == 0)
            def _():
                x_copy(unit).wait_recv()

            backward(unit)

            @pl.when(section == 1)
            def _():
                x_copy(unit).start()

        return 0

    lax.fori_loop(0, 2 * units, slot_step, 0)

    def strip_copy(group):
        source = (2 * group + 1) * rows + either(rows - REACH, 0)
        return pltpu.make_async_remote_copy(
            src_ref=ob.at[1, pl.ds(pl.multiple_of(source, 16), REACH)], dst_ref=strip.at[group],
            send_sem=y_send.at[micro + group], recv_sem=y_recv.at[micro + group],
            device_id=beside, device_id_type=MESH,
        )

    def outputs(group, side):
        even, odd = 2 * group * rows, (2 * group + 1) * rows
        if side == 0:
            parts = ((even, 0, shift), (odd, shift, local - shift))
        else:
            parts = ((odd + REACH, 0, shift - REACH), (even, shift - REACH, rows))
        return [
            pltpu.make_async_copy(
                ob.at[1, pl.ds(source, size)], result.at[0, group, 0, pl.ds(target, size)],
                out_sem.at[group, index],
            )
            for index, (source, target, size) in enumerate(parts)
        ]

    for group in range(micro):
        strip_copy(group).start()

    def finish():
        for group in range(micro):
            low_unit, high_unit = 2 * group + copy, 2 * group + 1 - copy
            over = rows - shift
            kept = pl.ds(pl.multiple_of(low_unit * rows + shift, 16), over)
            moved = pl.ds(pl.multiple_of(high_unit * rows, 16), over)
            ob[1, moved] = jnp.where(owned(low_unit, shift, over), ob[1, kept], ob[1, moved])
            strip_copy(group).wait_recv()
            odd_unit = 2 * group + 1
            first = either(shift, REACH)
            edge = pl.ds(pl.multiple_of(odd_unit * rows + first, 16), REACH)
            ob[1, edge] = jnp.where(owned(odd_unit, first, REACH), ob[1, edge], strip[group])
        for side in range(2):
            @pl.when(copy == side)
            def _():
                for group in range(micro):
                    for part in outputs(group, side):
                        part.start()

    half = 1024
    seg = half // chips

    def sib_copy(group):
        return [
            pltpu.make_async_remote_copy(
                src_ref=probs.at[pl.ds(0, half), pl.ds(pl.multiple_of((group * 2 + way) * 256, 256), 256)],
                dst_ref=sib.at[group, way], send_sem=sib_send.at[group, way],
                recv_sem=sib_recv.at[group, way], device_id=sibling, device_id_type=MESH,
            )
            for way in range(2)
        ]

    def keep(group, block, value):
        value = value.astype(BF16)
        spot = pl.ds(pl.multiple_of(lax.rem(block, 2) * 512, 512), 512)
        here = lax.div(block, 2) == core

        @pl.when(here)
        def _():
            for way in range(2):
                mine[group, way, spot] = value[:, way * 256 : (way + 1) * 256]

        @pl.when(jnp.logical_not(here))
        def _():
            for way in range(2):
                cols = pl.ds((group * 2 + way) * 256, 256)
                probs[spot, cols] = value[:, way * 256 : (way + 1) * 256]

    def outer_block(block, _):
        cols = pl.ds(pl.multiple_of(block * 512, 512), 512)
        keep(0, block, contract(act[:, cols], goi[...]))
        return 0

    def inner_block(block, _):
        cols = pl.ds(pl.multiple_of(block * 512, 512), 512)
        keep(1, block, contract(nlow[...], dg[:, cols]))
        return 0

    def mixed_block(block, _):
        cols = pl.ds(pl.multiple_of((block - 1) * 512, 512), 512)
        keep(2, block, contract(xb[section], gmix[:, cols]))
        return 0

    def joined(group):
        for way, copy_of in enumerate(sib_copy(group)):
            copy_of.wait_recv()
            mine[group, way] = (mine[group, way].astype(F32) + sib[group, way].astype(F32)).astype(BF16)

    def segment(position):
        return pl.ds(pl.multiple_of(around(position) * seg, 16), seg)

    def target(way):
        return tuple(jnp.where(way == 0, a, b) for a, b in zip(ahead, behind))

    def rs_copy(group, way, step, source):
        return pltpu.make_async_remote_copy(
            src_ref=source, dst_ref=rsb.at[group, way, step], send_sem=rs_send.at[group, way, step],
            recv_sem=rs_recv.at[group, way, step], device_id=target(way), device_id_type=MESH,
        )

    def final_rows(position):
        return pl.ds(pl.multiple_of(core * half + around(position) * seg, 16), seg)

    def ag_copy(group, way, step, source, position):
        return pltpu.make_async_remote_copy(
            src_ref=source, dst_ref=summed.at[group, way, final_rows(position)],
            send_sem=ag_send.at[group, way, step], recv_sem=ag_recv.at[group, way, step],
            device_id=target(way), device_id_type=MESH,
        )

    def pass_copy(group, way, source, position):
        return pltpu.make_async_remote_copy(
            src_ref=source, dst_ref=summed.at[group, way, final_rows(position)],
            send_sem=pass_send.at[group, way], recv_sem=pass_recv.at[group, way],
            device_id=sibling, device_id_type=MESH,
        )

    def own_copy(group, way):
        sign = 1 - 2 * way
        return pltpu.make_async_copy(
            rsb.at[group, way, chips - 2], summed.at[group, way, final_rows(place + sign)],
            own_sem.at[group, way],
        )

    def ring(group, way, step):
        sign = 1 - 2 * way

        @pl.when(step == 0)
        def _():
            rs_copy(group, way, 0, mine.at[group, way, segment(place)]).start()

        @pl.when(jnp.logical_and(step >= 1, step < chips))
        def _():
            last = step - 1
            slot = rsb.at[group, way, last]
            rs_copy(group, way, last, slot).wait_recv()
            part = mine[group, way, segment(place - sign * step)]
            rsb[group, way, last] = (rsb[group, way, last].astype(F32) + part.astype(F32)).astype(BF16)

            @pl.when(step < chips - 1)
            def _():
                rs_copy(group, way, step, slot).start()

            @pl.when(step == chips - 1)
            def _():
                ag_copy(group, way, 0, slot, place + sign).start()
                pass_copy(group, way, slot, place + sign).start()
                own_copy(group, way).start()

        @pl.when(jnp.logical_and(step >= chips, step < 2 * chips - 1))
        def _():
            last = step - chips
            position = place - sign * last
            arrived = summed.at[group, way, final_rows(position)]
            ag_copy(group, way, last, arrived, position).wait_recv()

            @pl.when(last + 1 < chips - 1)
            def _():
                ag_copy(group, way, last + 1, arrived, position).start()

            pass_copy(group, way, arrived, position).start()

    def slot_copy(step):
        return pltpu.make_async_remote_copy(
            src_ref=slots.at[step], dst_ref=slots.at[step + 1], send_sem=slot_send.at[step],
            recv_sem=slot_recv.at[step], device_id=ahead, device_id_type=MESH,
        )

    vec_copy = pltpu.make_async_remote_copy(
        src_ref=vec.at[pl.ds(0, 8)], dst_ref=vec.at[pl.ds(8, 8)], send_sem=slot_send.at[chips],
        recv_sem=slot_recv.at[chips], device_id=sibling, device_id_type=MESH,
    )
    vec_copy.start()
    lax.fori_loop(0, 4, outer_block, 0)
    for copy_of in sib_copy(0):
        copy_of.start()
    lax.fori_loop(0, 4, inner_block, 0)
    for copy_of in sib_copy(1):
        copy_of.start()
    joined(0)
    for way in range(2):
        ring(0, way, 0)
    keep(2, 0, contract(att[...], gai[...]))
    lax.fori_loop(1, 4, mixed_block, 0)
    for copy_of in sib_copy(2):
        copy_of.start()
    joined(1)
    joined(2)
    finish()
    vec_copy.wait()
    slots[0] = vec[0:8] + vec[8:16]

    def round_step(index, _):
        def each(flat, _):
            group, way = lax.div(flat, 2), lax.rem(flat, 2)
            step = jnp.where(group == 0, index, index - 1)

            @pl.when(step >= 0)
            def _():
                ring(group, way, step)

            return 0

        lax.fori_loop(0, 2 * GROUPS, each, 0)

        @pl.when(index < chips)
        def _():
            @pl.when(index > 1)
            def _():
                slot_copy(index - 2).wait_recv()

            slot_copy(index - 1).start()

        return 0

    lax.fori_loop(1, 2 * chips, round_step, 0)
    slot_copy(chips - 2).wait_recv()
    total = jnp.zeros((8, width), F32)
    for position in range(chips):
        total = total + slots[around(place - position)]
    vectors[...] = total

    def drain(flat, _):
        group, way = lax.div(flat, 2), lax.rem(flat, 2)
        own_copy(group, way).wait()

        def each(step, _):
            rs_copy(group, way, step, rsb.at[group, way, 0]).wait_send()
            ag_copy(group, way, step, rsb.at[group, way, 0], place).wait_send()
            return 0

        lax.fori_loop(0, chips - 1, each, 0)
        whole = pltpu.make_async_remote_copy(
            src_ref=summed.at[group, way, pl.ds(0, half)], dst_ref=summed.at[group, way, pl.ds(0, half)],
            send_sem=pass_send.at[group, way], recv_sem=pass_recv.at[group, way],
            device_id=sibling, device_id_type=MESH,
        )
        whole.wait_send()
        whole.wait_recv()
        return 0

    lax.fori_loop(0, 2 * GROUPS, drain, 0)
    for group in range(GROUPS):
        for copy_of in sib_copy(group):
            copy_of.wait_send()

    def drain_slots(step, _):
        slot_copy(step).wait_send()
        return 0

    lax.fori_loop(0, chips - 1, drain_slots, 0)

    def drain_units(unit, _):
        x_copy(unit).wait_send()
        return 0

    lax.fori_loop(0, units, drain_units, 0)
    for group in range(micro):
        halo(group).wait_send()
        strip_copy(group).wait_send()
    for side in range(2):
        @pl.when(copy == side)
        def _():
            for group in range(micro):
                for part in outputs(group, side):
                    part.wait()


def widen(summed, vectors, qkv, out, inner, outer, gain, shift):
    step = pl.program_id(0)
    wide = jnp.concatenate([summed[0, 0], summed[0, 1]], axis=1).astype(F32)

    @pl.when(step < 4)
    def _():
        outer[0] = wide

    @pl.when(jnp.logical_and(step >= 4, step < 8))
    def _():
        inner[0] = wide

    @pl.when(step == 8)
    def _():
        out[0] = wide

    @pl.when(step > 8)
    def _():
        qkv[0] = wide

    gain[0] = vectors[0:2]
    shift[0] = vectors[2:4]


def per_device(mesh, boundary, sentence_ids, qkv_weight, out_weight, inner_weight, outer_weight, norm_gain, norm_bias):
    micro, local, width = boundary.shape[1], boundary.shape[3], boundary.shape[4]
    inner_width = inner_weight.shape[2]
    length = sentence_ids.shape[2]
    chips = mesh.shape["copy"] * mesh.shape["dp"] // 2
    rows = (local + REACH) // 2 + REACH
    units = micro * 2
    tokens = units * rows
    any_space = pl.BlockSpec(memory_space=pl.ANY)
    vmem = pl.BlockSpec(memory_space=pltpu.VMEM)
    dma = pltpu.SemaphoreType.DMA
    hops = chips - 1
    result, summed, vectors = pl.pallas_call(
        functools.partial(kernel, units, rows, chips, width, inner_width),
        out_shape=(
            jax.ShapeDtypeStruct(boundary.shape, BF16),
            jax.ShapeDtypeStruct((GROUPS, 2, 2048, 256), BF16),
            jax.ShapeDtypeStruct((8, width), F32),
        ),
        in_specs=[any_space, vmem] + [any_space] * 4 + [vmem] * 2,
        out_specs=(any_space, any_space, vmem),
        scratch_shapes=[
            pltpu.VMEM((width, 3 * width), BF16),
            pltpu.VMEM((width, width), BF16),
            pltpu.VMEM((width, inner_width), BF16),
            pltpu.VMEM((inner_width, width), BF16),
            pltpu.VMEM((128, length), F32),
            pltpu.VMEM((length, 128), F32),
            pltpu.VMEM((2, tokens, width), BF16),
            pltpu.VMEM((2, tokens, width), BF16),
            pltpu.VMEM((tokens, 3 * width), BF16),
            pltpu.VMEM((tokens, width), BF16),
            pltpu.VMEM((tokens, width), BF16),
            pltpu.VMEM((tokens, inner_width), BF16),
            pltpu.VMEM((tokens, inner_width), BF16),
            pltpu.VMEM((tokens, width), F32),
            pltpu.VMEM((tokens, width), F32),
            pltpu.VMEM((tokens, 1), F32),
            pltpu.VMEM((tokens, 1), F32),
            pltpu.VMEM((tokens, width), BF16),
            pltpu.VMEM((tokens, width), BF16),
            pltpu.VMEM((tokens, 3 * width), BF16),
            pltpu.VMEM((tokens, HEADS * WINDOW), BF16),
            pltpu.VMEM((tokens, width), F32),
            pltpu.VMEM((rows, WINDOW), F32),
            pltpu.VMEM((rows, width), BF16),
            pltpu.VMEM((rows, width), F32),
            pltpu.VMEM((2, rows, 128), F32),
            pltpu.VMEM((micro, REACH, width), BF16),
            pltpu.VMEM((GROUPS, 2, 1024, 256), BF16),
            pltpu.VMEM((GROUPS, 2, 1024, 256), BF16),
            pltpu.VMEM((GROUPS, 2, hops, 1024 // chips, 256), BF16),
            pltpu.VMEM((16, width), F32),
            pltpu.VMEM((chips, 8, width), F32),
            dma((4,)), dma((units,)), dma((micro, 2)), dma((units,)), dma((units,)),
            dma((2 * micro,)), dma((2 * micro,)), dma((GROUPS, 2)), dma((GROUPS, 2)),
            dma((GROUPS, 2, hops)), dma((GROUPS, 2, hops)), dma((GROUPS, 2, hops)), dma((GROUPS, 2, hops)),
            dma((chips + 1,)), dma((chips + 1,)), dma((GROUPS, 2)), dma((GROUPS, 2)), dma((GROUPS, 2)),
        ],
        compiler_params=pltpu.CompilerParams(
            collective_id=0, has_side_effects=True, vmem_limit_bytes=63 * 1024 * 1024
        ),
    )(boundary, sentence_ids, qkv_weight, out_weight, inner_weight, outer_weight, norm_gain, norm_bias)

    def block(low, count, column):
        def index(step):
            spot = jnp.clip(step - low, 0, count - 1)
            return (0, 0, spot) if column else (0, spot, 0)

        return pl.BlockSpec((1, 512, 512), index)

    vector = pl.BlockSpec((1, 2, width), lambda step: (0, 0, 0))
    grad_qkv, grad_out, grad_inner, grad_outer, grad_gain, grad_bias = pl.pallas_call(
        widen,
        grid=(4 * GROUPS,),
        out_shape=tuple(
            jax.ShapeDtypeStruct(item.shape, F32)
            for item in (qkv_weight, out_weight, inner_weight, outer_weight, norm_gain, norm_bias)
        ),
        in_specs=[
            pl.BlockSpec((1, 2, 512, 256), lambda step: (step // 4, 0, step % 4, 0)),
            pl.BlockSpec((8, width), lambda step: (0, 0)),
        ],
        out_specs=(
            block(9, 3, True), block(8, 1, True), block(4, 4, True), block(0, 4, False), vector, vector,
        ),
    )(summed, vectors)
    return (result, grad_qkv, grad_out, grad_inner, grad_outer, grad_gain, grad_bias)


def solution(mesh):
    weight = P("section", None, None)
    edge = P("section", None, "dp", "copy", None)
    return jax.shard_map(
        functools.partial(per_device, mesh),
        mesh=mesh,
        in_specs=(edge, P(None, "dp", None)) + (weight,) * 6,
        out_specs=(edge,) + (weight,) * 6,
        check_vma=False,
    )
```

```python
import functools

import jax
import jax.numpy as jnp
from jax import lax
from jax.experimental import pallas as pl
from jax.experimental.pallas import tpu as pltpu
from jax.sharding import PartitionSpec as P

HEADS = 8
REACH = 32
WINDOW = 256
NEG = -1e30
EPS = 1e-05
GROUPS = 3
BLOCKS = ((0, 192, 0), (192, 112, 128))
MESH = pl.DeviceIdType.MESH
F32 = jnp.float32
BF16 = jnp.bfloat16


def mul(left, right):
    return jnp.dot(left, right, preferred_element_type=F32)


def against(left, right):
    return lax.dot_general(left, right, (((1,), (1,)), ((), ())), preferred_element_type=F32)


def contract(left, right):
    return lax.dot_general(left, right, (((0,), (0,)), ((), ())), preferred_element_type=F32)


def gelu(x):
    phi = 0.5 + 0.5 * lax.erf(x * 0.7071067811865476)
    bell = jnp.exp(x * x * -0.5) * 0.3989422804014327
    return (x * phi).astype(BF16), (phi + x * bell).astype(BF16)


def normalize(resid):
    center = resid - jnp.mean(resid, axis=-1, keepdims=True)
    spread = jnp.mean(center * center, axis=-1, keepdims=True)
    inverse = lax.rsqrt(spread + EPS)
    return center * inverse, inverse


def normalize_back(upstream, scaled, inverse, gain):
    tilted = upstream * gain
    first = jnp.mean(tilted, axis=-1, keepdims=True)
    second = jnp.mean(tilted * scaled, axis=-1, keepdims=True)
    return inverse * (tilted - first - scaled * second)


def halves(pair):
    lane = lax.broadcasted_iota(jnp.int32, pair.shape, 1)
    zero = jnp.zeros_like(pair)
    return jnp.where(lane < 64, pair, zero), jnp.where(lane < 64, zero, pair)


def kernel(
    units, rows, chips, width, inner_width,
    boundary, ids, qkv_weight, out_weight, inner_weight, outer_weight, gain_rows, shift_rows,
    result, summed, vectors,
    w_qkv, w_out, w_in, w_outer, info, column,
    xb, ob, mixed, att, nlow, act, dg, one, two, inv_one, inv_two, goi, gai, gmix, probs, scale,
    bias, gatt, hold, dkv, strip, mine, sib, rsb, vec, slots,
    weight_sem, in_sem, out_sem, x_send, x_recv, y_send, y_recv, sib_send, sib_recv, rs_send, rs_recv,
    ag_send, ag_recv, slot_send, slot_recv, pass_send, pass_recv, own_sem,
):
    blocks = BLOCKS
    micro, local = boundary.shape[1], boundary.shape[3]
    length = ids.shape[2]
    reach = local + REACH
    shift = reach - rows
    section, copy, dp = lax.axis_index("section"), lax.axis_index("copy"), lax.axis_index("dp")
    core, layer = lax.rem(dp, 2), lax.div(dp, 2)
    line = chips // 2
    place = jnp.where(copy == 0, layer, chips - 1 - layer)
    gains, shifts = gain_rows.at[0], shift_rows.at[0]

    def either(first, second):
        return jnp.where(copy == 0, first, second)

    def at(position):
        far = position >= line
        return (section, jnp.where(far, 1, 0), 2 * jnp.where(far, chips - 1 - position, position) + core)

    def around(position):
        return lax.rem(position + 2 * chips, chips)

    across = (1 - section, copy, dp)
    beside = (section, 1 - copy, dp)
    sibling = (section, copy, dp + 1 - 2 * core)
    ahead, behind = at(around(place + 1)), at(around(place - 1))

    def load(unit):
        group, odd = unit // 2, unit % 2
        if odd:
            source, target, size = either(shift, 0), either(0, REACH), rows - REACH
        else:
            source, target, size = either(0, local - rows), 0, rows
        return pltpu.make_async_copy(
            boundary.at[0, group, 0, pl.ds(pl.multiple_of(source, 16), size)],
            xb.at[0, pl.ds(pl.multiple_of(unit * rows + target, 16), size)], in_sem.at[unit],
        )

    def halo(group):
        source, target = either(local - REACH, 0), (2 * group + 1) * rows + either(0, rows - REACH)
        return pltpu.make_async_remote_copy(
            src_ref=boundary.at[0, group, 0, pl.ds(pl.multiple_of(source, 16), REACH)],
            dst_ref=xb.at[0, pl.ds(pl.multiple_of(target, 16), REACH)],
            send_sem=y_send.at[group], recv_sem=y_recv.at[group],
            device_id=beside, device_id_type=MESH,
        )

    weights = [
        pltpu.make_async_copy(source.at[0], target, weight_sem.at[index])
        for index, (source, target) in enumerate(
            ((qkv_weight, w_qkv), (out_weight, w_out), (inner_weight, w_in), (outer_weight, w_outer))
        )
    ]
    vec[...] = jnp.zeros_like(vec)
    mixed[...] = jnp.zeros_like(mixed)
    barrier = pltpu.get_barrier_semaphore()
    for other in (across, beside, sibling, ahead, behind):
        pl.semaphore_signal(barrier, inc=1, device_id=other, device_id_type=MESH)
    load(0).start()
    weights[0].start()
    for unit in range(1, units):
        load(unit).start()
    for weight in weights[1:]:
        weight.start()

    spot = lax.broadcasted_iota(jnp.int32, (micro, length), 1)
    sentence = ids[:, 0, :]
    cuts = (reach // 2, local, length - reach // 2)
    owner = jnp.zeros((micro, length), jnp.int32)
    for cut in cuts:
        owner = owner + jnp.where(spot >= cut, 1, 0)
    for index, cut in enumerate(cuts):
        crossing = sentence == sentence[:, cut - 1 : cut]
        left = jnp.sum(jnp.where(crossing & (spot < cut), 1.0, 0.0), axis=1, keepdims=True)
        right = jnp.sum(jnp.where(crossing & (spot >= cut), 1.0, 0.0), axis=1, keepdims=True)
        side = jnp.where(left >= right, index, index + 1)
        owner = jnp.where(crossing, side, owner)
    info[...] = jnp.zeros_like(info)
    info[0:micro] = sentence.astype(F32)
    info[micro : 2 * micro] = owner.astype(F32)
    column[...] = info[...].T

    def piece_of(unit):
        odd = lax.rem(unit, 2)
        return either(odd, 1 - odd)

    def begin_of(unit):
        return copy * (local - REACH) + piece_of(unit) * shift

    def pick(unit, first, size, kind):
        spots = pl.ds(pl.multiple_of(begin_of(unit) + first, 16), size)
        both = column[spots, kind * micro : (kind + 1) * micro]
        return jnp.where(unit < 2, both[:, 0:1], both[:, 1:2])

    def owned(unit, first, size):
        return pick(unit, first, size, 1) == (2 * copy + piece_of(unit)).astype(F32)

    load(0).wait()
    weights[0].wait()

    def unit_rows(unit):
        return pl.ds(pl.multiple_of(unit * rows, 16), rows)

    def x_copy(unit):
        span = unit_rows(unit)
        return pltpu.make_async_remote_copy(
            src_ref=ob.at[0, span], dst_ref=xb.at[1, span], send_sem=x_send.at[unit],
            recv_sem=x_recv.at[unit], device_id=across, device_id_type=MESH,
        )

    def forward(unit, slot):
        span = unit_rows(unit)
        start = pl.multiple_of(unit * rows, 16)
        hidden = xb[section, span]
        scaled_qkv = mul(hidden, w_qkv[...])
        lane = lax.broadcasted_iota(jnp.int32, scaled_qkv.shape, 1)
        mixed[span] = jnp.where(lane < width, scaled_qkv * 0.125, scaled_qkv).astype(BF16)
        for index, (first, size, begin) in enumerate(blocks):
            turned = pltpu.roll(info[0:8], length - begin_of(unit) - begin, 1)[0:micro, 0:WINDOW]
            near_ids = jnp.where(unit < 2, turned[0:1], turned[1:2])
            inside = lax.broadcasted_iota(jnp.int32, near_ids.shape, 1) < rows - begin
            near_ids = jnp.where(inside, near_ids, -1.0)
            allowed = pick(unit, first, size, 0) == near_ids
            bias[first : first + size] = jnp.where(allowed, 0.0, NEG)

        def pair_step(pair, _):
            lanes = pl.multiple_of(pair * 128, 128)
            for first, size, begin in blocks:
                near = pl.ds(pl.multiple_of(start + begin, 16), WINDOW)
                own = pl.ds(pl.multiple_of(start + first, 16), size)
                query = jnp.concatenate(halves(mixed[own, pl.ds(lanes, 128)]), axis=0)
                key = mixed[near, pl.ds(pl.multiple_of(width + pair * 128, 128), 128)]
                value = mixed[near, pl.ds(pl.multiple_of(2 * width + pair * 128, 128), 128)]
                barred = bias[first : first + size]
                scores = against(query, key) + jnp.concatenate([barred, barred], axis=0)
                share = jnp.exp(scores - jnp.max(scores, axis=-1, keepdims=True)).astype(BF16)
                for head in range(2):
                    cols = pl.ds(pl.multiple_of(pair * 512 + head * 256, 256), 256)
                    probs[own, cols] = share[head * size : (head + 1) * size]
                sums = mul(share, jnp.concatenate([value, jnp.ones((WINDOW, 128), BF16)], axis=1))
                lane = lax.broadcasted_iota(jnp.int32, (size, 128), 1)
                inverse = 1.0 / jnp.where(lane < 64, sums[:size, 128:], sums[size:, 128:])
                attended = jnp.where(lane < 64, sums[:size, :128], sums[size:, :128])
                att[own, pl.ds(lanes, 128)] = (attended * inverse).astype(BF16)
                scale[own, pl.ds(lanes, 128)] = inverse
            return 0

        lax.fori_loop(0, width // 128, pair_step, 0, unroll=True)
        @pl.when(slot == 0)
        def _():
            for weight in weights[1:]:
                weight.wait()
            for odd in range(1, units):
                load(odd).wait()
            pl.semaphore_wait(barrier, 5)
            for group in range(micro):
                halo(group).start()

        scaled, inverse = normalize(xb[section, span].astype(F32) + mul(att[span], w_out[...]))
        one[span] = scaled
        inv_one[span] = inverse
        normed = scaled * gains[0:1] + shifts[0:1]
        hold[...] = normed
        low = normed.astype(BF16)
        nlow[span] = low
        tile = 512
        count = inner_width // tile
        inner = mul(nlow[span], w_in[:, 0:tile])
        outer = hold[...]
        for step in range(count):
            ahead_inner = None
            if step + 1 < count:
                ahead_inner = mul(nlow[span], w_in[:, (step + 1) * tile : (step + 2) * tile])
            cols = pl.ds(step * tile, tile)
            active, slope = gelu(inner)
            act[span, cols] = active
            dg[span, cols] = slope
            outer = outer + mul(active, w_outer[cols])
            inner = ahead_inner
        scaled, inverse = normalize(outer)
        two[span] = scaled
        inv_two[span] = inverse
        ob[section, span] = (scaled * gains[1:2] + shifts[1:2]).astype(BF16)

    def backward_norm(unit):
        span = unit_rows(unit)
        upstream = jnp.where(owned(unit, 0, rows), xb[1 - section, span].astype(F32), 0.0)
        scaled = two[span]
        vec[1:2] += jnp.sum(upstream * scaled, axis=0, keepdims=True)
        vec[3:4] += jnp.sum(upstream, axis=0, keepdims=True)
        grad_two = normalize_back(upstream, scaled, inv_two[span], gains[1:2])
        hold[...] = grad_two
        goi[span] = grad_two.astype(BF16)

    def backward_feed(unit):
        span = unit_rows(unit)
        tile = 512
        count = inner_width // tile
        grad_active = against(goi[span], w_outer[0:tile])
        total = hold[...]
        for step in range(count):
            next_active = None
            if step + 1 < count:
                next_active = against(goi[span], w_outer[(step + 1) * tile : (step + 2) * tile])
            cols = pl.ds(step * tile, tile)
            grad_inner = (grad_active * dg[span, cols].astype(F32)).astype(BF16)
            dg[span, cols] = grad_inner
            total = total + against(grad_inner, w_in[:, step * tile : (step + 1) * tile])
            grad_active = next_active
        hold[...] = total

    def backward_rest(unit):
        span = unit_rows(unit)
        start = pl.multiple_of(unit * rows, 16)
        total = hold[...]
        scaled = one[span]
        vec[0:1] += jnp.sum(total * scaled, axis=0, keepdims=True)
        vec[2:3] += jnp.sum(total, axis=0, keepdims=True)
        grad_one = normalize_back(total, scaled, inv_one[span], gains[0:1])
        hold[...] = grad_one
        low = grad_one.astype(BF16)
        gai[span] = low
        gatt[...] = (against(low, w_out[...]) * scale[span]).astype(BF16)

        def pair_step(pair, _):
            lanes = pl.multiple_of(pair * 128, 128)
            key_lanes = pl.ds(pl.multiple_of(width + pair * 128, 128), 128)
            value_lanes = pl.ds(pl.multiple_of(2 * width + pair * 128, 128), 128)
            dkv[...] = jnp.zeros_like(dkv)
            for first, size, begin in blocks:
                near = pl.ds(pl.multiple_of(start + begin, 16), WINDOW)
                own = pl.ds(pl.multiple_of(start + first, 16), size)
                query = jnp.concatenate(halves(mixed[own, pl.ds(lanes, 128)]), axis=0)
                key = mixed[near, key_lanes]
                value = mixed[near, value_lanes]
                grad_pair = gatt[first : first + size, pl.ds(lanes, 128)]
                paired = (grad_pair.astype(F32) * att[own, pl.ds(lanes, 128)].astype(F32)).astype(BF16)
                grad = jnp.concatenate(halves(grad_pair), axis=0)
                left = jnp.concatenate([grad, jnp.concatenate(halves(paired), axis=0)], axis=1)
                share = jnp.concatenate(
                    [probs[own, pl.ds(pl.multiple_of(pair * 512 + head * 256, 256), 256)] for head in range(2)],
                    axis=0,
                )
                tilt = against(left, jnp.concatenate([value, jnp.full((WINDOW, 128), -1.0, BF16)], axis=1))
                grads = (share.astype(F32) * tilt).astype(BF16)
                wide = mul(grads, key)
                lane = lax.broadcasted_iota(jnp.int32, (size, 128), 1)
                grad_query = jnp.where(lane < 64, wide[:size], wide[size:])
                gmix[own, pl.ds(lanes, 128)] = (grad_query * 0.125).astype(BF16)
                for kind, (small, sides) in enumerate(((mixed[own, pl.ds(lanes, 128)], grads), (grad_pair, share))):
                    turned = small.T
                    for head in range(2):
                        heads = slice(head * 64, (head + 1) * 64)
                        dkv[kind, heads, begin : begin + WINDOW] += mul(
                            turned[heads], sides[head * size : (head + 1) * size]
                        )
            gmix[span, key_lanes] = dkv[0].astype(BF16).T[0:rows]
            gmix[span, value_lanes] = dkv[1].astype(BF16).T[0:rows]
            return 0

        lax.fori_loop(0, width // 128, pair_step, 0, unroll=True)
        ob[1 - section, span] = (hold[...] + against(gmix[span], w_qkv[...])).astype(BF16)

    def backward(unit):
        backward_norm(unit)
        backward_feed(unit)
        backward_rest(unit)

    def slot_step(slot, _):
        is_forward = jnp.where(section == 0, slot < units, lax.rem(slot, 2) == 0)
        unit = jnp.where(section == 0, lax.rem(slot, units), lax.div(slot, 2))

        first_use = jnp.where(section == 0, is_forward, jnp.logical_not(is_forward))

        @pl.when(jnp.logical_and(first_use, lax.rem(unit, 2) == 1))
        def _():
            halo(lax.div(unit, 2)).wait_recv()

        @pl.when(is_forward)
        def _():
            @pl.when(section == 1)
            def _():
                x_copy(unit).wait_recv()

            forward(unit, slot)

            @pl.when(section == 0)
            def _():
                x_copy(unit).start()

        held = jnp.logical_and(section == 0, slot == 2 * units - 1)

        @pl.when(jnp.logical_not(jnp.logical_or(is_forward, held)))
        def _():
            @pl.when(section == 0)
            def _():
                x_copy(unit).wait_recv()

            backward(unit)

            @pl.when(section == 1)
            def _():
                x_copy(unit).start()

        return 0

    lax.fori_loop(0, 2 * units, slot_step, 0)

    def strip_copy(group):
        source = (2 * group + 1) * rows + either(rows - REACH, 0)
        return pltpu.make_async_remote_copy(
            src_ref=ob.at[1, pl.ds(pl.multiple_of(source, 16), REACH)], dst_ref=strip.at[group],
            send_sem=y_send.at[micro + group], recv_sem=y_recv.at[micro + group],
            device_id=beside, device_id_type=MESH,
        )

    def outputs(group, side):
        even, odd = 2 * group * rows, (2 * group + 1) * rows
        if side == 0:
            parts = ((even, 0, shift), (odd, shift, local - shift))
        else:
            parts = ((odd + REACH, 0, shift - REACH), (even, shift - REACH, rows))
        return [
            pltpu.make_async_copy(
                ob.at[1, pl.ds(source, size)], result.at[0, group, 0, pl.ds(target, size)],
                out_sem.at[group, index],
            )
            for index, (source, target, size) in enumerate(parts)
        ]

    def finish():
        for group in range(micro):
            low_unit, high_unit = 2 * group + copy, 2 * group + 1 - copy
            over = rows - shift
            kept = pl.ds(pl.multiple_of(low_unit * rows + shift, 16), over)
            moved = pl.ds(pl.multiple_of(high_unit * rows, 16), over)
            ob[1, moved] = jnp.where(owned(low_unit, shift, over), ob[1, kept], ob[1, moved])
            strip_copy(group).wait_recv()
            odd_unit = 2 * group + 1
            first = either(shift, REACH)
            edge = pl.ds(pl.multiple_of(odd_unit * rows + first, 16), REACH)
            ob[1, edge] = jnp.where(owned(odd_unit, first, REACH), ob[1, edge], strip[group])
        for side in range(2):
            @pl.when(copy == side)
            def _():
                for group in range(micro):
                    for part in outputs(group, side):
                        part.start()

    half = 1024
    seg = half // chips

    def spare(group, way, index):
        tile = way * 2 + index
        if group == 2:
            return mixed.at[pl.ds(0, 512), pl.ds(tile * 256, 256)]
        return probs.at[pl.ds(0, 512), pl.ds((group * 4 + tile) * 256, 256)]

    def sib_copy(group, way, index):
        return pltpu.make_async_remote_copy(
            src_ref=spare(group, way, index), dst_ref=sib.at[group, way, pl.ds(index * 512, 512)],
            send_sem=sib_send.at[group, way, index], recv_sem=sib_recv.at[group, way, index],
            device_id=sibling, device_id_type=MESH,
        )

    def block_of(group, block, span):
        cols = pl.ds(pl.multiple_of(block * 512, 512), 512)
        if group == 0:
            return contract(act[span, cols], goi[span])
        if group == 1:
            return contract(nlow[span], dg[span, cols])
        cols = pl.ds(pl.multiple_of(jnp.maximum(block - 1, 0) * 512, 512), 512)
        left = jnp.where(block == 0, att[span], xb[section, span])
        return contract(left, jnp.where(block == 0, gai[span], gmix[span, cols]))

    early, late = pl.ds(0, (units - 1) * rows), pl.ds((units - 1) * rows, rows)

    def prepare(group):
        for index in range(2):
            value = block_of(group, (1 - core) * 2 + index, early).astype(BF16)
            for way in range(2):
                spare(group, way, index)[...] = value[:, way * 256 : (way + 1) * 256]
        for index in range(2):
            value = block_of(group, core * 2 + index, early).astype(BF16)
            for way in range(2):
                mine[group, way, index * 512 : (index + 1) * 512] = value[:, way * 256 : (way + 1) * 256]

    def others(group):
        for index in range(2):
            value = block_of(group, (1 - core) * 2 + index, late)
            for way in range(2):
                part = value[:, way * 256 : (way + 1) * 256]
                room = spare(group, way, index)
                room[...] = (room[...].astype(F32) + part).astype(BF16)
                sib_copy(group, way, index).start()

    def ours(group):
        for index in range(2):
            value = block_of(group, core * 2 + index, late)
            for way in range(2):
                sib_copy(group, way, index).wait_recv()
                part = value[:, way * 256 : (way + 1) * 256]
                span = slice(index * 512, (index + 1) * 512)
                total = mine[group, way, span].astype(F32) + part + sib[group, way, span].astype(F32)
                mine[group, way, span] = total.astype(BF16)

    def segment(position):
        return pl.ds(pl.multiple_of(around(position) * seg, 16), seg)

    def target(way):
        return tuple(jnp.where(way == 0, a, b) for a, b in zip(ahead, behind))

    def rs_copy(group, way, step, source):
        return pltpu.make_async_remote_copy(
            src_ref=source, dst_ref=rsb.at[group, way, step], send_sem=rs_send.at[group, way, step],
            recv_sem=rs_recv.at[group, way, step], device_id=target(way), device_id_type=MESH,
        )

    def final_rows(position):
        return pl.ds(pl.multiple_of(core * half + around(position) * seg, 16), seg)

    def ag_copy(group, way, step, source, position):
        return pltpu.make_async_remote_copy(
            src_ref=source, dst_ref=summed.at[group, way, final_rows(position)],
            send_sem=ag_send.at[group, way, step], recv_sem=ag_recv.at[group, way, step],
            device_id=target(way), device_id_type=MESH,
        )

    def pass_copy(group, way, source, position):
        return pltpu.make_async_remote_copy(
            src_ref=source, dst_ref=summed.at[group, way, final_rows(position)],
            send_sem=pass_send.at[group, way], recv_sem=pass_recv.at[group, way],
            device_id=sibling, device_id_type=MESH,
        )

    def own_copy(group, way):
        sign = 1 - 2 * way
        return pltpu.make_async_copy(
            rsb.at[group, way, chips - 2], summed.at[group, way, final_rows(place + sign)],
            own_sem.at[group, way],
        )

    def ring(group, way, step):
        sign = 1 - 2 * way

        @pl.when(step == 0)
        def _():
            rs_copy(group, way, 0, mine.at[group, way, segment(place)]).start()

        @pl.when(jnp.logical_and(step >= 1, step < chips))
        def _():
            last = step - 1
            slot = rsb.at[group, way, last]
            rs_copy(group, way, last, slot).wait_recv()
            part = mine[group, way, segment(place - sign * step)]
            rsb[group, way, last] = (rsb[group, way, last].astype(F32) + part.astype(F32)).astype(BF16)

            @pl.when(step < chips - 1)
            def _():
                rs_copy(group, way, step, slot).start()

            @pl.when(step == chips - 1)
            def _():
                ag_copy(group, way, 0, slot, place + sign).start()
                pass_copy(group, way, slot, place + sign).start()
                own_copy(group, way).start()

        @pl.when(jnp.logical_and(step >= chips, step < 2 * chips - 1))
        def _():
            last = step - chips
            position = place - sign * last
            arrived = summed.at[group, way, final_rows(position)]
            ag_copy(group, way, last, arrived, position).wait_recv()

            @pl.when(last + 1 < chips - 1)
            def _():
                ag_copy(group, way, last + 1, arrived, position).start()

            pass_copy(group, way, arrived, position).start()

    def slot_copy(step):
        return pltpu.make_async_remote_copy(
            src_ref=slots.at[step], dst_ref=slots.at[step + 1], send_sem=slot_send.at[step],
            recv_sem=slot_recv.at[step], device_id=ahead, device_id_type=MESH,
        )

    vec_copy = pltpu.make_async_remote_copy(
        src_ref=vec.at[pl.ds(0, 8)], dst_ref=vec.at[pl.ds(8, 8)], send_sem=slot_send.at[chips],
        recv_sem=slot_recv.at[chips], device_id=sibling, device_id_type=MESH,
    )
    def serve(group, step):
        def each(way, _):
            ring(group, way, step)
            return 0

        lax.fori_loop(0, 2, each, 0)

    last = units - 1
    for group in range(GROUPS):
        prepare(group)

    @pl.when(section == 0)
    def _():
        x_copy(last).wait_recv()
        backward_norm(last)

    others(0)

    @pl.when(section == 0)
    def _():
        backward_feed(last)

    others(1)
    ours(0)
    serve(0, 0)

    @pl.when(section == 0)
    def _():
        backward_rest(last)

    for group in range(micro):
        strip_copy(group).start()
    vec_copy.start()
    others(2)
    ours(1)
    serve(1, 0)
    ours(2)
    serve(2, 0)
    finish()
    vec_copy.wait()
    slots[0] = vec[0:8] + vec[8:16]

    def round_step(index, _):
        def each(flat, _):
            group, way = lax.div(flat, 2), lax.rem(flat, 2)
            ring(group, way, index)
            return 0

        lax.fori_loop(0, 2 * GROUPS, each, 0)

        @pl.when(index < chips)
        def _():
            @pl.when(index > 1)
            def _():
                slot_copy(index - 2).wait_recv()

            slot_copy(index - 1).start()

        return 0

    lax.fori_loop(1, 2 * chips - 1, round_step, 0)
    slot_copy(chips - 2).wait_recv()
    total = jnp.zeros((8, width), F32)
    for position in range(chips):
        total = total + slots[around(place - position)]
    vectors[...] = total

    def drain(flat, _):
        group, way = lax.div(flat, 2), lax.rem(flat, 2)
        own_copy(group, way).wait()

        def each(step, _):
            rs_copy(group, way, step, rsb.at[group, way, 0]).wait_send()
            ag_copy(group, way, step, rsb.at[group, way, 0], place).wait_send()
            return 0

        lax.fori_loop(0, chips - 1, each, 0)
        whole = pltpu.make_async_remote_copy(
            src_ref=summed.at[group, way, pl.ds(0, half)], dst_ref=summed.at[group, way, pl.ds(0, half)],
            send_sem=pass_send.at[group, way], recv_sem=pass_recv.at[group, way],
            device_id=sibling, device_id_type=MESH,
        )
        whole.wait_send()
        whole.wait_recv()
        return 0

    lax.fori_loop(0, 2 * GROUPS, drain, 0)
    for group in range(GROUPS):
        for way in range(2):
            for index in range(2):
                sib_copy(group, way, index).wait_send()

    def drain_slots(step, _):
        slot_copy(step).wait_send()
        return 0

    lax.fori_loop(0, chips - 1, drain_slots, 0)

    def drain_units(unit, _):
        x_copy(unit).wait_send()
        return 0

    lax.fori_loop(0, units, drain_units, 0)
    for group in range(micro):
        halo(group).wait_send()
        strip_copy(group).wait_send()
    for side in range(2):
        @pl.when(copy == side)
        def _():
            for group in range(micro):
                for part in outputs(group, side):
                    part.wait()


def widen(summed, vectors, qkv, out, inner, outer, gain, shift, narrow, wide, in_sem, out_sem):
    homes = [outer.at[0, pl.ds(index * 512, 512)] for index in range(4)]
    homes += [inner.at[0, :, pl.ds(index * 512, 512)] for index in range(4)]
    homes += [out.at[0]] + [qkv.at[0, :, pl.ds(index * 512, 512)] for index in range(3)]
    loads = [
        pltpu.make_async_copy(
            summed.at[index // 4, :, pl.ds(index % 4 * 512, 512)], narrow.at[index], in_sem.at[index]
        )
        for index in range(len(homes))
    ]
    stores = [
        pltpu.make_async_copy(wide.at[index], home, out_sem.at[index]) for index, home in enumerate(homes)
    ]
    for load in loads:
        load.start()
    gain[0] = vectors[0:2]
    shift[0] = vectors[2:4]
    for index, (load, store) in enumerate(zip(loads, stores)):
        load.wait()
        for way in range(2):
            wide[index, :, way * 256 : (way + 1) * 256] = narrow[index, way].astype(F32)
        store.start()
    for store in stores:
        store.wait()


def per_device(mesh, boundary, sentence_ids, qkv_weight, out_weight, inner_weight, outer_weight, norm_gain, norm_bias):
    micro, local, width = boundary.shape[1], boundary.shape[3], boundary.shape[4]
    inner_width = inner_weight.shape[2]
    length = sentence_ids.shape[2]
    chips = mesh.shape["copy"] * mesh.shape["dp"] // 2
    rows = (local + REACH) // 2 + REACH
    units = micro * 2
    tokens = units * rows
    any_space = pl.BlockSpec(memory_space=pl.ANY)
    vmem = pl.BlockSpec(memory_space=pltpu.VMEM)
    dma = pltpu.SemaphoreType.DMA
    hops = chips - 1
    result, summed, vectors = pl.pallas_call(
        functools.partial(kernel, units, rows, chips, width, inner_width),
        out_shape=(
            jax.ShapeDtypeStruct(boundary.shape, BF16),
            jax.ShapeDtypeStruct((GROUPS, 2, 2048, 256), BF16),
            jax.ShapeDtypeStruct((8, width), F32),
        ),
        in_specs=[any_space, vmem] + [any_space] * 4 + [vmem] * 2,
        out_specs=(any_space, any_space, vmem),
        scratch_shapes=[
            pltpu.VMEM((width, 3 * width), BF16),
            pltpu.VMEM((width, width), BF16),
            pltpu.VMEM((width, inner_width), BF16),
            pltpu.VMEM((inner_width, width), BF16),
            pltpu.VMEM((128, length), F32),
            pltpu.VMEM((length, 128), F32),
            pltpu.VMEM((2, tokens, width), BF16),
            pltpu.VMEM((2, tokens, width), BF16),
            pltpu.VMEM((tokens + 80, 3 * width), BF16),
            pltpu.VMEM((tokens, width), BF16),
            pltpu.VMEM((tokens, width), BF16),
            pltpu.VMEM((tokens, inner_width), BF16),
            pltpu.VMEM((tokens, inner_width), BF16),
            pltpu.VMEM((tokens, width), F32),
            pltpu.VMEM((tokens, width), F32),
            pltpu.VMEM((tokens, 1), F32),
            pltpu.VMEM((tokens, 1), F32),
            pltpu.VMEM((tokens, width), BF16),
            pltpu.VMEM((tokens, width), BF16),
            pltpu.VMEM((tokens, 3 * width), BF16),
            pltpu.VMEM((tokens, HEADS * WINDOW), BF16),
            pltpu.VMEM((tokens, width), F32),
            pltpu.VMEM((rows, WINDOW), F32),
            pltpu.VMEM((rows, width), BF16),
            pltpu.VMEM((rows, width), F32),
            pltpu.VMEM((2, 128, 384), F32),
            pltpu.VMEM((micro, REACH, width), BF16),
            pltpu.VMEM((GROUPS, 2, 1024, 256), BF16),
            pltpu.VMEM((GROUPS, 2, 1024, 256), BF16),
            pltpu.VMEM((GROUPS, 2, hops, 1024 // chips, 256), BF16),
            pltpu.VMEM((16, width), F32),
            pltpu.VMEM((chips, 8, width), F32),
            dma((4,)), dma((units,)), dma((micro, 2)), dma((units,)), dma((units,)),
            dma((2 * micro,)), dma((2 * micro,)), dma((GROUPS, 2, 2)), dma((GROUPS, 2, 2)),
            dma((GROUPS, 2, hops)), dma((GROUPS, 2, hops)), dma((GROUPS, 2, hops)), dma((GROUPS, 2, hops)),
            dma((chips + 1,)), dma((chips + 1,)), dma((GROUPS, 2)), dma((GROUPS, 2)), dma((GROUPS, 2)),
        ],
        compiler_params=pltpu.CompilerParams(
            collective_id=0, has_side_effects=True, vmem_limit_bytes=63 * 1024 * 1024
        ),
    )(boundary, sentence_ids, qkv_weight, out_weight, inner_weight, outer_weight, norm_gain, norm_bias)

    blocks = 4 * GROUPS
    grad_qkv, grad_out, grad_inner, grad_outer, grad_gain, grad_bias = pl.pallas_call(
        widen,
        out_shape=tuple(
            jax.ShapeDtypeStruct(item.shape, F32)
            for item in (qkv_weight, out_weight, inner_weight, outer_weight, norm_gain, norm_bias)
        ),
        in_specs=[any_space, vmem],
        out_specs=(any_space,) * 4 + (vmem,) * 2,
        scratch_shapes=[
            pltpu.VMEM((blocks, 2, 512, 256), BF16), pltpu.VMEM((blocks, 512, 512), F32),
            dma((blocks,)), dma((blocks,)),
        ],
        compiler_params=pltpu.CompilerParams(vmem_limit_bytes=48 * 1024 * 1024),
    )(summed, vectors)
    return (result, grad_qkv, grad_out, grad_inner, grad_outer, grad_gain, grad_bias)


def solution(mesh):
    weight = P("section", None, None)
    edge = P("section", None, "dp", "copy", None)
    return jax.shard_map(
        functools.partial(per_device, mesh),
        mesh=mesh,
        in_specs=(edge, P(None, "dp", None)) + (weight,) * 6,
        out_specs=(edge,) + (weight,) * 6,
        check_vma=False,
    )
```

```python
import functools

import jax
import jax.numpy as jnp
from jax import lax
from jax.experimental import pallas as pl
from jax.experimental.pallas import tpu as pltpu
from jax.sharding import PartitionSpec as P

HEADS = 8
REACH = 32
WINDOW = 256
NEG = -1e30
EPS = 1e-05
GROUPS = 3
BLOCKS = ((0, 192, 0), (192, 112, 128))
MESH = pl.DeviceIdType.MESH
F32 = jnp.float32
BF16 = jnp.bfloat16


def mul(left, right):
    return jnp.dot(left, right, preferred_element_type=F32)


def against(left, right):
    return lax.dot_general(left, right, (((1,), (1,)), ((), ())), preferred_element_type=F32)


def contract(left, right):
    return lax.dot_general(left, right, (((0,), (0,)), ((), ())), preferred_element_type=F32)


def gelu(x):
    phi = 0.5 + 0.5 * lax.erf(x * 0.7071067811865476)
    bell = jnp.exp(x * x * -0.5) * 0.3989422804014327
    return (x * phi).astype(BF16), (phi + x * bell).astype(BF16)


def normalize(resid):
    center = resid - jnp.mean(resid, axis=-1, keepdims=True)
    spread = jnp.mean(center * center, axis=-1, keepdims=True)
    inverse = lax.rsqrt(spread + EPS)
    return center * inverse, inverse


def normalize_back(upstream, scaled, inverse, gain):
    tilted = upstream * gain
    first = jnp.mean(tilted, axis=-1, keepdims=True)
    second = jnp.mean(tilted * scaled, axis=-1, keepdims=True)
    return inverse * (tilted - first - scaled * second)


def halves(pair):
    lane = lax.broadcasted_iota(jnp.int32, pair.shape, 1)
    zero = jnp.zeros_like(pair)
    return jnp.where(lane < 64, pair, zero), jnp.where(lane < 64, zero, pair)


def kernel(
    units, rows, chips, width, inner_width,
    boundary, ids, qkv_weight, out_weight, inner_weight, outer_weight, gain_rows, shift_rows,
    result, summed, vectors,
    w_qkv, w_out, w_in, w_outer, info, column,
    xb, ob, mixed, att, nlow, act, dg, one, two, inv, goi, gai, gmix, probs, scale,
    bias, gatt, hold, dkv, strip, mine, sib, rsb, vec, slots,
    peer_act, peer_nlow, peer_att, peer_in, peer_goi, peer_dg, peer_gai, peer_gmix,
    weight_sem, in_sem, out_sem, x_send, x_recv, y_send, y_recv, sib_send, sib_recv, rs_send, rs_recv,
    ag_send, ag_recv, slot_send, slot_recv, pass_send, pass_recv, own_sem, peer_send, peer_recv,
):
    blocks = BLOCKS
    micro, local = boundary.shape[1], boundary.shape[3]
    length = ids.shape[2]
    reach = local + REACH
    shift = reach - rows
    section, copy, dp = lax.axis_index("section"), lax.axis_index("copy"), lax.axis_index("dp")
    core, layer = lax.rem(dp, 2), lax.div(dp, 2)
    line = chips // 2
    place = jnp.where(copy == 0, layer, chips - 1 - layer)
    gains, shifts = gain_rows.at[0], shift_rows.at[0]

    def either(first, second):
        return jnp.where(copy == 0, first, second)

    def at(position):
        far = position >= line
        return (section, jnp.where(far, 1, 0), 2 * jnp.where(far, chips - 1 - position, position) + core)

    def around(position):
        return lax.rem(position + 2 * chips, chips)

    across = (1 - section, copy, dp)
    beside = (section, 1 - copy, dp)
    sibling = (section, copy, dp + 1 - 2 * core)
    ahead, behind = at(around(place + 1)), at(around(place - 1))

    def load(unit):
        group, odd = unit // 2, unit % 2
        if odd:
            source, target, size = either(shift, 0), either(0, REACH), rows - REACH
        else:
            source, target, size = either(0, local - rows), 0, rows
        return pltpu.make_async_copy(
            boundary.at[0, group, 0, pl.ds(pl.multiple_of(source, 16), size)],
            xb.at[0, pl.ds(pl.multiple_of(unit * rows + target, 16), size)], in_sem.at[unit],
        )

    def halo(group):
        source, target = either(local - REACH, 0), (2 * group + 1) * rows + either(0, rows - REACH)
        return pltpu.make_async_remote_copy(
            src_ref=boundary.at[0, group, 0, pl.ds(pl.multiple_of(source, 16), REACH)],
            dst_ref=xb.at[0, pl.ds(pl.multiple_of(target, 16), REACH)],
            send_sem=y_send.at[group], recv_sem=y_recv.at[group],
            device_id=beside, device_id_type=MESH,
        )

    weights = [
        pltpu.make_async_copy(source.at[0], target, weight_sem.at[index])
        for index, (source, target) in enumerate(
            ((qkv_weight, w_qkv), (out_weight, w_out), (inner_weight, w_in), (outer_weight, w_outer))
        )
    ]
    vec[...] = jnp.zeros_like(vec)
    for unit in range(units):
        mixed[(unit + 1) * rows : (unit + 1) * rows + 80] = jnp.zeros((80, 3 * width), BF16)
    barrier = pltpu.get_barrier_semaphore()
    for other in (across, beside, sibling, ahead, behind):
        pl.semaphore_signal(barrier, inc=1, device_id=other, device_id_type=MESH)
    load(0).start()
    weights[0].start()
    for unit in range(1, units):
        load(unit).start()
    for weight in weights[1:]:
        weight.start()

    spot = lax.broadcasted_iota(jnp.int32, (micro, length), 1)
    sentence = ids[:, 0, :]
    cuts = (reach // 2, local, length - reach // 2)
    owner = jnp.zeros((micro, length), jnp.int32)
    for cut in cuts:
        owner = owner + jnp.where(spot >= cut, 1, 0)
    for index, cut in enumerate(cuts):
        crossing = sentence == sentence[:, cut - 1 : cut]
        left = jnp.sum(jnp.where(crossing & (spot < cut), 1.0, 0.0), axis=1, keepdims=True)
        right = jnp.sum(jnp.where(crossing & (spot >= cut), 1.0, 0.0), axis=1, keepdims=True)
        side = jnp.where(left >= right, index, index + 1)
        owner = jnp.where(crossing, side, owner)
    info[...] = jnp.zeros_like(info)
    info[0:micro] = sentence.astype(F32)
    info[micro : 2 * micro] = owner.astype(F32)
    column[...] = info[...].T

    def piece_of(unit):
        odd = lax.rem(unit, 2)
        return either(odd, 1 - odd)

    def begin_of(unit):
        return copy * (local - REACH) + piece_of(unit) * shift

    def pick(unit, first, size, kind):
        spots = pl.ds(pl.multiple_of(begin_of(unit) + first, 16), size)
        both = column[spots, kind * micro : (kind + 1) * micro]
        return jnp.where(unit < 2, both[:, 0:1], both[:, 1:2])

    def owned(unit, first, size):
        return pick(unit, first, size, 1) == (2 * copy + piece_of(unit)).astype(F32)

    load(0).wait()
    weights[0].wait()

    def unit_rows(unit):
        return pl.ds(pl.multiple_of(unit * rows, 16), rows)

    def x_copy(unit):
        span = unit_rows(unit)
        return pltpu.make_async_remote_copy(
            src_ref=ob.at[0, span], dst_ref=xb.at[1, span], send_sem=x_send.at[unit],
            recv_sem=x_recv.at[unit], device_id=across, device_id_type=MESH,
        )

    def forward(unit, slot):
        span = unit_rows(unit)
        start = pl.multiple_of(unit * rows, 16)
        hidden = xb[section, span]
        scaled_qkv = mul(hidden, w_qkv[...])
        lane = lax.broadcasted_iota(jnp.int32, scaled_qkv.shape, 1)
        mixed[span] = jnp.where(lane < width, scaled_qkv * 0.125, scaled_qkv).astype(BF16)
        for index, (first, size, begin) in enumerate(blocks):
            turned = pltpu.roll(info[...], length - begin_of(unit) - begin, 1)[0:micro, 0:WINDOW]
            near_ids = jnp.where(unit < 2, turned[0:1], turned[1:2])
            inside = lax.broadcasted_iota(jnp.int32, near_ids.shape, 1) < rows - begin
            near_ids = jnp.where(inside, near_ids, -1.0)
            allowed = pick(unit, first, size, 0) == near_ids
            bias[first : first + size] = jnp.where(allowed, 0.0, NEG)

        def pair_step(pair, _):
            lanes = pl.multiple_of(pair * 128, 128)
            for first, size, begin in blocks:
                near = pl.ds(pl.multiple_of(start + begin, 16), WINDOW)
                own = pl.ds(pl.multiple_of(start + first, 16), size)
                query = jnp.concatenate(halves(mixed[own, pl.ds(lanes, 128)]), axis=0)
                key = mixed[near, pl.ds(pl.multiple_of(width + pair * 128, 128), 128)]
                value = mixed[near, pl.ds(pl.multiple_of(2 * width + pair * 128, 128), 128)]
                barred = bias[first : first + size]
                scores = against(query, key) + jnp.concatenate([barred, barred], axis=0)
                share = jnp.exp(scores - jnp.max(scores, axis=-1, keepdims=True)).astype(BF16)
                for head in range(2):
                    cols = pl.ds(pl.multiple_of(pair * 512 + head * 256, 256), 256)
                    probs[own, cols] = share[head * size : (head + 1) * size]
                sums = mul(share, jnp.concatenate([value, jnp.ones((WINDOW, 128), BF16)], axis=1))
                lane = lax.broadcasted_iota(jnp.int32, (size, 128), 1)
                inverse = 1.0 / jnp.where(lane < 64, sums[:size, 128:], sums[size:, 128:])
                attended = jnp.where(lane < 64, sums[:size, :128], sums[size:, :128])
                att[own, pl.ds(lanes, 128)] = (attended * inverse).astype(BF16)
                scale[own, pl.ds(lanes, 128)] = inverse
            return 0

        lax.fori_loop(0, width // 128, pair_step, 0, unroll=True)
        @pl.when(slot == 0)
        def _():
            for weight in weights[1:]:
                weight.wait()
            for odd in range(1, units):
                load(odd).wait()
            pl.semaphore_wait(barrier, 5)
            for group in range(micro):
                halo(group).start()

        scaled, inverse = normalize(xb[section, span].astype(F32) + mul(att[span], w_out[...]))
        one[span] = scaled
        inv[span, 0:1] = inverse
        normed = scaled * gains[0:1] + shifts[0:1]
        hold[...] = normed
        low = normed.astype(BF16)
        nlow[span] = low
        tile = 512
        count = inner_width // tile
        inner = mul(nlow[span], w_in[:, 0:tile])
        outer = hold[...]
        for step in range(count):
            ahead_inner = None
            if step + 1 < count:
                ahead_inner = mul(nlow[span], w_in[:, (step + 1) * tile : (step + 2) * tile])
            cols = pl.ds(step * tile, tile)
            active, slope = gelu(inner)
            act[span, cols] = active
            dg[span, cols] = slope
            outer = outer + mul(active, w_outer[cols])
            inner = ahead_inner
        scaled, inverse = normalize(outer)
        two[span] = scaled
        inv[span, 1:2] = inverse
        ob[section, span] = (scaled * gains[1:2] + shifts[1:2]).astype(BF16)

    def backward_norm(unit):
        span = unit_rows(unit)
        upstream = jnp.where(owned(unit, 0, rows), xb[1 - section, span].astype(F32), 0.0)
        scaled = two[span]
        vec[1:2] += jnp.sum(upstream * scaled, axis=0, keepdims=True)
        vec[3:4] += jnp.sum(upstream, axis=0, keepdims=True)
        grad_two = normalize_back(upstream, scaled, inv[span, 1:2], gains[1:2])
        hold[...] = grad_two
        goi[span] = grad_two.astype(BF16)

    def backward_feed(unit):
        span = unit_rows(unit)
        tile = 512
        count = inner_width // tile
        grad_active = against(goi[span], w_outer[0:tile])
        total = hold[...]
        for step in range(count):
            next_active = None
            if step + 1 < count:
                next_active = against(goi[span], w_outer[(step + 1) * tile : (step + 2) * tile])
            cols = pl.ds(step * tile, tile)
            grad_inner = (grad_active * dg[span, cols].astype(F32)).astype(BF16)
            dg[span, cols] = grad_inner
            total = total + against(grad_inner, w_in[:, step * tile : (step + 1) * tile])
            grad_active = next_active
        hold[...] = total

    def backward_rest(unit):
        span = unit_rows(unit)
        start = pl.multiple_of(unit * rows, 16)
        total = hold[...]
        scaled = one[span]
        vec[0:1] += jnp.sum(total * scaled, axis=0, keepdims=True)
        vec[2:3] += jnp.sum(total, axis=0, keepdims=True)
        grad_one = normalize_back(total, scaled, inv[span, 0:1], gains[0:1])
        hold[...] = grad_one
        low = grad_one.astype(BF16)
        gai[span] = low
        gatt[...] = (against(low, w_out[...]) * scale[span]).astype(BF16)

        def pair_step(pair, _):
            lanes = pl.multiple_of(pair * 128, 128)
            key_lanes = pl.ds(pl.multiple_of(width + pair * 128, 128), 128)
            value_lanes = pl.ds(pl.multiple_of(2 * width + pair * 128, 128), 128)
            dkv[...] = jnp.zeros_like(dkv)
            for first, size, begin in blocks:
                near = pl.ds(pl.multiple_of(start + begin, 16), WINDOW)
                own = pl.ds(pl.multiple_of(start + first, 16), size)
                query = jnp.concatenate(halves(mixed[own, pl.ds(lanes, 128)]), axis=0)
                key = mixed[near, key_lanes]
                value = mixed[near, value_lanes]
                grad_pair = gatt[first : first + size, pl.ds(lanes, 128)]
                paired = (grad_pair.astype(F32) * att[own, pl.ds(lanes, 128)].astype(F32)).astype(BF16)
                grad = jnp.concatenate(halves(grad_pair), axis=0)
                left = jnp.concatenate([grad, jnp.concatenate(halves(paired), axis=0)], axis=1)
                share = jnp.concatenate(
                    [probs[own, pl.ds(pl.multiple_of(pair * 512 + head * 256, 256), 256)] for head in range(2)],
                    axis=0,
                )
                tilt = against(left, jnp.concatenate([value, jnp.full((WINDOW, 128), -1.0, BF16)], axis=1))
                grads = (share.astype(F32) * tilt).astype(BF16)
                wide = mul(grads, key)
                lane = lax.broadcasted_iota(jnp.int32, (size, 128), 1)
                grad_query = jnp.where(lane < 64, wide[:size], wide[size:])
                gmix[own, pl.ds(lanes, 128)] = (grad_query * 0.125).astype(BF16)
                for kind, (small, sides) in enumerate(((mixed[own, pl.ds(lanes, 128)], grads), (grad_pair, share))):
                    turned = small.T
                    for head in range(2):
                        heads = slice(head * 64, (head + 1) * 64)
                        dkv[kind, heads, begin : begin + WINDOW] += mul(
                            turned[heads], sides[head * size : (head + 1) * size]
                        )
            gmix[span, key_lanes] = dkv[0].astype(BF16).T[0:rows]
            gmix[span, value_lanes] = dkv[1].astype(BF16).T[0:rows]
            return 0

        lax.fori_loop(0, width // 128, pair_step, 0, unroll=True)

    def backward_input(unit):
        span = unit_rows(unit)
        ob[1 - section, span] = (hold[...] + against(gmix[span], w_qkv[...])).astype(BF16)

    def backward(unit):
        backward_norm(unit)
        backward_feed(unit)
        backward_rest(unit)
        backward_input(unit)

    half = 1024
    seg = half // chips

    def spare(group, way, index):
        tile = way * 2 + index
        if group == 2:
            return mixed.at[pl.ds(0, 512), pl.ds(tile * 256, 256)]
        return probs.at[pl.ds(0, 512), pl.ds((group * 4 + tile) * 256, 256)]

    def sib_copy(group, way, index):
        return pltpu.make_async_remote_copy(
            src_ref=spare(group, way, index), dst_ref=sib.at[group, way, pl.ds(index * 512, 512)],
            send_sem=sib_send.at[group, way, index], recv_sem=sib_recv.at[group, way, index],
            device_id=sibling, device_id_type=MESH,
        )

    def block_of(group, block, span):
        cols = pl.ds(pl.multiple_of(block * 512, 512), 512)
        if group == 0:
            return contract(act[span, cols], goi[span])
        if group == 1:
            return contract(nlow[span], dg[span, cols])
        cols = pl.ds(pl.multiple_of(jnp.maximum(block - 1, 0) * 512, 512), 512)
        left = jnp.where(block == 0, att[span], xb[section, span])
        return contract(left, jnp.where(block == 0, gai[span], gmix[span, cols]))

    def both(own, peer):
        return jnp.concatenate([own, peer], axis=0)

    def last_block(group, index):
        span = pl.ds((units - 1) * rows, rows)
        block = core * 2 + index
        cols = pl.ds(pl.multiple_of(block * 512, 512), 512)
        here = slice(index * 512, (index + 1) * 512)
        if group == 0:
            return contract(both(act[span, cols], peer_act[:, here]), both(goi[span], peer_goi[...]))
        if group == 1:
            return contract(both(nlow[span], peer_nlow[...]), both(dg[span, cols], peer_dg[:, here]))
        cols = pl.ds(pl.multiple_of(jnp.maximum(block - 1, 0) * 512, 512), 512)
        first = block == 0
        peer_cols = pl.ds(pl.multiple_of(jnp.where(first, 0, (core + index - 1) * 512), 512), 512)
        left = jnp.where(first, both(att[span], peer_att[...]), both(xb[section, span], peer_in[...]))
        right = jnp.where(first, both(gai[span], peer_gai[...]), both(gmix[span, cols], peer_gmix[:, peer_cols]))
        return contract(left, right)

    def peer_copy(index):
        span = pl.ds((units - 1) * rows, rows)
        wide = pl.ds(pl.multiple_of((1 - core) * 1024, 512), 1024)
        near = pl.ds(pl.multiple_of((1 - core) * 512, 512), 1024)
        source, target = (
            (act.at[span, wide], peer_act), (nlow.at[span], peer_nlow), (att.at[span], peer_att),
            (xb.at[section, span], peer_in), (goi.at[span], peer_goi), (dg.at[span, wide], peer_dg),
            (gai.at[span], peer_gai), (gmix.at[span, near], peer_gmix),
        )[index]
        return pltpu.make_async_remote_copy(
            src_ref=source, dst_ref=target, send_sem=peer_send.at[index], recv_sem=peer_recv.at[index],
            device_id=sibling, device_id_type=MESH,
        )

    def put(room, part, first):
        room[...] = (part if first else part + room[...].astype(F32)).astype(BF16)

    def fill_own(group, span, first):
        for index in range(2):
            value = block_of(group, core * 2 + index, span)
            for way in range(2):
                room = mine.at[group, way, pl.ds(index * 512, 512)]
                put(room, value[:, way * 256 : (way + 1) * 256], first)

    def fill_other(group, span, first):
        for index in range(2):
            value = block_of(group, (1 - core) * 2 + index, span)
            for way in range(2):
                put(spare(group, way, index), value[:, way * 256 : (way + 1) * 256], first)

    def sib_start(group):
        for way in range(2):
            for index in range(2):
                sib_copy(group, way, index).start()

    def slot_step(slot, _):
        is_forward = jnp.where(section == 0, slot < units, lax.rem(slot, 2) == 0)
        unit = jnp.where(section == 0, lax.rem(slot, units), lax.div(slot, 2))

        first_use = jnp.where(section == 0, is_forward, jnp.logical_not(is_forward))

        @pl.when(jnp.logical_and(first_use, lax.rem(unit, 2) == 1))
        def _():
            halo(lax.div(unit, 2)).wait_recv()

        @pl.when(is_forward)
        def _():
            @pl.when(section == 1)
            def _():
                x_copy(unit).wait_recv()

            forward(unit, slot)

            @pl.when(section == 0)
            def _():
                x_copy(unit).start()

        held = jnp.logical_and(section == 0, slot == 2 * units - 1)

        @pl.when(jnp.logical_not(jnp.logical_or(is_forward, held)))
        def _():
            @pl.when(section == 0)
            def _():
                x_copy(unit).wait_recv()

            backward(unit)

            @pl.when(section == 1)
            def _():
                x_copy(unit).start()

            @pl.when(jnp.logical_and(section == 0, unit == 0))
            def _():
                for group in range(GROUPS):
                    fill_own(group, pl.ds(0, rows), True)

            @pl.when(jnp.logical_and(section == 0, unit == 1))
            def _():
                for group in range(GROUPS):
                    fill_other(group, pl.ds(0, 2 * rows), True)

            return None

        @pl.when(jnp.logical_and(is_forward, unit == units - 1))
        def _():
            for index in range(4):
                peer_copy(index).start()

        return 0

    lax.fori_loop(0, 2 * units, slot_step, 0)

    def strip_copy(group):
        source = (2 * group + 1) * rows + either(rows - REACH, 0)
        return pltpu.make_async_remote_copy(
            src_ref=ob.at[1, pl.ds(pl.multiple_of(source, 16), REACH)], dst_ref=strip.at[group],
            send_sem=y_send.at[micro + group], recv_sem=y_recv.at[micro + group],
            device_id=beside, device_id_type=MESH,
        )

    def outputs(group, side):
        even, odd = 2 * group * rows, (2 * group + 1) * rows
        if side == 0:
            parts = ((even, 0, shift), (odd, shift, local - shift))
        else:
            parts = ((odd + REACH, 0, shift - REACH), (even, shift - REACH, rows))
        return [
            pltpu.make_async_copy(
                ob.at[1, pl.ds(source, size)], result.at[group, pl.ds(target, size)],
                out_sem.at[group, index],
            )
            for index, (source, target, size) in enumerate(parts)
        ]

    def finish():
        for group in range(micro):
            low_unit, high_unit = 2 * group + copy, 2 * group + 1 - copy
            over = rows - shift
            kept = pl.ds(pl.multiple_of(low_unit * rows + shift, 16), over)
            moved = pl.ds(pl.multiple_of(high_unit * rows, 16), over)
            ob[1, moved] = jnp.where(owned(low_unit, shift, over), ob[1, kept], ob[1, moved])
            strip_copy(group).wait_recv()
            odd_unit = 2 * group + 1
            first = either(shift, REACH)
            edge = pl.ds(pl.multiple_of(odd_unit * rows + first, 16), REACH)
            ob[1, edge] = jnp.where(owned(odd_unit, first, REACH), ob[1, edge], strip[group])
        for side in range(2):
            @pl.when(copy == side)
            def _():
                for group in range(micro):
                    for part in outputs(group, side):
                        part.start()

    def ours(group):
        for index in range(2):
            value = last_block(group, index)
            span = slice(index * 512, (index + 1) * 512)
            for way in range(2):
                sib_copy(group, way, index).wait_recv()
                part = value[:, way * 256 : (way + 1) * 256]
                total = part + mine[group, way, span].astype(F32) + sib[group, way, span].astype(F32)
                mine[group, way, span] = total.astype(BF16)

    def segment(position):
        return pl.ds(pl.multiple_of(around(position) * seg, 16), seg)

    def target(way):
        return tuple(jnp.where(way == 0, a, b) for a, b in zip(ahead, behind))

    def rs_copy(group, way, step, source):
        return pltpu.make_async_remote_copy(
            src_ref=source, dst_ref=rsb.at[group, way, step], send_sem=rs_send.at[group, way, step],
            recv_sem=rs_recv.at[group, way, step], device_id=target(way), device_id_type=MESH,
        )

    def final_rows(position):
        return pl.ds(pl.multiple_of(core * half + around(position) * seg, 16), seg)

    def ag_copy(group, way, step, source, position):
        return pltpu.make_async_remote_copy(
            src_ref=source, dst_ref=summed.at[group, way, final_rows(position)],
            send_sem=ag_send.at[group, way, step], recv_sem=ag_recv.at[group, way, step],
            device_id=target(way), device_id_type=MESH,
        )

    def pass_copy(group, way, source, position):
        return pltpu.make_async_remote_copy(
            src_ref=source, dst_ref=summed.at[group, way, final_rows(position)],
            send_sem=pass_send.at[group, way], recv_sem=pass_recv.at[group, way],
            device_id=sibling, device_id_type=MESH,
        )

    def own_copy(group, way):
        sign = 1 - 2 * way
        return pltpu.make_async_copy(
            rsb.at[group, way, chips - 2], summed.at[group, way, final_rows(place + sign)],
            own_sem.at[group, way],
        )

    def ring(group, way, step):
        sign = 1 - 2 * way

        @pl.when(step == 0)
        def _():
            rs_copy(group, way, 0, mine.at[group, way, segment(place)]).start()

        @pl.when(jnp.logical_and(step >= 1, step < chips))
        def _():
            last = step - 1
            slot = rsb.at[group, way, last]
            rs_copy(group, way, last, slot).wait_recv()
            part = mine[group, way, segment(place - sign * step)]
            rsb[group, way, last] = (rsb[group, way, last].astype(F32) + part.astype(F32)).astype(BF16)

            @pl.when(step < chips - 1)
            def _():
                rs_copy(group, way, step, slot).start()

            @pl.when(step == chips - 1)
            def _():
                ag_copy(group, way, 0, slot, place + sign).start()
                pass_copy(group, way, slot, place + sign).start()
                own_copy(group, way).start()

        @pl.when(jnp.logical_and(step >= chips, step < 2 * chips - 1))
        def _():
            last = step - chips
            position = place - sign * last
            arrived = summed.at[group, way, final_rows(position)]
            ag_copy(group, way, last, arrived, position).wait_recv()

            @pl.when(last + 1 < chips - 1)
            def _():
                ag_copy(group, way, last + 1, arrived, position).start()

            pass_copy(group, way, arrived, position).start()

    def slot_copy(step):
        return pltpu.make_async_remote_copy(
            src_ref=slots.at[step], dst_ref=slots.at[step + 1], send_sem=slot_send.at[step],
            recv_sem=slot_recv.at[step], device_id=ahead, device_id_type=MESH,
        )

    vec_copy = pltpu.make_async_remote_copy(
        src_ref=vec.at[pl.ds(0, 8)], dst_ref=vec.at[pl.ds(8, 8)], send_sem=slot_send.at[chips],
        recv_sem=slot_recv.at[chips], device_id=sibling, device_id_type=MESH,
    )
    def serve(group, step):
        def each(way, _):
            ring(group, way, step)
            return 0

        lax.fori_loop(0, 2, each, 0)

    last = units - 1
    @pl.when(section == 0)
    def _():
        for group in range(GROUPS):
            fill_other(group, pl.ds(2 * rows, rows), False)
            sib_start(group)
        for group in range(GROUPS):
            fill_own(group, pl.ds(rows, 2 * rows), False)

    @pl.when(section == 1)
    def _():
        for group in range(GROUPS):
            fill_other(group, pl.ds(0, 3 * rows), True)
            sib_start(group)
        for group in range(GROUPS):
            fill_own(group, pl.ds(0, 3 * rows), True)

    @pl.when(section == 0)
    def _():
        x_copy(last).wait_recv()
        backward_norm(last)

    peer_copy(4).start()

    @pl.when(section == 0)
    def _():
        backward_feed(last)

    peer_copy(5).start()

    @pl.when(section == 0)
    def _():
        backward_rest(last)

    peer_copy(6).start()
    peer_copy(7).start()
    vec_copy.start()
    for index in range(5):
        peer_copy(index).wait_recv()
    ours(0)
    serve(0, 0)
    peer_copy(5).wait_recv()
    ours(1)
    serve(1, 0)
    peer_copy(6).wait_recv()
    peer_copy(7).wait_recv()
    ours(2)
    serve(2, 0)

    @pl.when(section == 0)
    def _():
        backward_input(last)

    for group in range(micro):
        strip_copy(group).start()
    vec_copy.wait()
    slots[0] = vec[0:8] + vec[8:16]

    def round_step(index, _):
        def each(flat, _):
            group, way = lax.div(flat, 2), lax.rem(flat, 2)
            ring(group, way, index)
            return 0

        lax.fori_loop(0, 2 * GROUPS, each, 0)

        @pl.when(index < chips)
        def _():
            @pl.when(index > 1)
            def _():
                slot_copy(index - 2).wait_recv()

            slot_copy(index - 1).start()

        return 0

    lax.fori_loop(1, 4, round_step, 0)
    finish()
    lax.fori_loop(4, 2 * chips - 1, round_step, 0)
    slot_copy(chips - 2).wait_recv()
    total = jnp.zeros((8, width), F32)
    for position in range(chips):
        total = total + slots[around(place - position)]
    vec[0:8] = total
    told = pltpu.make_async_copy(vec.at[pl.ds(0, 8)], vectors.at[pl.ds(0, 8)], in_sem.at[0])
    told.start()

    def drain(flat, _):
        group, way = lax.div(flat, 2), lax.rem(flat, 2)
        own_copy(group, way).wait()

        def each(step, _):
            rs_copy(group, way, step, rsb.at[group, way, 0]).wait_send()
            ag_copy(group, way, step, rsb.at[group, way, 0], place).wait_send()
            return 0

        lax.fori_loop(0, chips - 1, each, 0)
        whole = pltpu.make_async_remote_copy(
            src_ref=summed.at[group, way, pl.ds(0, half)], dst_ref=summed.at[group, way, pl.ds(0, half)],
            send_sem=pass_send.at[group, way], recv_sem=pass_recv.at[group, way],
            device_id=sibling, device_id_type=MESH,
        )
        whole.wait_send()
        whole.wait_recv()
        return 0

    lax.fori_loop(0, 2 * GROUPS, drain, 0)
    for group in range(GROUPS):
        for way in range(2):
            for index in range(2):
                sib_copy(group, way, index).wait_send()
    for index in range(8):
        peer_copy(index).wait_send()

    def drain_slots(step, _):
        slot_copy(step).wait_send()
        return 0

    lax.fori_loop(0, chips - 1, drain_slots, 0)

    def drain_units(unit, _):
        x_copy(unit).wait_send()
        return 0

    lax.fori_loop(0, units, drain_units, 0)
    told.wait()
    for group in range(micro):
        halo(group).wait_send()
        strip_copy(group).wait_send()
    for side in range(2):
        @pl.when(copy == side)
        def _():
            for group in range(micro):
                for part in outputs(group, side):
                    part.wait()


def widen(summed, vectors, merged, qkv, out, inner, outer, gain, shift, result, narrow, wide, held, rows, in_sem, out_sem, rest_sem):
    homes = []
    for index in range(8):
        homes.append(outer.at[0, pl.ds(index * 256, 256)])
    for column in range(4):
        for part in range(2):
            homes.append(inner.at[0, pl.ds(part * 256, 256), pl.ds(column * 512, 512)])
    for part in range(2):
        homes.append(out.at[0, pl.ds(part * 256, 256)])
    for column in range(3):
        for part in range(2):
            homes.append(qkv.at[0, pl.ds(part * 256, 256), pl.ds(column * 512, 512)])
    loads = [
        pltpu.make_async_copy(
            summed.at[index // 8, :, pl.ds(index % 8 * 256, 256)], narrow.at[index], in_sem.at[index]
        )
        for index in range(len(homes))
    ]
    stores = [
        pltpu.make_async_copy(wide.at[index], home, out_sem.at[index]) for index, home in enumerate(homes)
    ]
    firsts = [
        pltpu.make_async_copy(merged.at[pl.ds(0, held.shape[0])], held, rest_sem.at[0]),
        pltpu.make_async_copy(vectors.at[pl.ds(0, 8)], rows, rest_sem.at[1]),
    ]
    seconds = [
        pltpu.make_async_copy(held, result.at[0, :, 0], rest_sem.at[2]),
        pltpu.make_async_copy(rows.at[pl.ds(0, 2)], gain.at[0], rest_sem.at[3]),
        pltpu.make_async_copy(rows.at[pl.ds(2, 2)], shift.at[0], rest_sem.at[4]),
    ]
    for load in loads:
        load.start()
    for copy_of in firsts:
        copy_of.start()
    for index, (load, store) in enumerate(zip(loads, stores)):
        load.wait()
        for way in range(2):
            wide[index, :, way * 256 : (way + 1) * 256] = narrow[index, way].astype(F32)
        store.start()
    for copy_of in firsts:
        copy_of.wait()
    for copy_of in seconds:
        copy_of.start()
    for copy_of in stores + seconds:
        copy_of.wait()


def per_device(mesh, boundary, sentence_ids, qkv_weight, out_weight, inner_weight, outer_weight, norm_gain, norm_bias):
    micro, local, width = boundary.shape[1], boundary.shape[3], boundary.shape[4]
    inner_width = inner_weight.shape[2]
    length = sentence_ids.shape[2]
    chips = mesh.shape["copy"] * mesh.shape["dp"] // 2
    rows = (local + REACH) // 2 + REACH
    units = micro * 2
    tokens = units * rows
    any_space = pl.BlockSpec(memory_space=pl.ANY)
    vmem = pl.BlockSpec(memory_space=pltpu.VMEM)
    dma = pltpu.SemaphoreType.DMA
    hops = chips - 1
    result, summed, vectors = pl.pallas_call(
        functools.partial(kernel, units, rows, chips, width, inner_width),
        out_shape=(
            jax.ShapeDtypeStruct((4 * micro, local, width), BF16),
            jax.ShapeDtypeStruct((GROUPS, 2, 2048, 256), BF16),
            jax.ShapeDtypeStruct((2048, width), F32),
        ),
        in_specs=[any_space, vmem] + [any_space] * 4 + [vmem] * 2,
        out_specs=(any_space, any_space, any_space),
        scratch_shapes=[
            pltpu.VMEM((width, 3 * width), BF16),
            pltpu.VMEM((width, width), BF16),
            pltpu.VMEM((width, inner_width), BF16),
            pltpu.VMEM((inner_width, width), BF16),
            pltpu.VMEM((8, length), F32),
            pltpu.VMEM((length, 8), F32),
            pltpu.VMEM((2, tokens, width), BF16),
            pltpu.VMEM((2, tokens, width), BF16),
            pltpu.VMEM((tokens + 80, 3 * width), BF16),
            pltpu.VMEM((tokens, width), BF16),
            pltpu.VMEM((tokens, width), BF16),
            pltpu.VMEM((tokens, inner_width), BF16),
            pltpu.VMEM((tokens, inner_width), BF16),
            pltpu.VMEM((tokens, width), F32),
            pltpu.VMEM((tokens, width), F32),
            pltpu.VMEM((tokens, 2), F32),
            pltpu.VMEM((tokens, width), BF16),
            pltpu.VMEM((tokens, width), BF16),
            pltpu.VMEM((tokens, 3 * width), BF16),
            pltpu.VMEM((tokens, HEADS * WINDOW), BF16),
            pltpu.VMEM((tokens, width), F32),
            pltpu.VMEM((rows, WINDOW), F32),
            pltpu.VMEM((rows, width), BF16),
            pltpu.VMEM((rows, width), F32),
            pltpu.VMEM((2, 128, 384), F32),
            pltpu.VMEM((micro, REACH, width), BF16),
            pltpu.VMEM((GROUPS, 2, 1024, 256), BF16),
            pltpu.VMEM((GROUPS, 2, 1024, 256), BF16),
            pltpu.VMEM((GROUPS, 2, hops, 1024 // chips, 256), BF16),
            pltpu.VMEM((16, width), F32),
            pltpu.VMEM((chips, 8, width), F32),
            pltpu.VMEM((rows, 1024), BF16),
            pltpu.VMEM((rows, width), BF16),
            pltpu.VMEM((rows, width), BF16),
            pltpu.VMEM((rows, width), BF16),
            pltpu.VMEM((rows, width), BF16),
            pltpu.VMEM((rows, 1024), BF16),
            pltpu.VMEM((rows, width), BF16),
            pltpu.VMEM((rows, 1024), BF16),
            dma((4,)), dma((units,)), dma((micro, 2)), dma((units,)), dma((units,)),
            dma((2 * micro,)), dma((2 * micro,)), dma((GROUPS, 2, 2)), dma((GROUPS, 2, 2)),
            dma((GROUPS, 2, hops)), dma((GROUPS, 2, hops)), dma((GROUPS, 2, hops)), dma((GROUPS, 2, hops)),
            dma((chips + 1,)), dma((chips + 1,)), dma((GROUPS, 2)), dma((GROUPS, 2)), dma((GROUPS, 2)),
            dma((8,)), dma((8,)),
        ],
        compiler_params=pltpu.CompilerParams(
            collective_id=0, has_side_effects=True, vmem_limit_bytes=63 * 1024 * 1024
        ),
    )(boundary, sentence_ids, qkv_weight, out_weight, inner_weight, outer_weight, norm_gain, norm_bias)

    blocks = 8 * GROUPS
    hbm = pl.BlockSpec(memory_space=pltpu.HBM)
    grad_qkv, grad_out, grad_inner, grad_outer, grad_gain, grad_bias, result = pl.pallas_call(
        widen,
        out_shape=tuple(
            jax.ShapeDtypeStruct(item.shape, F32)
            for item in (qkv_weight, out_weight, inner_weight, outer_weight, norm_gain, norm_bias)
        )
        + (jax.ShapeDtypeStruct(boundary.shape, BF16),),
        in_specs=[hbm] * 3,
        out_specs=(hbm,) * 7,
        scratch_shapes=[
            pltpu.VMEM((blocks, 2, 256, 256), BF16), pltpu.VMEM((blocks, 256, 512), F32),
            pltpu.VMEM((micro, local, width), BF16), pltpu.VMEM((8, width), F32), dma((blocks,)), dma((blocks,)), dma((5,)),
        ],
        compiler_params=pltpu.CompilerParams(vmem_limit_bytes=62 * 1024 * 1024),
    )(summed, vectors, result)
    return (result, grad_qkv, grad_out, grad_inner, grad_outer, grad_gain, grad_bias)


def solution(mesh):
    weight = P("section", None, None)
    edge = P("section", None, "dp", "copy", None)
    return jax.shard_map(
        functools.partial(per_device, mesh),
        mesh=mesh,
        in_specs=(edge, P(None, "dp", None)) + (weight,) * 6,
        out_specs=(edge,) + (weight,) * 6,
        check_vma=False,
    )
```

```python
import functools

import jax
import jax.numpy as jnp
from jax import lax
from jax.experimental import pallas as pl
from jax.experimental.pallas import tpu as pltpu
from jax.sharding import PartitionSpec as P

HEADS = 8
REACH = 32
WINDOW = 256
NEG = -1e30
EPS = 1e-05
GROUPS = 3
BLOCKS = ((0, 192, 0), (192, 112, 128))
MESH = pl.DeviceIdType.MESH
F32 = jnp.float32
BF16 = jnp.bfloat16


def mul(left, right):
    return jnp.dot(left, right, preferred_element_type=F32)


def against(left, right):
    return lax.dot_general(left, right, (((1,), (1,)), ((), ())), preferred_element_type=F32)


def contract(left, right):
    return lax.dot_general(left, right, (((0,), (0,)), ((), ())), preferred_element_type=F32)


def gelu(x):
    phi = 0.5 + 0.5 * lax.erf(x * 0.7071067811865476)
    bell = jnp.exp2(x * x * -0.7213475204444817)
    return (x * phi).astype(BF16), (phi + x * 0.3989422804014327 * bell).astype(BF16)


def normalize(resid):
    center = resid - jnp.mean(resid, axis=-1, keepdims=True)
    spread = jnp.mean(center * center, axis=-1, keepdims=True)
    inverse = lax.rsqrt(spread + EPS)
    return center * inverse, inverse


def normalize_back(upstream, scaled, inverse, gain):
    tilted = upstream * gain
    first = jnp.mean(tilted, axis=-1, keepdims=True)
    second = jnp.mean(tilted * scaled, axis=-1, keepdims=True)
    return inverse * (tilted - first - scaled * second)


def halves(pair):
    lane = lax.broadcasted_iota(jnp.int32, pair.shape, 1)
    zero = jnp.zeros_like(pair)
    return jnp.where(lane < 64, pair, zero), jnp.where(lane < 64, zero, pair)


def kernel(
    units, rows, chips, width, inner_width,
    boundary, ids, qkv_weight, out_weight, inner_weight, outer_weight, gain_rows, shift_rows,
    result, summed, vectors,
    w_qkv, w_out, w_in, w_outer, info, column,
    xb, ob, mixed, att, nlow, act, dg, one, two, inv, goi, gai, gmix, probs, scale,
    bias, gatt, hold, strip, mine, sib, rsb, vec, slots,
    peer_act, peer_nlow, peer_att, peer_in, peer_goi, peer_dg, peer_gai, peer_gmix,
    weight_sem, in_sem, out_sem, x_send, x_recv, y_send, y_recv, sib_send, sib_recv, rs_send, rs_recv,
    ag_send, ag_recv, slot_send, slot_recv, pass_send, pass_recv, own_sem, peer_send, peer_recv,
):
    blocks = BLOCKS
    micro, local = boundary.shape[1], boundary.shape[3]
    length = ids.shape[2]
    reach = local + REACH
    shift = reach - rows
    section, copy, dp = lax.axis_index("section"), lax.axis_index("copy"), lax.axis_index("dp")
    core, layer = lax.rem(dp, 2), lax.div(dp, 2)
    line = chips // 2
    place = jnp.where(copy == 0, layer, chips - 1 - layer)
    gains, shifts = gain_rows.at[0], shift_rows.at[0]

    def either(first, second):
        return jnp.where(copy == 0, first, second)

    def at(position):
        far = position >= line
        return (section, jnp.where(far, 1, 0), 2 * jnp.where(far, chips - 1 - position, position) + core)

    def around(position):
        return lax.rem(position + 2 * chips, chips)

    across = (1 - section, copy, dp)
    beside = (section, 1 - copy, dp)
    sibling = (section, copy, dp + 1 - 2 * core)
    ahead, behind = at(around(place + 1)), at(around(place - 1))

    def load(unit):
        group, odd = unit // 2, unit % 2
        if odd:
            source, target, size = either(shift, 0), either(0, REACH), rows - REACH
        else:
            source, target, size = either(0, local - rows), 0, rows
        return pltpu.make_async_copy(
            boundary.at[0, group, 0, pl.ds(pl.multiple_of(source, 16), size)],
            xb.at[0, pl.ds(pl.multiple_of(unit * rows + target, 16), size)], in_sem.at[unit],
        )

    def halo(group):
        source, target = either(local - REACH, 0), (2 * group + 1) * rows + either(0, rows - REACH)
        return pltpu.make_async_remote_copy(
            src_ref=boundary.at[0, group, 0, pl.ds(pl.multiple_of(source, 16), REACH)],
            dst_ref=xb.at[0, pl.ds(pl.multiple_of(target, 16), REACH)],
            send_sem=y_send.at[group], recv_sem=y_recv.at[group],
            device_id=beside, device_id_type=MESH,
        )

    weights = [
        pltpu.make_async_copy(source.at[0], target, weight_sem.at[index])
        for index, (source, target) in enumerate(
            ((qkv_weight, w_qkv), (out_weight, w_out), (inner_weight, w_in), (outer_weight, w_outer))
        )
    ]
    load(0).start()
    for weight in weights:
        weight.start()
    for unit in range(1, units):
        load(unit).start()
    vec[...] = jnp.zeros_like(vec)
    for unit in range(units):
        mixed[(unit + 1) * rows : (unit + 1) * rows + 80] = jnp.zeros((80, 3 * width), BF16)
    barrier = pltpu.get_barrier_semaphore()
    for other in (across, beside, sibling, ahead, behind):
        pl.semaphore_signal(barrier, inc=1, device_id=other, device_id_type=MESH)

    spot = lax.broadcasted_iota(jnp.int32, (micro, length), 1)
    sentence = ids[:, 0, :]
    cuts = (reach // 2, local, length - reach // 2)
    owner = jnp.zeros((micro, length), jnp.int32)
    for cut in cuts:
        owner = owner + jnp.where(spot >= cut, 1, 0)
    for index, cut in enumerate(cuts):
        crossing = sentence == sentence[:, cut - 1 : cut]
        left = jnp.sum(jnp.where(crossing & (spot < cut), 1.0, 0.0), axis=1, keepdims=True)
        right = jnp.sum(jnp.where(crossing & (spot >= cut), 1.0, 0.0), axis=1, keepdims=True)
        side = jnp.where(left >= right, index, index + 1)
        owner = jnp.where(crossing, side, owner)
    info[...] = jnp.zeros_like(info)
    info[0:micro] = sentence.astype(F32)
    info[micro : 2 * micro] = owner.astype(F32)
    column[...] = info[...].T

    def piece_of(unit):
        odd = lax.rem(unit, 2)
        return either(odd, 1 - odd)

    def begin_of(unit):
        return copy * (local - REACH) + piece_of(unit) * shift

    def pick(unit, first, size, kind):
        spots = pl.ds(pl.multiple_of(begin_of(unit) + first, 16), size)
        both = column[spots, kind * micro : (kind + 1) * micro]
        return jnp.where(unit < 2, both[:, 0:1], both[:, 1:2])

    def owned(unit, first, size):
        return pick(unit, first, size, 1) == (2 * copy + piece_of(unit)).astype(F32)

    load(0).wait()
    weights[0].wait()

    def unit_rows(unit):
        return pl.ds(pl.multiple_of(unit * rows, 16), rows)

    def x_copy(unit):
        span = unit_rows(unit)
        return pltpu.make_async_remote_copy(
            src_ref=ob.at[0, span], dst_ref=xb.at[1, span], send_sem=x_send.at[unit],
            recv_sem=x_recv.at[unit], device_id=across, device_id_type=MESH,
        )

    def forward(unit, slot):
        span = unit_rows(unit)
        start = pl.multiple_of(unit * rows, 16)
        hidden = xb[section, span]
        mixed[span, 0:width] = (mul(hidden, w_qkv[:, 0:width]) * 0.125).astype(BF16)
        mixed[span, width:] = mul(hidden, w_qkv[:, width:]).astype(BF16)
        for index, (first, size, begin) in enumerate(blocks):
            turned = pltpu.roll(info[...], length - begin_of(unit) - begin, 1)[0:micro, 0:WINDOW]
            near_ids = jnp.where(unit < 2, turned[0:1], turned[1:2])
            inside = lax.broadcasted_iota(jnp.int32, near_ids.shape, 1) < rows - begin
            near_ids = jnp.where(inside, near_ids, -1.0)
            allowed = pick(unit, first, size, 0) == near_ids
            bias[first : first + size] = jnp.where(allowed, 0.0, NEG)

        def pair_step(pair, _):
            lanes = pl.multiple_of(pair * 128, 128)
            for first, size, begin in blocks:
                near = pl.ds(pl.multiple_of(start + begin, 16), WINDOW)
                own = pl.ds(pl.multiple_of(start + first, 16), size)
                query = jnp.concatenate(halves(mixed[own, pl.ds(lanes, 128)]), axis=0)
                key = mixed[near, pl.ds(pl.multiple_of(width + pair * 128, 128), 128)]
                value = mixed[near, pl.ds(pl.multiple_of(2 * width + pair * 128, 128), 128)]
                barred = bias[first : first + size]
                scores = against(query, key) + jnp.concatenate([barred, barred], axis=0)
                share = jnp.exp(scores - jnp.max(scores, axis=-1, keepdims=True)).astype(BF16)
                for head in range(2):
                    cols = pl.ds(pl.multiple_of(pair * 512 + head * 256, 256), 256)
                    probs[own, cols] = share[head * size : (head + 1) * size]
                sums = mul(share, jnp.concatenate([value, jnp.ones((WINDOW, 128), BF16)], axis=1))
                lane = lax.broadcasted_iota(jnp.int32, (size, 128), 1)
                inverse = 1.0 / jnp.where(lane < 64, sums[:size, 128:], sums[size:, 128:])
                attended = jnp.where(lane < 64, sums[:size, :128], sums[size:, :128])
                att[own, pl.ds(lanes, 128)] = (attended * inverse).astype(BF16)
                scale[own, pl.ds(lanes, 128)] = inverse
            return 0

        lax.fori_loop(0, width // 128, pair_step, 0, unroll=True)
        @pl.when(slot == 0)
        def _():
            for weight in weights[1:]:
                weight.wait()
            for odd in range(1, units):
                load(odd).wait()
            pl.semaphore_wait(barrier, 5)
            for group in range(micro):
                halo(group).start()

        scaled, inverse = normalize(xb[section, span].astype(F32) + mul(att[span], w_out[...]))
        one[span] = scaled
        inv[span, 0:1] = inverse
        normed = scaled * gains[0:1] + shifts[0:1]
        hold[...] = normed
        low = normed.astype(BF16)
        nlow[span] = low
        tile = 256
        count = inner_width // tile
        inner = mul(nlow[span], w_in[:, 0:tile])
        outer = hold[...]
        for step in range(count):
            ahead_inner = None
            if step + 1 < count:
                ahead_inner = mul(nlow[span], w_in[:, (step + 1) * tile : (step + 2) * tile])
            cols = pl.ds(step * tile, tile)
            active, slope = gelu(inner)
            act[span, cols] = active
            dg[span, cols] = slope
            outer = outer + mul(active, w_outer[cols])
            inner = ahead_inner
        scaled, inverse = normalize(outer)
        two[span] = scaled
        inv[span, 1:2] = inverse
        ob[section, span] = (scaled * gains[1:2] + shifts[1:2]).astype(BF16)

    def backward_norm(unit):
        span = unit_rows(unit)
        upstream = jnp.where(owned(unit, 0, rows), xb[1 - section, span].astype(F32), 0.0)
        scaled = two[span]
        vec[1:2] += jnp.sum(upstream * scaled, axis=0, keepdims=True)
        vec[3:4] += jnp.sum(upstream, axis=0, keepdims=True)
        grad_two = normalize_back(upstream, scaled, inv[span, 1:2], gains[1:2])
        goi[span] = grad_two.astype(BF16)
        return grad_two

    def backward_feed(unit, grad_two):
        span = unit_rows(unit)
        tile = 512
        count = inner_width // tile
        grad_active = against(goi[span], w_outer[0:tile])
        total = grad_two
        for step in range(count):
            next_active = None
            if step + 1 < count:
                next_active = against(goi[span], w_outer[(step + 1) * tile : (step + 2) * tile])
            cols = pl.ds(step * tile, tile)
            grad_inner = (grad_active * dg[span, cols].astype(F32)).astype(BF16)
            dg[span, cols] = grad_inner
            total = total + against(grad_inner, w_in[:, step * tile : (step + 1) * tile])
            grad_active = next_active
        return total

    def backward_rest(unit, total):
        span = unit_rows(unit)
        start = pl.multiple_of(unit * rows, 16)
        scaled = one[span]
        vec[0:1] += jnp.sum(total * scaled, axis=0, keepdims=True)
        vec[2:3] += jnp.sum(total, axis=0, keepdims=True)
        grad_one = normalize_back(total, scaled, inv[span, 0:1], gains[0:1])
        hold[...] = grad_one
        low = grad_one.astype(BF16)
        gai[span] = low
        gatt[...] = (against(low, w_out[...]) * scale[span]).astype(BF16)

        def pair_step(pair, _):
            lanes = pl.multiple_of(pair * 128, 128)
            key_lanes = pl.ds(pl.multiple_of(width + pair * 128, 128), 128)
            value_lanes = pl.ds(pl.multiple_of(2 * width + pair * 128, 128), 128)
            parts = ([], [])
            for first, size, begin in blocks:
                near = pl.ds(pl.multiple_of(start + begin, 16), WINDOW)
                own = pl.ds(pl.multiple_of(start + first, 16), size)
                query = jnp.concatenate(halves(mixed[own, pl.ds(lanes, 128)]), axis=0)
                key = mixed[near, key_lanes]
                value = mixed[near, value_lanes]
                grad_pair = gatt[first : first + size, pl.ds(lanes, 128)]
                paired = (grad_pair.astype(F32) * att[own, pl.ds(lanes, 128)].astype(F32)).astype(BF16)
                grad = jnp.concatenate(halves(grad_pair), axis=0)
                left = jnp.concatenate([grad, jnp.concatenate(halves(paired), axis=0)], axis=1)
                share = jnp.concatenate(
                    [probs[own, pl.ds(pl.multiple_of(pair * 512 + head * 256, 256), 256)] for head in range(2)],
                    axis=0,
                )
                tilt = against(left, jnp.concatenate([value, jnp.full((WINDOW, 128), -1.0, BF16)], axis=1))
                grads = (share.astype(F32) * tilt).astype(BF16)
                wide = mul(grads, key)
                lane = lax.broadcasted_iota(jnp.int32, (size, 128), 1)
                grad_query = jnp.where(lane < 64, wide[:size], wide[size:])
                gmix[own, pl.ds(lanes, 128)] = (grad_query * 0.125).astype(BF16)
                for kind, (small, sides) in enumerate(((mixed[own, pl.ds(lanes, 128)], grads), (grad_pair, share))):
                    turned = small.T
                    heads = [
                        mul(turned[head * 64 : (head + 1) * 64], sides[head * size : (head + 1) * size])
                        for head in range(2)
                    ]
                    parts[kind].append(jnp.concatenate(heads, axis=0))
            for kind, home in enumerate((key_lanes, value_lanes)):
                low, high = parts[kind]
                middle = low[:, 128:] + high[:, :128]
                whole = jnp.concatenate([low[:, :128], middle, high[:, 128:]], axis=1)
                gmix[span, home] = whole.astype(BF16).T[0:rows]
            return 0

        lax.fori_loop(0, width // 128, pair_step, 0, unroll=True)

    def backward_input(unit):
        span = unit_rows(unit)
        ob[1 - section, span] = (hold[...] + against(gmix[span], w_qkv[...])).astype(BF16)

    def backward(unit):
        backward_rest(unit, backward_feed(unit, backward_norm(unit)))
        backward_input(unit)

    half = 1024
    seg = half // chips

    def spare(group, way, index):
        tile = way * 2 + index
        if group == 2:
            return mixed.at[pl.ds(0, 512), pl.ds(tile * 256, 256)]
        return probs.at[pl.ds(0, 512), pl.ds((group * 4 + tile) * 256, 256)]

    def sib_copy(group, way, index):
        return pltpu.make_async_remote_copy(
            src_ref=spare(group, way, index), dst_ref=sib.at[group, way, pl.ds(index * 512, 512)],
            send_sem=sib_send.at[group, way, index], recv_sem=sib_recv.at[group, way, index],
            device_id=sibling, device_id_type=MESH,
        )

    def block_of(group, block, span):
        cols = pl.ds(pl.multiple_of(block * 512, 512), 512)
        if group == 0:
            return contract(act[span, cols], goi[span])
        if group == 1:
            return contract(nlow[span], dg[span, cols])
        cols = pl.ds(pl.multiple_of(jnp.maximum(block - 1, 0) * 512, 512), 512)
        left = jnp.where(block == 0, att[span], xb[section, span])
        return contract(left, jnp.where(block == 0, gai[span], gmix[span, cols]))

    def both(own, peer):
        return jnp.concatenate([own, peer], axis=0)

    def last_block(group, index):
        span = pl.ds((units - 1) * rows, rows)
        block = core * 2 + index
        cols = pl.ds(pl.multiple_of(block * 512, 512), 512)
        here = slice(index * 512, (index + 1) * 512)
        if group == 0:
            return contract(both(act[span, cols], peer_act[:, here]), both(goi[span], peer_goi[...]))
        if group == 1:
            return contract(both(nlow[span], peer_nlow[...]), both(dg[span, cols], peer_dg[:, here]))
        cols = pl.ds(pl.multiple_of(jnp.maximum(block - 1, 0) * 512, 512), 512)
        first = block == 0
        peer_cols = pl.ds(pl.multiple_of(jnp.where(first, 0, (core + index - 1) * 512), 512), 512)
        left = jnp.where(first, both(att[span], peer_att[...]), both(xb[section, span], peer_in[...]))
        right = jnp.where(first, both(gai[span], peer_gai[...]), both(gmix[span, cols], peer_gmix[:, peer_cols]))
        return contract(left, right)

    def peer_copy(index):
        span = pl.ds((units - 1) * rows, rows)
        wide = pl.ds(pl.multiple_of((1 - core) * 1024, 512), 1024)
        near = pl.ds(pl.multiple_of((1 - core) * 512, 512), 1024)
        source, target = (
            (act.at[span, wide], peer_act), (nlow.at[span], peer_nlow), (att.at[span], peer_att),
            (xb.at[section, span], peer_in), (goi.at[span], peer_goi), (dg.at[span, wide], peer_dg),
            (gai.at[span], peer_gai), (gmix.at[span, near], peer_gmix),
        )[index]
        return pltpu.make_async_remote_copy(
            src_ref=source, dst_ref=target, send_sem=peer_send.at[index], recv_sem=peer_recv.at[index],
            device_id=sibling, device_id_type=MESH,
        )

    def put(room, part, first):
        room[...] = (part if first else part + room[...].astype(F32)).astype(BF16)

    def fill_own(group, span, first):
        for index in range(2):
            value = block_of(group, core * 2 + index, span)
            for way in range(2):
                room = mine.at[group, way, pl.ds(index * 512, 512)]
                put(room, value[:, way * 256 : (way + 1) * 256], first)

    def fill_other(group, span, first):
        for index in range(2):
            value = block_of(group, (1 - core) * 2 + index, span)
            for way in range(2):
                put(spare(group, way, index), value[:, way * 256 : (way + 1) * 256], first)

    def sib_start(group):
        for way in range(2):
            for index in range(2):
                sib_copy(group, way, index).start()

    def slot_step(slot, _):
        is_forward = jnp.where(section == 0, slot < units, lax.rem(slot, 2) == 0)
        unit = jnp.where(section == 0, lax.rem(slot, units), lax.div(slot, 2))

        first_use = jnp.where(section == 0, is_forward, jnp.logical_not(is_forward))

        @pl.when(jnp.logical_and(first_use, lax.rem(unit, 2) == 1))
        def _():
            halo(lax.div(unit, 2)).wait_recv()

        @pl.when(is_forward)
        def _():
            @pl.when(section == 1)
            def _():
                x_copy(unit).wait_recv()

            forward(unit, slot)

            @pl.when(section == 0)
            def _():
                x_copy(unit).start()

        held = jnp.logical_and(section == 0, slot == 2 * units - 1)

        @pl.when(jnp.logical_not(jnp.logical_or(is_forward, held)))
        def _():
            @pl.when(section == 0)
            def _():
                x_copy(unit).wait_recv()

            backward(unit)

            @pl.when(section == 1)
            def _():
                x_copy(unit).start()

            @pl.when(jnp.logical_and(section == 0, unit == 0))
            def _():
                for group in range(GROUPS):
                    fill_own(group, pl.ds(0, rows), True)

            @pl.when(jnp.logical_and(section == 0, unit == 1))
            def _():
                for group in range(GROUPS):
                    fill_other(group, pl.ds(0, 2 * rows), True)

            return None

        @pl.when(jnp.logical_and(is_forward, unit == units - 1))
        def _():
            for index in range(4):
                peer_copy(index).start()

        return 0

    lax.fori_loop(0, 2 * units, slot_step, 0)

    def strip_copy(group):
        source = (2 * group + 1) * rows + either(rows - REACH, 0)
        return pltpu.make_async_remote_copy(
            src_ref=ob.at[1, pl.ds(pl.multiple_of(source, 16), REACH)], dst_ref=strip.at[group],
            send_sem=y_send.at[micro + group], recv_sem=y_recv.at[micro + group],
            device_id=beside, device_id_type=MESH,
        )

    def outputs(group, side):
        even, odd = 2 * group * rows, (2 * group + 1) * rows
        if side == 0:
            parts = ((even, 0, shift), (odd, shift, local - shift))
        else:
            parts = ((odd + REACH, 0, shift - REACH), (even, shift - REACH, rows))
        return [
            pltpu.make_async_copy(
                ob.at[1, pl.ds(source, size)], result.at[group, pl.ds(target, size)],
                out_sem.at[group, index],
            )
            for index, (source, target, size) in enumerate(parts)
        ]

    def finish():
        for group in range(micro):
            low_unit, high_unit = 2 * group + copy, 2 * group + 1 - copy
            over = rows - shift
            kept = pl.ds(pl.multiple_of(low_unit * rows + shift, 16), over)
            moved = pl.ds(pl.multiple_of(high_unit * rows, 16), over)
            ob[1, moved] = jnp.where(owned(low_unit, shift, over), ob[1, kept], ob[1, moved])
            strip_copy(group).wait_recv()
            odd_unit = 2 * group + 1
            first = either(shift, REACH)
            edge = pl.ds(pl.multiple_of(odd_unit * rows + first, 16), REACH)
            ob[1, edge] = jnp.where(owned(odd_unit, first, REACH), ob[1, edge], strip[group])
        for side in range(2):
            @pl.when(copy == side)
            def _():
                for group in range(micro):
                    for part in outputs(group, side):
                        part.start()

    def ours(group):
        for index in range(2):
            value = last_block(group, index)
            span = slice(index * 512, (index + 1) * 512)
            for way in range(2):
                sib_copy(group, way, index).wait_recv()
                part = value[:, way * 256 : (way + 1) * 256]
                total = part + mine[group, way, span].astype(F32) + sib[group, way, span].astype(F32)
                mine[group, way, span] = total.astype(BF16)

    def segment(position):
        return pl.ds(pl.multiple_of(around(position) * seg, 16), seg)

    def target(way):
        return tuple(jnp.where(way == 0, a, b) for a, b in zip(ahead, behind))

    def rs_copy(group, way, step, source):
        return pltpu.make_async_remote_copy(
            src_ref=source, dst_ref=rsb.at[group, way, step], send_sem=rs_send.at[group, way, step],
            recv_sem=rs_recv.at[group, way, step], device_id=target(way), device_id_type=MESH,
        )

    def final_rows(position):
        return pl.ds(pl.multiple_of(core * half + around(position) * seg, 16), seg)

    def ag_copy(group, way, step, source, position):
        return pltpu.make_async_remote_copy(
            src_ref=source, dst_ref=summed.at[group, way, final_rows(position)],
            send_sem=ag_send.at[group, way, step], recv_sem=ag_recv.at[group, way, step],
            device_id=target(way), device_id_type=MESH,
        )

    def pass_copy(group, way, source, position):
        return pltpu.make_async_remote_copy(
            src_ref=source, dst_ref=summed.at[group, way, final_rows(position)],
            send_sem=pass_send.at[group, way], recv_sem=pass_recv.at[group, way],
            device_id=sibling, device_id_type=MESH,
        )

    def own_copy(group, way):
        sign = 1 - 2 * way
        return pltpu.make_async_copy(
            rsb.at[group, way, chips - 2], summed.at[group, way, final_rows(place + sign)],
            own_sem.at[group, way],
        )

    def ring(group, way, step):
        sign = 1 - 2 * way

        @pl.when(step == 0)
        def _():
            rs_copy(group, way, 0, mine.at[group, way, segment(place)]).start()

        @pl.when(jnp.logical_and(step >= 1, step < chips))
        def _():
            last = step - 1
            slot = rsb.at[group, way, last]
            rs_copy(group, way, last, slot).wait_recv()
            part = mine[group, way, segment(place - sign * step)]
            rsb[group, way, last] = (rsb[group, way, last].astype(F32) + part.astype(F32)).astype(BF16)

            @pl.when(step < chips - 1)
            def _():
                rs_copy(group, way, step, slot).start()

            @pl.when(step == chips - 1)
            def _():
                ag_copy(group, way, 0, slot, place + sign).start()
                pass_copy(group, way, slot, place + sign).start()
                own_copy(group, way).start()

        @pl.when(jnp.logical_and(step >= chips, step < 2 * chips - 1))
        def _():
            last = step - chips
            position = place - sign * last
            arrived = summed.at[group, way, final_rows(position)]
            ag_copy(group, way, last, arrived, position).wait_recv()

            @pl.when(last + 1 < chips - 1)
            def _():
                ag_copy(group, way, last + 1, arrived, position).start()

            pass_copy(group, way, arrived, position).start()

    def slot_copy(step):
        return pltpu.make_async_remote_copy(
            src_ref=slots.at[step], dst_ref=slots.at[step + 1], send_sem=slot_send.at[step],
            recv_sem=slot_recv.at[step], device_id=ahead, device_id_type=MESH,
        )

    vec_copy = pltpu.make_async_remote_copy(
        src_ref=vec.at[pl.ds(0, 8)], dst_ref=vec.at[pl.ds(8, 8)], send_sem=slot_send.at[chips],
        recv_sem=slot_recv.at[chips], device_id=sibling, device_id_type=MESH,
    )
    def serve(group, step):
        def each(way, _):
            ring(group, way, step)
            return 0

        lax.fori_loop(0, 2, each, 0)

    last = units - 1
    @pl.when(section == 0)
    def _():
        for group in range(GROUPS):
            fill_other(group, pl.ds(2 * rows, rows), False)
            sib_start(group)
        for group in range(GROUPS):
            fill_own(group, pl.ds(rows, 2 * rows), False)

    @pl.when(section == 1)
    def _():
        for group in range(GROUPS):
            fill_other(group, pl.ds(0, 3 * rows), True)
            sib_start(group)
        for group in range(GROUPS):
            fill_own(group, pl.ds(0, 3 * rows), True)

    @pl.when(section == 0)
    def _():
        x_copy(last).wait_recv()
        hold[...] = backward_norm(last)

    peer_copy(4).start()

    @pl.when(section == 0)
    def _():
        hold[...] = backward_feed(last, hold[...])

    peer_copy(5).start()

    @pl.when(section == 0)
    def _():
        backward_rest(last, hold[...])

    peer_copy(6).start()
    peer_copy(7).start()
    vec_copy.start()
    for index in range(5):
        peer_copy(index).wait_recv()
    ours(0)
    serve(0, 0)
    peer_copy(5).wait_recv()
    ours(1)
    serve(1, 0)
    peer_copy(6).wait_recv()
    peer_copy(7).wait_recv()
    ours(2)
    serve(2, 0)

    @pl.when(section == 0)
    def _():
        backward_input(last)

    for group in range(micro):
        strip_copy(group).start()
    vec_copy.wait()
    slots[0] = vec[0:8] + vec[8:16]

    def round_step(index, _):
        def each(flat, _):
            group, way = lax.div(flat, 2), lax.rem(flat, 2)
            ring(group, way, index)
            return 0

        lax.fori_loop(0, 2 * GROUPS, each, 0)

        @pl.when(index < chips)
        def _():
            @pl.when(index > 1)
            def _():
                slot_copy(index - 2).wait_recv()

            slot_copy(index - 1).start()

        return 0

    lax.fori_loop(1, 4, round_step, 0)
    finish()
    lax.fori_loop(4, 2 * chips - 1, round_step, 0)
    slot_copy(chips - 2).wait_recv()
    total = jnp.zeros((8, width), F32)
    for position in range(chips):
        total = total + slots[around(place - position)]
    vec[0:8] = total
    told = pltpu.make_async_copy(vec.at[pl.ds(0, 8)], vectors.at[pl.ds(0, 8)], in_sem.at[0])
    told.start()

    def drain(flat, _):
        group, way = lax.div(flat, 2), lax.rem(flat, 2)
        own_copy(group, way).wait()

        def each(step, _):
            rs_copy(group, way, step, rsb.at[group, way, 0]).wait_send()
            ag_copy(group, way, step, rsb.at[group, way, 0], place).wait_send()
            return 0

        lax.fori_loop(0, chips - 1, each, 0)
        whole = pltpu.make_async_remote_copy(
            src_ref=summed.at[group, way, pl.ds(0, half)], dst_ref=summed.at[group, way, pl.ds(0, half)],
            send_sem=pass_send.at[group, way], recv_sem=pass_recv.at[group, way],
            device_id=sibling, device_id_type=MESH,
        )
        whole.wait_send()
        whole.wait_recv()
        return 0

    lax.fori_loop(0, 2 * GROUPS, drain, 0)
    for group in range(GROUPS):
        for way in range(2):
            for index in range(2):
                sib_copy(group, way, index).wait_send()
    for index in range(8):
        peer_copy(index).wait_send()

    def drain_slots(step, _):
        slot_copy(step).wait_send()
        return 0

    lax.fori_loop(0, chips - 1, drain_slots, 0)

    def drain_units(unit, _):
        x_copy(unit).wait_send()
        return 0

    lax.fori_loop(0, units, drain_units, 0)
    told.wait()
    for group in range(micro):
        halo(group).wait_send()
        strip_copy(group).wait_send()
    for side in range(2):
        @pl.when(copy == side)
        def _():
            for group in range(micro):
                for part in outputs(group, side):
                    part.wait()


def widen(summed, vectors, merged, qkv, out, inner, outer, gain, shift, result, narrow, wide, held, rows, in_sem, out_sem, rest_sem):
    homes = []
    for index in range(8):
        homes.append(outer.at[0, pl.ds(index * 256, 256)])
    for column in range(4):
        for part in range(2):
            homes.append(inner.at[0, pl.ds(part * 256, 256), pl.ds(column * 512, 512)])
    for part in range(2):
        homes.append(out.at[0, pl.ds(part * 256, 256)])
    for column in range(3):
        for part in range(2):
            homes.append(qkv.at[0, pl.ds(part * 256, 256), pl.ds(column * 512, 512)])
    loads = [
        pltpu.make_async_copy(
            summed.at[index // 8, :, pl.ds(index % 8 * 256, 256)], narrow.at[index], in_sem.at[index]
        )
        for index in range(len(homes))
    ]
    stores = [
        pltpu.make_async_copy(wide.at[index], home, out_sem.at[index]) for index, home in enumerate(homes)
    ]
    firsts = [
        pltpu.make_async_copy(merged.at[pl.ds(0, held.shape[0])], held, rest_sem.at[0]),
        pltpu.make_async_copy(vectors.at[pl.ds(0, 8)], rows, rest_sem.at[1]),
    ]
    seconds = [
        pltpu.make_async_copy(held, result.at[0, :, 0], rest_sem.at[2]),
        pltpu.make_async_copy(rows.at[pl.ds(0, 2)], gain.at[0], rest_sem.at[3]),
        pltpu.make_async_copy(rows.at[pl.ds(2, 2)], shift.at[0], rest_sem.at[4]),
    ]
    for load in loads:
        load.start()
    for copy_of in firsts:
        copy_of.start()
    for index, (load, store) in enumerate(zip(loads, stores)):
        load.wait()
        for way in range(2):
            wide[index, :, way * 256 : (way + 1) * 256] = narrow[index, way].astype(F32)
        store.start()
    for copy_of in firsts:
        copy_of.wait()
    for copy_of in seconds:
        copy_of.start()
    for copy_of in stores + seconds:
        copy_of.wait()


def per_device(mesh, boundary, sentence_ids, qkv_weight, out_weight, inner_weight, outer_weight, norm_gain, norm_bias):
    micro, local, width = boundary.shape[1], boundary.shape[3], boundary.shape[4]
    inner_width = inner_weight.shape[2]
    length = sentence_ids.shape[2]
    chips = mesh.shape["copy"] * mesh.shape["dp"] // 2
    rows = (local + REACH) // 2 + REACH
    units = micro * 2
    tokens = units * rows
    any_space = pl.BlockSpec(memory_space=pl.ANY)
    vmem = pl.BlockSpec(memory_space=pltpu.VMEM)
    dma = pltpu.SemaphoreType.DMA
    hops = chips - 1
    result, summed, vectors = pl.pallas_call(
        functools.partial(kernel, units, rows, chips, width, inner_width),
        out_shape=(
            jax.ShapeDtypeStruct((4 * micro, local, width), BF16),
            jax.ShapeDtypeStruct((GROUPS, 2, 2048, 256), BF16),
            jax.ShapeDtypeStruct((2048, width), F32),
        ),
        in_specs=[any_space, vmem] + [any_space] * 4 + [vmem] * 2,
        out_specs=(any_space, any_space, any_space),
        scratch_shapes=[
            pltpu.VMEM((width, 3 * width), BF16),
            pltpu.VMEM((width, width), BF16),
            pltpu.VMEM((width, inner_width), BF16),
            pltpu.VMEM((inner_width, width), BF16),
            pltpu.VMEM((8, length), F32),
            pltpu.VMEM((length, 8), F32),
            pltpu.VMEM((2, tokens, width), BF16),
            pltpu.VMEM((2, tokens, width), BF16),
            pltpu.VMEM((tokens + 80, 3 * width), BF16),
            pltpu.VMEM((tokens, width), BF16),
            pltpu.VMEM((tokens, width), BF16),
            pltpu.VMEM((tokens, inner_width), BF16),
            pltpu.VMEM((tokens, inner_width), BF16),
            pltpu.VMEM((tokens, width), F32),
            pltpu.VMEM((tokens, width), F32),
            pltpu.VMEM((tokens, 2), F32),
            pltpu.VMEM((tokens, width), BF16),
            pltpu.VMEM((tokens, width), BF16),
            pltpu.VMEM((tokens, 3 * width), BF16),
            pltpu.VMEM((tokens, HEADS * WINDOW), BF16),
            pltpu.VMEM((tokens, width), F32),
            pltpu.VMEM((rows, WINDOW), F32),
            pltpu.VMEM((rows, width), BF16),
            pltpu.VMEM((rows, width), F32),
            pltpu.VMEM((micro, REACH, width), BF16),
            pltpu.VMEM((GROUPS, 2, 1024, 256), BF16),
            pltpu.VMEM((GROUPS, 2, 1024, 256), BF16),
            pltpu.VMEM((GROUPS, 2, hops, 1024 // chips, 256), BF16),
            pltpu.VMEM((16, width), F32),
            pltpu.VMEM((chips, 8, width), F32),
            pltpu.VMEM((rows, 1024), BF16),
            pltpu.VMEM((rows, width), BF16),
            pltpu.VMEM((rows, width), BF16),
            pltpu.VMEM((rows, width), BF16),
            pltpu.VMEM((rows, width), BF16),
            pltpu.VMEM((rows, 1024), BF16),
            pltpu.VMEM((rows, width), BF16),
            pltpu.VMEM((rows, 1024), BF16),
            dma((4,)), dma((units,)), dma((micro, 2)), dma((units,)), dma((units,)),
            dma((2 * micro,)), dma((2 * micro,)), dma((GROUPS, 2, 2)), dma((GROUPS, 2, 2)),
            dma((GROUPS, 2, hops)), dma((GROUPS, 2, hops)), dma((GROUPS, 2, hops)), dma((GROUPS, 2, hops)),
            dma((chips + 1,)), dma((chips + 1,)), dma((GROUPS, 2)), dma((GROUPS, 2)), dma((GROUPS, 2)),
            dma((8,)), dma((8,)),
        ],
        compiler_params=pltpu.CompilerParams(
            collective_id=0, has_side_effects=True, vmem_limit_bytes=63 * 1024 * 1024
        ),
    )(boundary, sentence_ids, qkv_weight, out_weight, inner_weight, outer_weight, norm_gain, norm_bias)

    blocks = 8 * GROUPS
    hbm = pl.BlockSpec(memory_space=pltpu.HBM)
    grad_qkv, grad_out, grad_inner, grad_outer, grad_gain, grad_bias, result = pl.pallas_call(
        widen,
        out_shape=tuple(
            jax.ShapeDtypeStruct(item.shape, F32)
            for item in (qkv_weight, out_weight, inner_weight, outer_weight, norm_gain, norm_bias)
        )
        + (jax.ShapeDtypeStruct(boundary.shape, BF16),),
        in_specs=[hbm] * 3,
        out_specs=(hbm,) * 7,
        scratch_shapes=[
            pltpu.VMEM((blocks, 2, 256, 256), BF16), pltpu.VMEM((blocks, 256, 512), F32),
            pltpu.VMEM((micro, local, width), BF16), pltpu.VMEM((8, width), F32), dma((blocks,)), dma((blocks,)), dma((5,)),
        ],
        compiler_params=pltpu.CompilerParams(vmem_limit_bytes=62 * 1024 * 1024),
    )(summed, vectors, result)
    return (result, grad_qkv, grad_out, grad_inner, grad_outer, grad_gain, grad_bias)


def solution(mesh):
    weight = P("section", None, None)
    edge = P("section", None, "dp", "copy", None)
    return jax.shard_map(
        functools.partial(per_device, mesh),
        mesh=mesh,
        in_specs=(edge, P(None, "dp", None)) + (weight,) * 6,
        out_specs=(edge,) + (weight,) * 6,
        check_vma=False,
    )
```

```python
import functools

import jax
import jax.numpy as jnp
from jax import lax
from jax.experimental import pallas as pl
from jax.experimental.pallas import tpu as pltpu
from jax.sharding import PartitionSpec as P

HEADS = 8
REACH = 32
WINDOW = 256
NEG = -1e30
EPS = 1e-05
GROUPS = 3
BLOCKS = ((0, 192, 0), (192, 112, 128))
MESH = pl.DeviceIdType.MESH
F32 = jnp.float32
BF16 = jnp.bfloat16


def mul(left, right):
    return jnp.dot(left, right, preferred_element_type=F32)


def against(left, right):
    return lax.dot_general(left, right, (((1,), (1,)), ((), ())), preferred_element_type=F32)


def contract(left, right):
    return lax.dot_general(left, right, (((0,), (0,)), ((), ())), preferred_element_type=F32)


def gelu(x):
    phi = 0.5 + 0.5 * lax.erf(x * 0.7071067811865476)
    bell = jnp.exp2(x * x * -0.7213475204444817)
    return (x * phi).astype(BF16), (phi + x * 0.3989422804014327 * bell).astype(BF16)


def normalize(resid):
    center = resid - jnp.mean(resid, axis=-1, keepdims=True)
    spread = jnp.mean(center * center, axis=-1, keepdims=True)
    inverse = lax.rsqrt(spread + EPS)
    return center * inverse, inverse


def normalize_back(upstream, scaled, inverse, gain):
    tilted = upstream * gain
    first = jnp.mean(tilted, axis=-1, keepdims=True)
    second = jnp.mean(tilted * scaled, axis=-1, keepdims=True)
    return inverse * (tilted - first - scaled * second)


def halves(pair):
    lane = lax.broadcasted_iota(jnp.int32, pair.shape, 1)
    zero = jnp.zeros_like(pair)
    return jnp.where(lane < 64, pair, zero), jnp.where(lane < 64, zero, pair)


def kernel(
    units, rows, chips, width, inner_width,
    boundary, ids, qkv_weight, out_weight, inner_weight, outer_weight, gain_rows, shift_rows,
    result, summed, vectors,
    w_qkv, w_out, w_in, w_outer, info, column,
    xb, ob, mixed, att, nlow, act, dg, one, two, inv, goi, gai, gmix, probs, scale,
    bias, gatt, hold, strip, mine, sib, rsb, vec, slots,
    peer_act, peer_nlow, peer_att, peer_in, peer_goi, peer_dg, peer_gai, peer_gmix,
    weight_sem, in_sem, out_sem, x_send, x_recv, y_send, y_recv, sib_send, sib_recv, rs_send, rs_recv,
    ag_send, ag_recv, slot_send, slot_recv, pass_send, pass_recv, own_sem, peer_send, peer_recv,
):
    blocks = BLOCKS
    micro, local = boundary.shape[1], boundary.shape[3]
    length = ids.shape[2]
    reach = local + REACH
    shift = reach - rows
    section, copy, dp = lax.axis_index("section"), lax.axis_index("copy"), lax.axis_index("dp")
    core, layer = lax.rem(dp, 2), lax.div(dp, 2)
    line = chips // 2
    place = jnp.where(copy == 0, layer, chips - 1 - layer)
    gains, shifts = gain_rows.at[0], shift_rows.at[0]

    def either(first, second):
        return jnp.where(copy == 0, first, second)

    def at(position):
        far = position >= line
        return (section, jnp.where(far, 1, 0), 2 * jnp.where(far, chips - 1 - position, position) + core)

    def around(position):
        return lax.rem(position + 2 * chips, chips)

    across = (1 - section, copy, dp)
    beside = (section, 1 - copy, dp)
    sibling = (section, copy, dp + 1 - 2 * core)
    ahead, behind = at(around(place + 1)), at(around(place - 1))

    def load(unit):
        group, odd = unit // 2, unit % 2
        if odd:
            source, target, size = either(shift, 0), either(0, REACH), rows - REACH
        else:
            source, target, size = either(0, local - rows), 0, rows
        return pltpu.make_async_copy(
            boundary.at[0, group, 0, pl.ds(pl.multiple_of(source, 16), size)],
            xb.at[0, pl.ds(pl.multiple_of(unit * rows + target, 16), size)], in_sem.at[unit],
        )

    def halo(group):
        source, target = either(local - REACH, 0), (2 * group + 1) * rows + either(0, rows - REACH)
        return pltpu.make_async_remote_copy(
            src_ref=boundary.at[0, group, 0, pl.ds(pl.multiple_of(source, 16), REACH)],
            dst_ref=xb.at[0, pl.ds(pl.multiple_of(target, 16), REACH)],
            send_sem=y_send.at[group], recv_sem=y_recv.at[group],
            device_id=beside, device_id_type=MESH,
        )

    weights = [
        pltpu.make_async_copy(source.at[0], target, weight_sem.at[index])
        for index, (source, target) in enumerate(
            ((qkv_weight, w_qkv), (out_weight, w_out), (inner_weight, w_in), (outer_weight, w_outer))
        )
    ]
    load(0).start()
    for weight in weights:
        weight.start()
    for unit in range(1, units):
        load(unit).start()
    vec[...] = jnp.zeros_like(vec)
    for unit in range(units):
        mixed[(unit + 1) * rows : (unit + 1) * rows + 80] = jnp.zeros((80, 3 * width), BF16)
    barrier = pltpu.get_barrier_semaphore()
    for other in (across, beside, sibling, ahead, behind):
        pl.semaphore_signal(barrier, inc=1, device_id=other, device_id_type=MESH)

    spot = lax.broadcasted_iota(jnp.int32, (micro, length), 1)
    sentence = ids[:, 0, :]
    cuts = (reach // 2, local, length - reach // 2)
    owner = jnp.zeros((micro, length), jnp.int32)
    for cut in cuts:
        owner = owner + jnp.where(spot >= cut, 1, 0)
    for index, cut in enumerate(cuts):
        crossing = sentence == sentence[:, cut - 1 : cut]
        left = jnp.sum(jnp.where(crossing & (spot < cut), 1.0, 0.0), axis=1, keepdims=True)
        right = jnp.sum(jnp.where(crossing & (spot >= cut), 1.0, 0.0), axis=1, keepdims=True)
        side = jnp.where(left >= right, index, index + 1)
        owner = jnp.where(crossing, side, owner)
    info[...] = jnp.zeros_like(info)
    info[0:micro] = sentence.astype(F32)
    info[micro : 2 * micro] = owner.astype(F32)
    column[...] = info[...].T

    def piece_of(unit):
        odd = lax.rem(unit, 2)
        return either(odd, 1 - odd)

    def begin_of(unit):
        return copy * (local - REACH) + piece_of(unit) * shift

    def pick(unit, first, size, kind):
        spots = pl.ds(pl.multiple_of(begin_of(unit) + first, 16), size)
        both = column[spots, kind * micro : (kind + 1) * micro]
        return jnp.where(unit < 2, both[:, 0:1], both[:, 1:2])

    def owned(unit, first, size):
        return pick(unit, first, size, 1) == (2 * copy + piece_of(unit)).astype(F32)

    load(0).wait()
    weights[0].wait()

    def unit_rows(unit):
        return pl.ds(pl.multiple_of(unit * rows, 16), rows)

    def x_copy(unit):
        span = unit_rows(unit)
        return pltpu.make_async_remote_copy(
            src_ref=ob.at[0, span], dst_ref=xb.at[1, span], send_sem=x_send.at[unit],
            recv_sem=x_recv.at[unit], device_id=across, device_id_type=MESH,
        )

    def forward(unit, slot):
        span = unit_rows(unit)
        start = pl.multiple_of(unit * rows, 16)
        hidden = xb[section, span]
        mixed[span, 0:width] = (mul(hidden, w_qkv[:, 0:width]) * 0.125).astype(BF16)
        mixed[span, width:] = mul(hidden, w_qkv[:, width:]).astype(BF16)
        for index, (first, size, begin) in enumerate(blocks):
            turned = pltpu.roll(info[...], length - begin_of(unit) - begin, 1)[0:micro, 0:WINDOW]
            near_ids = jnp.where(unit < 2, turned[0:1], turned[1:2])
            inside = lax.broadcasted_iota(jnp.int32, near_ids.shape, 1) < rows - begin
            near_ids = jnp.where(inside, near_ids, -1.0)
            allowed = pick(unit, first, size, 0) == near_ids
            bias[first : first + size] = jnp.where(allowed, 0.0, NEG)

        def pair_step(pair, _):
            lanes = pl.multiple_of(pair * 128, 128)
            for first, size, begin in blocks:
                near = pl.ds(pl.multiple_of(start + begin, 16), WINDOW)
                own = pl.ds(pl.multiple_of(start + first, 16), size)
                query = jnp.concatenate(halves(mixed[own, pl.ds(lanes, 128)]), axis=0)
                key = mixed[near, pl.ds(pl.multiple_of(width + pair * 128, 128), 128)]
                value = mixed[near, pl.ds(pl.multiple_of(2 * width + pair * 128, 128), 128)]
                barred = bias[first : first + size]
                scores = against(query, key) + jnp.concatenate([barred, barred], axis=0)
                share = jnp.exp(scores - jnp.max(scores, axis=-1, keepdims=True)).astype(BF16)
                for head in range(2):
                    cols = pl.ds(pl.multiple_of(pair * 512 + head * 256, 256), 256)
                    probs[own, cols] = share[head * size : (head + 1) * size]
                sums = mul(share, jnp.concatenate([value, jnp.ones((WINDOW, 128), BF16)], axis=1))
                lane = lax.broadcasted_iota(jnp.int32, (size, 128), 1)
                inverse = 1.0 / jnp.where(lane < 64, sums[:size, 128:], sums[size:, 128:])
                attended = jnp.where(lane < 64, sums[:size, :128], sums[size:, :128])
                att[own, pl.ds(lanes, 128)] = (attended * inverse).astype(BF16)
                scale[own, pl.ds(lanes, 128)] = inverse
            return 0

        lax.fori_loop(0, width // 128, pair_step, 0, unroll=True)
        @pl.when(slot == 0)
        def _():
            for weight in weights[1:]:
                weight.wait()
            for odd in range(1, units):
                load(odd).wait()
            pl.semaphore_wait(barrier, 5)
            for group in range(micro):
                halo(group).start()

        scaled, inverse = normalize(xb[section, span].astype(F32) + mul(att[span], w_out[...]))
        one[span] = scaled
        inv[span, 0:1] = inverse
        normed = scaled * gains[0:1] + shifts[0:1]
        hold[...] = normed
        low = normed.astype(BF16)
        nlow[span] = low
        tile = 256
        count = inner_width // tile
        inner = mul(nlow[span], w_in[:, 0:tile])
        outer = hold[...]
        for step in range(count):
            ahead_inner = None
            if step + 1 < count:
                ahead_inner = mul(nlow[span], w_in[:, (step + 1) * tile : (step + 2) * tile])
            cols = pl.ds(step * tile, tile)
            active, slope = gelu(inner)
            act[span, cols] = active
            dg[span, cols] = slope
            outer = outer + mul(active, w_outer[cols])
            inner = ahead_inner
        scaled, inverse = normalize(outer)
        two[span] = scaled
        inv[span, 1:2] = inverse
        ob[section, span] = (scaled * gains[1:2] + shifts[1:2]).astype(BF16)

    def backward_norm(unit):
        span = unit_rows(unit)
        upstream = jnp.where(owned(unit, 0, rows), xb[1 - section, span].astype(F32), 0.0)
        scaled = two[span]
        vec[1:2] += jnp.sum(upstream * scaled, axis=0, keepdims=True)
        vec[3:4] += jnp.sum(upstream, axis=0, keepdims=True)
        grad_two = normalize_back(upstream, scaled, inv[span, 1:2], gains[1:2])
        goi[span] = grad_two.astype(BF16)
        return grad_two

    def backward_feed(unit, grad_two):
        span = unit_rows(unit)
        tile = 512
        count = inner_width // tile
        grad_active = against(goi[span], w_outer[0:tile])
        total = grad_two
        for step in range(count):
            next_active = None
            if step + 1 < count:
                next_active = against(goi[span], w_outer[(step + 1) * tile : (step + 2) * tile])
            cols = pl.ds(step * tile, tile)
            grad_inner = (grad_active * dg[span, cols].astype(F32)).astype(BF16)
            dg[span, cols] = grad_inner
            total = total + against(grad_inner, w_in[:, step * tile : (step + 1) * tile])
            grad_active = next_active
        return total

    def backward_rest(unit, total):
        span = unit_rows(unit)
        start = pl.multiple_of(unit * rows, 16)
        scaled = one[span]
        vec[0:1] += jnp.sum(total * scaled, axis=0, keepdims=True)
        vec[2:3] += jnp.sum(total, axis=0, keepdims=True)
        grad_one = normalize_back(total, scaled, inv[span, 0:1], gains[0:1])
        hold[...] = grad_one
        low = grad_one.astype(BF16)
        gai[span] = low
        gatt[...] = (against(low, w_out[...]) * scale[span]).astype(BF16)

        def pair_step(pair, _):
            lanes = pl.multiple_of(pair * 128, 128)
            key_lanes = pl.ds(pl.multiple_of(width + pair * 128, 128), 128)
            value_lanes = pl.ds(pl.multiple_of(2 * width + pair * 128, 128), 128)
            parts = ([], [])
            for first, size, begin in blocks:
                near = pl.ds(pl.multiple_of(start + begin, 16), WINDOW)
                own = pl.ds(pl.multiple_of(start + first, 16), size)
                query = jnp.concatenate(halves(mixed[own, pl.ds(lanes, 128)]), axis=0)
                key = mixed[near, key_lanes]
                value = mixed[near, value_lanes]
                grad_pair = gatt[first : first + size, pl.ds(lanes, 128)]
                grad = jnp.concatenate(halves(grad_pair), axis=0)
                inverse = scale[own, pl.ds(lanes, 128)]
                inverse = jnp.concatenate([inverse[:, 0:1], inverse[:, 64:65]], axis=0)
                share = jnp.concatenate(
                    [probs[own, pl.ds(pl.multiple_of(pair * 512 + head * 256, 256), 256)] for head in range(2)],
                    axis=0,
                )
                tilt = against(grad, value)
                held_share = share.astype(F32)
                rowwise = jnp.sum(held_share * tilt, axis=-1, keepdims=True) * inverse
                grads = (held_share * (tilt - rowwise)).astype(BF16)
                wide = mul(grads, key)
                lane = lax.broadcasted_iota(jnp.int32, (size, 128), 1)
                grad_query = jnp.where(lane < 64, wide[:size], wide[size:])
                gmix[own, pl.ds(lanes, 128)] = (grad_query * 0.125).astype(BF16)
                for kind, (small, sides) in enumerate(((mixed[own, pl.ds(lanes, 128)], grads), (grad_pair, share))):
                    turned = small.T
                    heads = [
                        mul(turned[head * 64 : (head + 1) * 64], sides[head * size : (head + 1) * size])
                        for head in range(2)
                    ]
                    parts[kind].append(jnp.concatenate(heads, axis=0))
            for kind, home in enumerate((key_lanes, value_lanes)):
                low, high = parts[kind]
                middle = low[:, 128:] + high[:, :128]
                whole = jnp.concatenate([low[:, :128], middle, high[:, 128:]], axis=1)
                gmix[span, home] = whole.astype(BF16).T[0:rows]
            return 0

        lax.fori_loop(0, width // 128, pair_step, 0, unroll=True)

    def backward_input(unit):
        span = unit_rows(unit)
        ob[1 - section, span] = (hold[...] + against(gmix[span], w_qkv[...])).astype(BF16)

    def backward(unit):
        backward_rest(unit, backward_feed(unit, backward_norm(unit)))
        backward_input(unit)

    half = 1024
    seg = half // chips

    def spare(group, way, index):
        tile = way * 2 + index
        if group == 2:
            return mixed.at[pl.ds(0, 512), pl.ds(tile * 256, 256)]
        return probs.at[pl.ds(0, 512), pl.ds((group * 4 + tile) * 256, 256)]

    def sib_copy(group, way, index):
        return pltpu.make_async_remote_copy(
            src_ref=spare(group, way, index), dst_ref=sib.at[group, way, pl.ds(index * 512, 512)],
            send_sem=sib_send.at[group, way, index], recv_sem=sib_recv.at[group, way, index],
            device_id=sibling, device_id_type=MESH,
        )

    def block_of(group, block, span):
        cols = pl.ds(pl.multiple_of(block * 512, 512), 512)
        if group == 0:
            return contract(act[span, cols], goi[span])
        if group == 1:
            return contract(nlow[span], dg[span, cols])
        cols = pl.ds(pl.multiple_of(jnp.maximum(block - 1, 0) * 512, 512), 512)
        left = jnp.where(block == 0, att[span], xb[section, span])
        return contract(left, jnp.where(block == 0, gai[span], gmix[span, cols]))

    def both(own, peer):
        return jnp.concatenate([own, peer], axis=0)

    def last_block(group, index):
        span = pl.ds((units - 1) * rows, rows)
        block = core * 2 + index
        cols = pl.ds(pl.multiple_of(block * 512, 512), 512)
        here = slice(index * 512, (index + 1) * 512)
        if group == 0:
            return contract(both(act[span, cols], peer_act[:, here]), both(goi[span], peer_goi[...]))
        if group == 1:
            return contract(both(nlow[span], peer_nlow[...]), both(dg[span, cols], peer_dg[:, here]))
        cols = pl.ds(pl.multiple_of(jnp.maximum(block - 1, 0) * 512, 512), 512)
        first = block == 0
        peer_cols = pl.ds(pl.multiple_of(jnp.where(first, 0, (core + index - 1) * 512), 512), 512)
        left = jnp.where(first, both(att[span], peer_att[...]), both(xb[section, span], peer_in[...]))
        right = jnp.where(first, both(gai[span], peer_gai[...]), both(gmix[span, cols], peer_gmix[:, peer_cols]))
        return contract(left, right)

    def peer_copy(index):
        span = pl.ds((units - 1) * rows, rows)
        wide = pl.ds(pl.multiple_of((1 - core) * 1024, 512), 1024)
        near = pl.ds(pl.multiple_of((1 - core) * 512, 512), 1024)
        source, target = (
            (act.at[span, wide], peer_act), (nlow.at[span], peer_nlow), (att.at[span], peer_att),
            (xb.at[section, span], peer_in), (goi.at[span], peer_goi), (dg.at[span, wide], peer_dg),
            (gai.at[span], peer_gai), (gmix.at[span, near], peer_gmix),
        )[index]
        return pltpu.make_async_remote_copy(
            src_ref=source, dst_ref=target, send_sem=peer_send.at[index], recv_sem=peer_recv.at[index],
            device_id=sibling, device_id_type=MESH,
        )

    def put(room, part, first):
        room[...] = (part if first else part + room[...].astype(F32)).astype(BF16)

    def fill_own(group, span, first):
        for index in range(2):
            value = block_of(group, core * 2 + index, span)
            for way in range(2):
                room = mine.at[group, way, pl.ds(index * 512, 512)]
                put(room, value[:, way * 256 : (way + 1) * 256], first)

    def fill_other(group, span, first):
        for index in range(2):
            value = block_of(group, (1 - core) * 2 + index, span)
            for way in range(2):
                put(spare(group, way, index), value[:, way * 256 : (way + 1) * 256], first)

    def sib_start(group):
        for way in range(2):
            for index in range(2):
                sib_copy(group, way, index).start()

    def slot_step(slot, _):
        is_forward = jnp.where(section == 0, slot < units, lax.rem(slot, 2) == 0)
        unit = jnp.where(section == 0, lax.rem(slot, units), lax.div(slot, 2))

        first_use = jnp.where(section == 0, is_forward, jnp.logical_not(is_forward))

        @pl.when(jnp.logical_and(first_use, lax.rem(unit, 2) == 1))
        def _():
            halo(lax.div(unit, 2)).wait_recv()

        @pl.when(is_forward)
        def _():
            @pl.when(section == 1)
            def _():
                x_copy(unit).wait_recv()

            forward(unit, slot)

            @pl.when(section == 0)
            def _():
                x_copy(unit).start()

        held = jnp.logical_and(section == 0, slot == 2 * units - 1)

        @pl.when(jnp.logical_not(jnp.logical_or(is_forward, held)))
        def _():
            @pl.when(section == 0)
            def _():
                x_copy(unit).wait_recv()

            backward(unit)

            @pl.when(section == 1)
            def _():
                x_copy(unit).start()

            @pl.when(jnp.logical_and(section == 0, unit == 0))
            def _():
                for group in range(GROUPS):
                    fill_own(group, pl.ds(0, rows), True)

            @pl.when(jnp.logical_and(section == 0, unit == 1))
            def _():
                for group in range(GROUPS):
                    fill_other(group, pl.ds(0, 2 * rows), True)

            return None

        @pl.when(jnp.logical_and(is_forward, unit == units - 1))
        def _():
            for index in range(4):
                peer_copy(index).start()

        return 0

    lax.fori_loop(0, 2 * units, slot_step, 0)

    def strip_copy(group):
        source = (2 * group + 1) * rows + either(rows - REACH, 0)
        return pltpu.make_async_remote_copy(
            src_ref=ob.at[1, pl.ds(pl.multiple_of(source, 16), REACH)], dst_ref=strip.at[group],
            send_sem=y_send.at[micro + group], recv_sem=y_recv.at[micro + group],
            device_id=beside, device_id_type=MESH,
        )

    def outputs(group, side):
        even, odd = 2 * group * rows, (2 * group + 1) * rows
        if side == 0:
            parts = ((even, 0, shift), (odd, shift, local - shift))
        else:
            parts = ((odd + REACH, 0, shift - REACH), (even, shift - REACH, rows))
        return [
            pltpu.make_async_copy(
                ob.at[1, pl.ds(source, size)], result.at[group, pl.ds(target, size)],
                out_sem.at[group, index],
            )
            for index, (source, target, size) in enumerate(parts)
        ]

    def finish():
        for group in range(micro):
            low_unit, high_unit = 2 * group + copy, 2 * group + 1 - copy
            over = rows - shift
            kept = pl.ds(pl.multiple_of(low_unit * rows + shift, 16), over)
            moved = pl.ds(pl.multiple_of(high_unit * rows, 16), over)
            ob[1, moved] = jnp.where(owned(low_unit, shift, over), ob[1, kept], ob[1, moved])
            strip_copy(group).wait_recv()
            odd_unit = 2 * group + 1
            first = either(shift, REACH)
            edge = pl.ds(pl.multiple_of(odd_unit * rows + first, 16), REACH)
            ob[1, edge] = jnp.where(owned(odd_unit, first, REACH), ob[1, edge], strip[group])
        for side in range(2):
            @pl.when(copy == side)
            def _():
                for group in range(micro):
                    for part in outputs(group, side):
                        part.start()

    def ours(group):
        for index in range(2):
            value = last_block(group, index)
            span = slice(index * 512, (index + 1) * 512)
            for way in range(2):
                sib_copy(group, way, index).wait_recv()
                part = value[:, way * 256 : (way + 1) * 256]
                total = part + mine[group, way, span].astype(F32) + sib[group, way, span].astype(F32)
                mine[group, way, span] = total.astype(BF16)

    def segment(position):
        return pl.ds(pl.multiple_of(around(position) * seg, 16), seg)

    def target(way):
        return tuple(jnp.where(way == 0, a, b) for a, b in zip(ahead, behind))

    def rs_copy(group, way, step, source):
        return pltpu.make_async_remote_copy(
            src_ref=source, dst_ref=rsb.at[group, way, step], send_sem=rs_send.at[group, way, step],
            recv_sem=rs_recv.at[group, way, step], device_id=target(way), device_id_type=MESH,
        )

    def final_rows(position):
        return pl.ds(pl.multiple_of(core * half + around(position) * seg, 16), seg)

    def ag_copy(group, way, step, source, position):
        return pltpu.make_async_remote_copy(
            src_ref=source, dst_ref=summed.at[group, way, final_rows(position)],
            send_sem=ag_send.at[group, way, step], recv_sem=ag_recv.at[group, way, step],
            device_id=target(way), device_id_type=MESH,
        )

    def pass_copy(group, way, source, position):
        return pltpu.make_async_remote_copy(
            src_ref=source, dst_ref=summed.at[group, way, final_rows(position)],
            send_sem=pass_send.at[group, way], recv_sem=pass_recv.at[group, way],
            device_id=sibling, device_id_type=MESH,
        )

    def own_copy(group, way):
        sign = 1 - 2 * way
        return pltpu.make_async_copy(
            rsb.at[group, way, chips - 2], summed.at[group, way, final_rows(place + sign)],
            own_sem.at[group, way],
        )

    def ring(group, way, step):
        sign = 1 - 2 * way

        @pl.when(step == 0)
        def _():
            rs_copy(group, way, 0, mine.at[group, way, segment(place)]).start()

        @pl.when(jnp.logical_and(step >= 1, step < chips))
        def _():
            last = step - 1
            slot = rsb.at[group, way, last]
            rs_copy(group, way, last, slot).wait_recv()
            part = mine[group, way, segment(place - sign * step)]
            rsb[group, way, last] = (rsb[group, way, last].astype(F32) + part.astype(F32)).astype(BF16)

            @pl.when(step < chips - 1)
            def _():
                rs_copy(group, way, step, slot).start()

            @pl.when(step == chips - 1)
            def _():
                ag_copy(group, way, 0, slot, place + sign).start()
                pass_copy(group, way, slot, place + sign).start()
                own_copy(group, way).start()

        @pl.when(jnp.logical_and(step >= chips, step < 2 * chips - 1))
        def _():
            last = step - chips
            position = place - sign * last
            arrived = summed.at[group, way, final_rows(position)]
            ag_copy(group, way, last, arrived, position).wait_recv()

            @pl.when(last + 1 < chips - 1)
            def _():
                ag_copy(group, way, last + 1, arrived, position).start()

            pass_copy(group, way, arrived, position).start()

    def slot_copy(step):
        return pltpu.make_async_remote_copy(
            src_ref=slots.at[step], dst_ref=slots.at[step + 1], send_sem=slot_send.at[step],
            recv_sem=slot_recv.at[step], device_id=ahead, device_id_type=MESH,
        )

    vec_copy = pltpu.make_async_remote_copy(
        src_ref=vec.at[pl.ds(0, 8)], dst_ref=vec.at[pl.ds(8, 8)], send_sem=slot_send.at[chips],
        recv_sem=slot_recv.at[chips], device_id=sibling, device_id_type=MESH,
    )
    def serve(group, step):
        def each(way, _):
            ring(group, way, step)
            return 0

        lax.fori_loop(0, 2, each, 0)

    last = units - 1
    @pl.when(section == 0)
    def _():
        for group in range(GROUPS):
            fill_other(group, pl.ds(2 * rows, rows), False)
            sib_start(group)
        for group in range(GROUPS):
            fill_own(group, pl.ds(rows, 2 * rows), False)

    @pl.when(section == 1)
    def _():
        for group in range(GROUPS):
            fill_other(group, pl.ds(0, 3 * rows), True)
            sib_start(group)
        for group in range(GROUPS):
            fill_own(group, pl.ds(0, 3 * rows), True)

    @pl.when(section == 0)
    def _():
        x_copy(last).wait_recv()
        hold[...] = backward_norm(last)

    peer_copy(4).start()

    @pl.when(section == 0)
    def _():
        hold[...] = backward_feed(last, hold[...])

    peer_copy(5).start()

    @pl.when(section == 0)
    def _():
        backward_rest(last, hold[...])

    peer_copy(6).start()
    peer_copy(7).start()
    vec_copy.start()
    for index in range(5):
        peer_copy(index).wait_recv()
    ours(0)
    serve(0, 0)
    peer_copy(5).wait_recv()
    ours(1)
    serve(1, 0)
    peer_copy(6).wait_recv()
    peer_copy(7).wait_recv()
    ours(2)
    serve(2, 0)

    @pl.when(section == 0)
    def _():
        backward_input(last)

    for group in range(micro):
        strip_copy(group).start()
    vec_copy.wait()
    slots[0] = vec[0:8] + vec[8:16]

    def round_step(index, _):
        def each(flat, _):
            group, way = lax.div(flat, 2), lax.rem(flat, 2)
            ring(group, way, index)
            return 0

        lax.fori_loop(0, 2 * GROUPS, each, 0)

        @pl.when(index < chips)
        def _():
            @pl.when(index > 1)
            def _():
                slot_copy(index - 2).wait_recv()

            slot_copy(index - 1).start()

        return 0

    lax.fori_loop(1, 4, round_step, 0)
    finish()
    lax.fori_loop(4, 2 * chips - 1, round_step, 0)
    slot_copy(chips - 2).wait_recv()
    total = jnp.zeros((8, width), F32)
    for position in range(chips):
        total = total + slots[around(place - position)]
    vec[0:8] = total
    told = pltpu.make_async_copy(vec.at[pl.ds(0, 8)], vectors.at[pl.ds(0, 8)], in_sem.at[0])
    told.start()

    def drain(flat, _):
        group, way = lax.div(flat, 2), lax.rem(flat, 2)
        own_copy(group, way).wait()

        def each(step, _):
            rs_copy(group, way, step, rsb.at[group, way, 0]).wait_send()
            ag_copy(group, way, step, rsb.at[group, way, 0], place).wait_send()
            return 0

        lax.fori_loop(0, chips - 1, each, 0)
        whole = pltpu.make_async_remote_copy(
            src_ref=summed.at[group, way, pl.ds(0, half)], dst_ref=summed.at[group, way, pl.ds(0, half)],
            send_sem=pass_send.at[group, way], recv_sem=pass_recv.at[group, way],
            device_id=sibling, device_id_type=MESH,
        )
        whole.wait_send()
        whole.wait_recv()
        return 0

    lax.fori_loop(0, 2 * GROUPS, drain, 0)
    for group in range(GROUPS):
        for way in range(2):
            for index in range(2):
                sib_copy(group, way, index).wait_send()
    for index in range(8):
        peer_copy(index).wait_send()

    def drain_slots(step, _):
        slot_copy(step).wait_send()
        return 0

    lax.fori_loop(0, chips - 1, drain_slots, 0)

    def drain_units(unit, _):
        x_copy(unit).wait_send()
        return 0

    lax.fori_loop(0, units, drain_units, 0)
    told.wait()
    for group in range(micro):
        halo(group).wait_send()
        strip_copy(group).wait_send()
    for side in range(2):
        @pl.when(copy == side)
        def _():
            for group in range(micro):
                for part in outputs(group, side):
                    part.wait()


def widen(summed, vectors, merged, qkv, out, inner, outer, gain, shift, result, narrow, wide, held, rows, in_sem, out_sem, rest_sem):
    homes = []
    for index in range(8):
        homes.append(outer.at[0, pl.ds(index * 256, 256)])
    for column in range(4):
        for part in range(2):
            homes.append(inner.at[0, pl.ds(part * 256, 256), pl.ds(column * 512, 512)])
    for part in range(2):
        homes.append(out.at[0, pl.ds(part * 256, 256)])
    for column in range(3):
        for part in range(2):
            homes.append(qkv.at[0, pl.ds(part * 256, 256), pl.ds(column * 512, 512)])
    loads = [
        pltpu.make_async_copy(
            summed.at[index // 8, :, pl.ds(index % 8 * 256, 256)], narrow.at[index], in_sem.at[index]
        )
        for index in range(len(homes))
    ]
    stores = [
        pltpu.make_async_copy(wide.at[index], home, out_sem.at[index]) for index, home in enumerate(homes)
    ]
    firsts = [
        pltpu.make_async_copy(merged.at[pl.ds(0, held.shape[0])], held, rest_sem.at[0]),
        pltpu.make_async_copy(vectors.at[pl.ds(0, 8)], rows, rest_sem.at[1]),
    ]
    seconds = [
        pltpu.make_async_copy(held, result.at[0, :, 0], rest_sem.at[2]),
        pltpu.make_async_copy(rows.at[pl.ds(0, 2)], gain.at[0], rest_sem.at[3]),
        pltpu.make_async_copy(rows.at[pl.ds(2, 2)], shift.at[0], rest_sem.at[4]),
    ]
    for load in loads:
        load.start()
    for copy_of in firsts:
        copy_of.start()
    for index, (load, store) in enumerate(zip(loads, stores)):
        load.wait()
        for way in range(2):
            wide[index, :, way * 256 : (way + 1) * 256] = narrow[index, way].astype(F32)
        store.start()
    for copy_of in firsts:
        copy_of.wait()
    for copy_of in seconds:
        copy_of.start()
    for copy_of in stores + seconds:
        copy_of.wait()


def per_device(mesh, boundary, sentence_ids, qkv_weight, out_weight, inner_weight, outer_weight, norm_gain, norm_bias):
    micro, local, width = boundary.shape[1], boundary.shape[3], boundary.shape[4]
    inner_width = inner_weight.shape[2]
    length = sentence_ids.shape[2]
    chips = mesh.shape["copy"] * mesh.shape["dp"] // 2
    rows = (local + REACH) // 2 + REACH
    units = micro * 2
    tokens = units * rows
    any_space = pl.BlockSpec(memory_space=pl.ANY)
    vmem = pl.BlockSpec(memory_space=pltpu.VMEM)
    dma = pltpu.SemaphoreType.DMA
    hops = chips - 1
    result, summed, vectors = pl.pallas_call(
        functools.partial(kernel, units, rows, chips, width, inner_width),
        out_shape=(
            jax.ShapeDtypeStruct((4 * micro, local, width), BF16),
            jax.ShapeDtypeStruct((GROUPS, 2, 2048, 256), BF16),
            jax.ShapeDtypeStruct((2048, width), F32),
        ),
        in_specs=[any_space, vmem] + [any_space] * 4 + [vmem] * 2,
        out_specs=(any_space, any_space, any_space),
        scratch_shapes=[
            pltpu.VMEM((width, 3 * width), BF16),
            pltpu.VMEM((width, width), BF16),
            pltpu.VMEM((width, inner_width), BF16),
            pltpu.VMEM((inner_width, width), BF16),
            pltpu.VMEM((8, length), F32),
            pltpu.VMEM((length, 8), F32),
            pltpu.VMEM((2, tokens, width), BF16),
            pltpu.VMEM((2, tokens, width), BF16),
            pltpu.VMEM((tokens + 80, 3 * width), BF16),
            pltpu.VMEM((tokens, width), BF16),
            pltpu.VMEM((tokens, width), BF16),
            pltpu.VMEM((tokens, inner_width), BF16),
            pltpu.VMEM((tokens, inner_width), BF16),
            pltpu.VMEM((tokens, width), F32),
            pltpu.VMEM((tokens, width), F32),
            pltpu.VMEM((tokens, 2), F32),
            pltpu.VMEM((tokens, width), BF16),
            pltpu.VMEM((tokens, width), BF16),
            pltpu.VMEM((tokens, 3 * width), BF16),
            pltpu.VMEM((tokens, HEADS * WINDOW), BF16),
            pltpu.VMEM((tokens, width), F32),
            pltpu.VMEM((rows, WINDOW), F32),
            pltpu.VMEM((rows, width), BF16),
            pltpu.VMEM((rows, width), F32),
            pltpu.VMEM((micro, REACH, width), BF16),
            pltpu.VMEM((GROUPS, 2, 1024, 256), BF16),
            pltpu.VMEM((GROUPS, 2, 1024, 256), BF16),
            pltpu.VMEM((GROUPS, 2, hops, 1024 // chips, 256), BF16),
            pltpu.VMEM((16, width), F32),
            pltpu.VMEM((chips, 8, width), F32),
            pltpu.VMEM((rows, 1024), BF16),
            pltpu.VMEM((rows, width), BF16),
            pltpu.VMEM((rows, width), BF16),
            pltpu.VMEM((rows, width), BF16),
            pltpu.VMEM((rows, width), BF16),
            pltpu.VMEM((rows, 1024), BF16),
            pltpu.VMEM((rows, width), BF16),
            pltpu.VMEM((rows, 1024), BF16),
            dma((4,)), dma((units,)), dma((micro, 2)), dma((units,)), dma((units,)),
            dma((2 * micro,)), dma((2 * micro,)), dma((GROUPS, 2, 2)), dma((GROUPS, 2, 2)),
            dma((GROUPS, 2, hops)), dma((GROUPS, 2, hops)), dma((GROUPS, 2, hops)), dma((GROUPS, 2, hops)),
            dma((chips + 1,)), dma((chips + 1,)), dma((GROUPS, 2)), dma((GROUPS, 2)), dma((GROUPS, 2)),
            dma((8,)), dma((8,)),
        ],
        compiler_params=pltpu.CompilerParams(
            collective_id=0, has_side_effects=True, vmem_limit_bytes=63 * 1024 * 1024
        ),
    )(boundary, sentence_ids, qkv_weight, out_weight, inner_weight, outer_weight, norm_gain, norm_bias)

    blocks = 8 * GROUPS
    hbm = pl.BlockSpec(memory_space=pltpu.HBM)
    grad_qkv, grad_out, grad_inner, grad_outer, grad_gain, grad_bias, result = pl.pallas_call(
        widen,
        out_shape=tuple(
            jax.ShapeDtypeStruct(item.shape, F32)
            for item in (qkv_weight, out_weight, inner_weight, outer_weight, norm_gain, norm_bias)
        )
        + (jax.ShapeDtypeStruct(boundary.shape, BF16),),
        in_specs=[hbm] * 3,
        out_specs=(hbm,) * 7,
        scratch_shapes=[
            pltpu.VMEM((blocks, 2, 256, 256), BF16), pltpu.VMEM((blocks, 256, 512), F32),
            pltpu.VMEM((micro, local, width), BF16), pltpu.VMEM((8, width), F32), dma((blocks,)), dma((blocks,)), dma((5,)),
        ],
        compiler_params=pltpu.CompilerParams(vmem_limit_bytes=62 * 1024 * 1024),
    )(summed, vectors, result)
    return (result, grad_qkv, grad_out, grad_inner, grad_outer, grad_gain, grad_bias)


def solution(mesh):
    weight = P("section", None, None)
    edge = P("section", None, "dp", "copy", None)
    return jax.shard_map(
        functools.partial(per_device, mesh),
        mesh=mesh,
        in_specs=(edge, P(None, "dp", None)) + (weight,) * 6,
        out_specs=(edge,) + (weight,) * 6,
        check_vma=False,
    )
```
